256 devices in a mesh: lon: 64 (over z, y_hi, x), lat: 4 (over y_lo, core).
Axes of the slice: x: 4, y: 4 (y_hi: 2, y_lo: 2; y = y_hi * 2 + y_lo), z: 8, core: 2. Of those that a mesh axis runs over, the one named last changes fastest.
Arguments:
- field: bfloat16 [2, 48, 1536, 192], P(None, 'lat', 'lon'), may hold values from -6 to 6
- region: int32 [48], replicated, may hold values from 0 to 2, never falling along the last dimension, each value on 1 to 24 neighbouring positions
- w_qkv: bfloat16 [192, 576], replicated, may hold values from -4 to 4
- w_out: bfloat16 [192, 192], replicated, may hold values from -0.4375 to 0.4375
- w_up: bfloat16 [192, 768], replicated, may hold values from -0.4375 to 0.4375
- w_down: bfloat16 [768, 192], replicated, may hold values from -0.21875 to 0.21875
- gain_attn: float32 [192], replicated, may hold values from 0.25 to 1.75
- gain_mlp: float32 [192], replicated, may hold values from 0.25 to 1.75
- grad_next: bfloat16 [2, 48, 1536, 192], P(None, 'lat', 'lon'), may hold values from -6 to 6
Outputs:
- output: bfloat16 [2, 48, 1536, 192], P(None, 'lat', 'lon')
- grad_field: bfloat16 [2, 48, 1536, 192], P(None, 'lat', 'lon')
- grad_qkv: float32 [192, 576], replicated
- grad_out: float32 [192, 192], replicated
- grad_up: float32 [192, 768], replicated
- grad_down: float32 [768, 192], replicated
- grad_gain_attn: float32 [192], replicated
- grad_gain_mlp: float32 [192], replicated
The draws below stay inside these ranges and needn't reach their ends.
Inputs may be any that keep to these rules, and one draw needn't show every extreme that they name: `region`: bands never fall along latitude, each band is one run of rows, at most 24 rows.
All inputs are finite; a program needn't handle non-finite values.
Results may differ from the reference program's by a relative error of at most 0.015.
The reference program's roundings to bfloat16 on the way count: a program that leaves them out, or rounds other values in their place, can miss the bound.
Values may be sent and summed in bfloat16 or wider, within the bound.
A program may use at most 64 MiB of HBM per device.

```python
import math
import jax
import jax.numpy as jnp
import numpy as np
from jax import lax

C = 192
HEADS = 6
FF = 768
LEV = 2
WIN_LAT = 6
WIN_LON = 12
NLAT = 48
NLON = 1536


def draw_w_qkv(key, part):
    key = jax.random.fold_in(key, 11)
    first, second, third = jax.random.split(key, 3)
    base = jax.random.normal(first, (C, C), jnp.float32)
    other = jax.random.normal(second, (C, C), jnp.float32)
    values = jax.random.normal(third, (C, C), jnp.float32) * C ** (-0.5)
    query = base * C ** (-0.5)
    keys = other * C ** (-0.5)
    whole = jnp.concatenate([query, keys, values], 1)
    return jnp.clip(whole, -4.0, 4.0).astype(jnp.bfloat16)


def shard_levels(rng, dims, shards, least, top_value):
    factor_of = 1.0
    for axis_at, parts in shards:
        heights = jax.random.uniform(jax.random.fold_in(jax.random.fold_in(rng, 6), axis_at), (parts,), jnp.float32, least / len(shards), top_value / len(shards))
        factor_of = factor_of * jnp.repeat(jnp.exp(heights), dims[axis_at] // parts).reshape((-1,) + (1,) * (len(dims) - 1 - axis_at))
    return factor_of


def length_profile(count, total, limit, lean):
    loads = [(1 << 20) // math.isqrt(grade ** lean) + 1 for grade in range(2, count + 1)]
    rest, given = total - limit - (count - 1), [1] * (count - 1)
    while rest > 0:
        candidates = [i for i in range(count - 1) if given[i] < limit]
        pool, remaining = sum([loads[i] for i in candidates]), rest
        for i in candidates:
            extra = min(limit - given[i], max(1, remaining * loads[i] // pool), rest)
            given[i] = given[i] + extra
            rest = rest - extra
    return np.array([limit] + given)


def ragged_sizes(own_key, count, total, reach, lean):
    if count == 2:
        one = jax.random.randint(own_key, (), max(1, total - reach), min(reach, total - 1) + 1)
        return jnp.stack([one, total - one])
    sizes = jnp.asarray(length_profile(count, total, reach, lean), jnp.int32)
    couples = (count - 1) // 2
    donor, sink = sizes[1:1 + 2 * couples:2], sizes[2:2 + 2 * couples:2]
    slack = jnp.minimum(donor - 1, reach - sink)
    passed = jax.random.randint(jax.random.fold_in(own_key, 1), (couples,), 0, 1 << 20) % (slack + 1)
    sizes = sizes.at[1:1 + 2 * couples:2].set(donor - passed).at[2:2 + 2 * couples:2].set(sink + passed)
    return sizes[jax.random.permutation(jax.random.fold_in(own_key, 2), count)]


def scatter_about(key, shape, deviation, reach, pieces=(), kind=jnp.bfloat16):
    drawn = deviation * jax.random.normal(key, shape, jnp.float32)
    if pieces:
        drawn = drawn * shard_levels(key, shape, pieces, -0.22, 0.18)
    return jnp.clip(drawn, -reach, reach).astype(kind)


def setup_inputs(seed: int = 0) -> dict:
    key_list = jax.random.split(jax.random.key(seed), 10)
    field = scatter_about(key_list[0], (LEV, NLAT, NLON, C), 1.0, 6.0, ((1, 4), (2, 64)))
    region = jnp.searchsorted(jnp.cumsum(ragged_sizes(key_list[1], 3, NLAT, NLAT // 2, 0)), jnp.arange(NLAT), side="right").astype(jnp.int32)
    w_qkv = draw_w_qkv(jax.random.fold_in(key_list[9], 71), 0)
    w_out = scatter_about(key_list[3], (C, C), C ** -0.5, 0.4375)
    w_up = scatter_about(key_list[4], (C, FF), C ** -0.5, 0.4375)
    w_down = scatter_about(key_list[5], (FF, C), FF ** -0.5, 0.21875)
    gain_attn = jnp.clip(1.0 + 0.15 * jax.random.normal(key_list[6], (C,), jnp.float32), 0.25, 1.75)
    gain_mlp = jnp.clip(1.0 + 0.15 * jax.random.normal(key_list[7], (C,), jnp.float32), 0.25, 1.75)
    grad_next = scatter_about(key_list[8], (LEV, NLAT, NLON, C), 1.0, 6.0, ((1, 4), (2, 64)))
    return dict(field=field, region=region, w_qkv=w_qkv, w_out=w_out, w_up=w_up, w_down=w_down, gain_attn=gain_attn, gain_mlp=gain_mlp, grad_next=grad_next)


def layer_norm(values, gain):
    mean = lax.optimization_barrier(jnp.mean(values, -1, keepdims=True))
    centred = values - mean
    inverse = lax.rsqrt(lax.optimization_barrier(jnp.mean(centred * centred, -1, keepdims=True)) + 1e-05)
    normed = centred * inverse
    return (normed * gain, normed, inverse)

def norm_back(grad_in, normed, inverse, gain):
    dnormed = grad_in * gain
    dvalues = inverse * (dnormed - lax.optimization_barrier(jnp.mean(dnormed, -1, keepdims=True)) - normed * lax.optimization_barrier(jnp.mean(dnormed * normed, -1, keepdims=True)))
    dgain = lax.optimization_barrier(jnp.sum((grad_in * normed).reshape(-1, gain.shape[0]), 0))
    return (dvalues, dgain)

def gelu_value(z):
    inner = 0.7978845608 * (z + 0.044715 * z * z * z)
    return 0.5 * z * (1.0 + jnp.tanh(inner))

def gelu_slope(z):
    inner = 0.7978845608 * (z + 0.044715 * z * z * z)
    tangent = jnp.tanh(inner)
    return 0.5 * (1.0 + tangent) + 0.5 * z * (1.0 - tangent * tangent) * 0.7978845608 * (1.0 + 3.0 * 0.044715 * z * z)

def to_windows(grid):
    levels, rows, cols, width = grid.shape
    blocks = grid.reshape(levels, rows // WIN_LAT, WIN_LAT, cols // WIN_LON, WIN_LON, width)
    return blocks.transpose(1, 3, 0, 2, 4, 5).reshape(rows // WIN_LAT * (cols // WIN_LON), levels * WIN_LAT * WIN_LON, width)

def from_windows(windows, levels, rows, cols):
    width = windows.shape[-1]
    blocks = windows.reshape(rows // WIN_LAT, cols // WIN_LON, levels, WIN_LAT, WIN_LON, width)
    return blocks.transpose(2, 0, 3, 1, 4, 5).reshape(levels, rows, cols, width)

def attend_forward(shifted, w_qkv, band_rows):
    levels, rows, cols, width = shifted.shape
    windows = to_windows(shifted)
    count, tokens = (windows.shape[0], windows.shape[1])
    qkv = jnp.dot(windows.reshape(-1, width), w_qkv, preferred_element_type=jnp.float32).astype(jnp.bfloat16)
    qkv = lax.optimization_barrier(qkv).reshape(count, tokens, 3, HEADS, width // HEADS)
    query = qkv[:, :, 0]
    keys = qkv[:, :, 1]
    values = qkv[:, :, 2]
    scores = jnp.einsum('wqhd,wkhd->whqk', query, keys, preferred_element_type=jnp.float32) * (width // HEADS) ** (-0.5)
    band = jnp.broadcast_to(band_rows.reshape(rows // WIN_LAT, 1, 1, WIN_LAT, 1), (rows // WIN_LAT, cols // WIN_LON, levels, WIN_LAT, WIN_LON)).reshape(count, tokens)
    allowed = band[:, None, :, None] == band[:, None, None, :]
    scores = jnp.where(allowed, scores, -1e+30)
    top = lax.optimization_barrier(jnp.max(scores, -1, keepdims=True))
    expo = jnp.exp(scores - top)
    probs = expo / lax.optimization_barrier(jnp.sum(expo, -1, keepdims=True))
    probs_b = lax.optimization_barrier(probs.astype(jnp.bfloat16))
    heads_out = jnp.einsum('whqk,wkhd->wqhd', probs_b, values, preferred_element_type=jnp.float32).astype(jnp.bfloat16)
    return (heads_out, qkv, probs, probs_b)

def attend_backward(grad_win, qkv, probs, probs_b):
    query = qkv[:, :, 0].astype(jnp.float32)
    keys = qkv[:, :, 1].astype(jnp.float32)
    values = qkv[:, :, 2]
    dvalues = jnp.einsum('whqk,wqhd->wkhd', probs_b, grad_win, preferred_element_type=jnp.float32)
    dprobs = jnp.einsum('wqhd,wkhd->whqk', grad_win, values, preferred_element_type=jnp.float32)
    dscores = probs * (dprobs - lax.optimization_barrier(jnp.sum(dprobs * probs, -1, keepdims=True))) * query.shape[-1] ** (-0.5)
    dquery = jnp.einsum('whqk,wkhd->wqhd', dscores, keys)
    dkeys = jnp.einsum('whqk,wqhd->wkhd', dscores, query)
    return jnp.stack([dquery, dkeys, dvalues], 2).astype(jnp.bfloat16)

def reference(field, region, w_qkv, w_out, w_up, w_down, gain_attn, gain_mlp, grad_next):
    half_lat = WIN_LAT // 2
    half_lon = WIN_LON // 2
    width = C
    x = field.astype(jnp.float32)
    scaled1, normed1, inverse1 = layer_norm(x, gain_attn)
    h1 = scaled1.astype(jnp.bfloat16)
    shifted = jnp.roll(h1, (-half_lat, -half_lon), axis=(1, 2))
    band_all = jnp.roll(region, -half_lat).reshape(NLAT // WIN_LAT, WIN_LAT)
    blocks = shifted.reshape(LEV, NLAT // WIN_LAT, WIN_LAT, NLON, width).transpose(1, 0, 2, 3, 4)

    def forward_block(pair):
        block, band_rows = pair
        heads_out = attend_forward(block, w_qkv, band_rows)[0]
        return from_windows(heads_out.reshape(heads_out.shape[0], heads_out.shape[1], width), LEV, WIN_LAT, NLON)
    heads = lax.map(forward_block, (blocks, band_all))
    heads = heads.transpose(1, 0, 2, 3, 4).reshape(LEV, NLAT, NLON, width)
    own = jnp.roll(heads, (half_lat, half_lon), axis=(1, 2))
    own_flat = own.reshape(-1, width)
    mixed = x + jnp.dot(own_flat, w_out, preferred_element_type=jnp.float32).reshape(x.shape)
    scaled2, normed2, inverse2 = layer_norm(mixed, gain_mlp)
    h2 = scaled2.astype(jnp.bfloat16).reshape(-1, width)
    pre = jnp.dot(h2, w_up, preferred_element_type=jnp.float32)
    act = gelu_value(pre).astype(jnp.bfloat16)
    output = (mixed + jnp.dot(act, w_down, preferred_element_type=jnp.float32).reshape(x.shape)).astype(jnp.bfloat16)
    grad_flat = grad_next.reshape(-1, width)
    grad_down = jnp.dot(act.T, grad_flat, preferred_element_type=jnp.float32)
    dact = jnp.dot(grad_flat, w_down.T, preferred_element_type=jnp.float32)
    dpre = (dact * gelu_slope(pre)).astype(jnp.bfloat16)
    grad_up = jnp.dot(h2.T, dpre, preferred_element_type=jnp.float32)
    dh2 = jnp.dot(dpre, w_up.T, preferred_element_type=jnp.float32).reshape(x.shape)
    dmix_norm, grad_gain_mlp = norm_back(dh2, normed2, inverse2, gain_mlp)
    dmixed = grad_next.astype(jnp.float32) + dmix_norm
    dmix_b = dmixed.astype(jnp.bfloat16).reshape(-1, width)
    grad_out = jnp.dot(own_flat.T, dmix_b, preferred_element_type=jnp.float32)
    downs = jnp.dot(dmix_b, w_out.T, preferred_element_type=jnp.float32).astype(jnp.bfloat16).reshape(x.shape)
    downs_shift = jnp.roll(downs, (-half_lat, -half_lon), axis=(1, 2))
    grad_blocks = downs_shift.reshape(LEV, NLAT // WIN_LAT, WIN_LAT, NLON, width).transpose(1, 0, 2, 3, 4)

    def backward_block(triple):
        block, band_rows, grad_block = triple
        heads_out, qkv, probs, probs_b = attend_forward(block, w_qkv, band_rows)
        count, tokens = (heads_out.shape[0], heads_out.shape[1])
        grad_win = to_windows(grad_block).reshape(count, tokens, HEADS, width // HEADS)
        dqkv = attend_backward(grad_win, qkv, probs, probs_b).reshape(-1, 3 * width)
        windows = to_windows(block).reshape(-1, width)
        term = jnp.dot(windows.T, dqkv, preferred_element_type=jnp.float32)
        dsource = jnp.dot(dqkv, w_qkv.T, preferred_element_type=jnp.float32).astype(jnp.bfloat16)
        return (from_windows(dsource.reshape(count, tokens, width), LEV, WIN_LAT, NLON), term)
    dsource, terms = lax.map(backward_block, (blocks, band_all, grad_blocks))
    grad_qkv = lax.optimization_barrier(jnp.sum(terms, 0))
    dsource = dsource.transpose(1, 0, 2, 3, 4).reshape(LEV, NLAT, NLON, width)
    dshift = jnp.roll(dsource, (half_lat, half_lon), axis=(1, 2))
    dx_norm, grad_gain_attn = norm_back(dshift.astype(jnp.float32), normed1, inverse1, gain_attn)
    grad_field = (dmixed + dx_norm).astype(jnp.bfloat16)
    return (output, grad_field, grad_qkv, grad_out, grad_up, grad_down, grad_gain_attn, grad_gain_mlp)
```

```python
import functools

import jax
import jax.numpy as jnp
import ml_dtypes
import numpy as np
from jax import lax
from jax.experimental import pallas as pl
from jax.experimental.pallas import tpu as pltpu
from jax.sharding import PartitionSpec as P

C = 192
HEADS = 6
FF = 768
ROWS = 12
COLS = 24
TOK = 2 * ROWS * COLS
WIN = 144
HQ = HEADS * WIN
STAY = 336
HALO = 272
ALL = STAY + HALO
MSG = ((0, 112), (112, 112), (224, 48))
SCALE = 32.0 ** -0.5
LOG2E = 1.4426950408889634
F32 = jnp.float32
BF = jnp.bfloat16
MESH = pl.DeviceIdType.MESH


def tables():
    def piece(rows, cols):
        return [(l * ROWS * COLS + r * COLS + c, r) for l in range(2) for r in rows for c in cols]

    top, mid, bot = range(0, 3), range(3, 9), range(9, 12)
    left, cen, rig = range(0, 6), range(6, 18), range(18, 24)
    pad = (-1, 0)
    order = piece(mid, cen)
    order += piece(mid, rig) + piece(bot, cen)
    order += piece(bot, rig) + [pad] * 12
    order += piece(mid, left) + piece(bot, left) + [pad] * 4
    order += piece(top, cen) + piece(top, rig) + [pad] * 4
    order += piece(top, left) + [pad] * 12
    assert len(order) == ALL
    to_order = np.zeros((ALL, TOK), np.float32)
    for at, (index, _) in enumerate(order):
        if index >= 0:
            to_order[at, index] = 1
    spans = [
        [(0, 144)],
        [(144, 72), (336, 72)],
        [(216, 72), (448, 72)],
        [(288, 36), (408, 36), (520, 36), (560, 36)],
    ]
    to_win = np.zeros((4 * WIN, ALL), np.float32)
    row_of = np.zeros((4 * WIN, 16), np.float32)
    at = 0
    for window in spans:
        for start, size in window:
            for pos in range(start, start + size):
                to_win[at, pos] = 1
                row = order[pos][1]
                row_of[at, row - 3 if row >= 3 else row + 9] = 1
                at += 1
    to_win = to_win[WIN:, WIN:]
    tile = np.tile(np.eye(WIN, dtype=np.float32), (1, HEADS))
    kind = ml_dtypes.bfloat16
    return tuple(
        np.ascontiguousarray(a).astype(kind)
        for a in (to_order, to_win, to_win.T, tile, row_of)
    ), np.ascontiguousarray(to_order.T).astype(kind)


def dot(a, b, dims=((1,), (0,))):
    return lax.dot_general(a, b, (dims, ((), ())), preferred_element_type=F32)


NT = ((1,), (1,))
TN = ((0,), (0,))


def norm(x):
    mean = jnp.mean(x, -1, keepdims=True)
    centred = x - mean
    inverse = lax.rsqrt(jnp.mean(centred * centred, -1, keepdims=True) + 1e-05)
    return centred * inverse, inverse


def norm_back(d, normed, inverse, gain):
    dn = d * gain
    return inverse * (
        dn - jnp.mean(dn, -1, keepdims=True) - normed * jnp.mean(dn * normed, -1, keepdims=True)
    )


class Plan:
    def __init__(self, rows, g1, g2):
        self.r = 16 * -(-rows // (16 * g1)) if rows > 16 * g1 else 16
        self.r = max(self.r, 16)
        if rows == 384 and g1 >= 12:
            self.r = 32
        self.own = -(-rows // self.r)
        self.rows = self.own * self.r
        self.t = 6 if g2 >= 6 else 3
        self.lanes = FF // self.t


def kernel(
    nlon, nlat, xg, plans,
    field, grad, region, w_qkv, w_out, w_up, w_down, gain_a, gain_m,
    to_order, to_win, from_win, tile, row_of,
    out_o, gf_o, gat_ab, gat_d,
    x_o, x_h, own, own_h, downs, downs_h, dsh, dsh_h,
    g_o, h1, normed1, t_win, wpad, qkv, qm, probs, heads,
    h2, act, dpre, dmix, dmixb, gsum,
    ab_src, d_src, ab_r1, d_r1, ab_s1, d_s1, ab_r2, d_r2, ab_fin, d_fin,
    halo_send, halo_recv, red_send, red_recv,
):
    lon = lax.axis_index("lon")
    lat = lax.axis_index("lat")
    g1 = xg * nlat
    g2 = nlon // xg
    u = lax.div(lon, xg)
    m1 = lax.rem(lon, xg) * nlat + lat

    def wrap(i, n):
        return lax.rem(i + n, n)

    def at(dlat, dlon):
        return {"lon": wrap(lon + dlon, nlon), "lat": wrap(lat + dlat, nlat)}

    def peer1(m):
        return {"lon": u * xg + lax.div(m, nlat), "lat": lax.rem(m, nlat)}

    def peer2(v):
        return {"lon": v * xg + lax.rem(lon, xg), "lat": lat}

    before = (at(0, -1), at(-1, 0), at(-1, -1))
    after = (at(0, 1), at(1, 0), at(1, 1))

    barrier = pltpu.get_barrier_semaphore()

    def greet1(k, _):
        pl.semaphore_signal(barrier, inc=1, device_id=peer1(wrap(m1 + k, g1)), device_id_type=MESH)
        return 0

    def greet2(k, _):
        pl.semaphore_signal(barrier, inc=1, device_id=peer2(wrap(u + k, g2)), device_id_type=MESH)
        return 0

    for device in before + after:
        pl.semaphore_signal(barrier, inc=1, device_id=device, device_id_type=MESH)
    lax.fori_loop(1, g1, greet1, 0)
    lax.fori_loop(1, g2, greet2, 0)

    def halo(which, src, base, dst, devices):
        copies = []
        for i, (start, size) in enumerate(MSG):
            copies.append(
                pltpu.make_async_remote_copy(
                    src_ref=src.at[pl.ds(base + start, size)],
                    dst_ref=dst.at[pl.ds(start, size)],
                    send_sem=halo_send.at[which, i],
                    recv_sem=halo_recv.at[which, i],
                    device_id=devices[i],
                    device_id_type=MESH,
                )
            )
        return copies

    ex = (
        halo(0, x_o, STAY, x_h, before),
        halo(1, own_h, 0, own, after),
        halo(2, downs, STAY, downs_h, before),
        halo(3, dsh_h, 0, dsh, after),
    )

    def start(copies):
        for copy in copies:
            copy.start()

    def arrive(copies):
        for copy in copies:
            copy.wait_recv()

    x_o[...] = dot(to_order[...], field[...]).astype(BF)
    pl.semaphore_wait(barrier, 6 + (g1 - 1) + (g2 - 1))
    start(ex[0])

    g_o[...] = dot(to_order[...], grad[...]).astype(BF)
    lane = lax.broadcasted_iota(jnp.int32, (1, 256), 1)
    wpad[...] = jnp.zeros_like(wpad)
    for i in range(3):
        wpad[:, 256 * i : 256 * i + C] = w_qkv[:, C * i : C * i + C]
    slot = lax.broadcasted_iota(jnp.int32, (16, 256), 0)
    value = jnp.full((16, 256), -1, jnp.int32)
    for j in range(ROWS):
        band = region[wrap(lat * ROWS + 3 + j, nlat * ROWS)]
        value = jnp.where(slot == j, band, value)
    column = lax.broadcasted_iota(jnp.int32, (16, 256), 1) - C
    band_hot = jnp.where((column >= 0) & (value == column), 1.0, 0.0).astype(BF)
    member = dot(row_of[...], band_hot)
    outside = jnp.where((lane >= C) & (lane < C + 3), (member - 1.0) * 1e30, 0.0).astype(BF)

    gain_attn = gain_a[...]
    gain_mlp = gain_m[...]

    normed, _ = norm(x_o[0:STAY, :].astype(F32))
    normed1[0:STAY, :] = normed
    h1[0:STAY, :] = (normed * gain_attn).astype(BF)

    def project(w0, count):
        rows = pl.ds(w0 * WIN, count * WIN)
        value = dot(t_win[rows, :], wpad[...])
        qkv[rows, 0:256] = value[:, 0:256].astype(BF)
        qkv[rows, 256:512] = (value[:, 256:512] + member[w0 * WIN : (w0 + count) * WIN]).astype(BF)
        qkv[rows, 512:768] = value[:, 512:768].astype(BF)

    eye = (
        lax.broadcasted_iota(jnp.int32, (C, C), 0) == lax.broadcasted_iota(jnp.int32, (C, C), 1)
    ).astype(F32).astype(BF)
    head_rows = lax.broadcasted_iota(jnp.int32, (C, HQ), 0)
    head_cols = lax.broadcasted_iota(jnp.int32, (C, HQ), 1)
    diagonal = jnp.zeros((C, HQ), jnp.bool_)
    for h in range(HEADS):
        diagonal = diagonal | (
            (head_rows >= 32 * h) & (head_rows < 32 * h + 32)
            & (head_cols >= WIN * h) & (head_cols < WIN * h + WIN)
        )

    def gather_heads(full):
        return dot(tile[...], jnp.where(diagonal, full, 0.0).astype(BF), NT).astype(BF)

    def forward(w):
        rows = pl.ds(w * WIN, WIN)
        query = qkv[rows, 0:256]
        closed = outside[w * WIN : (w + 1) * WIN]
        for h in range(HEADS):
            mine = (lane >= 32 * h) & (lane < 32 * h + 32)
            qm[w, pl.ds(h * WIN, WIN), :] = jnp.where(mine, query, closed)
        scores = dot(qkv[rows, 256:512], qm[w], NT) * (SCALE * LOG2E)
        top = jnp.max(scores, 0, keepdims=True)
        expo = jnp.exp2(scores - top)
        prob = expo * (1.0 / jnp.sum(expo, 0, keepdims=True))
        probs[w] = prob
        value_t = dot(eye, qkv[rows, 512:704], NT).astype(BF)
        heads[rows, :] = gather_heads(dot(value_t, prob.astype(BF)))

    t_win[0:WIN, :] = h1[0:WIN, :]
    project(0, 1)
    forward(0)

    arrive(ex[0])
    normed, _ = norm(x_h[...].astype(F32))
    normed1[STAY:ALL, :] = normed
    h1[STAY:ALL, :] = (normed * gain_attn).astype(BF)
    t_win[WIN:, :] = dot(to_win[...], h1[WIN:ALL, :]).astype(BF)
    project(1, 3)
    for w in range(1, 4):
        forward(w)
    back = dot(from_win[...], heads[WIN:, :]).astype(BF)
    own_h[...] = back[STAY - WIN :]
    start(ex[1])

    def mlp(rows, owned):
        x = x_o[rows, :].astype(F32)
        g = g_o[rows, :]
        mixed = x + dot(owned, w_out[...])
        normed2, inverse2 = norm(mixed)
        h2b = (normed2 * gain_mlp).astype(BF)
        h2[rows, :] = h2b
        pre = dot(h2b, w_up[...])
        square = pre * pre
        tangent = jnp.tanh(0.7978845608 * pre * (1.0 + 0.044715 * square))
        half = 0.5 * (1.0 + tangent)
        actb = (pre * half).astype(BF)
        act[rows, :] = actb
        slope = half + 0.5 * pre * (1.0 - tangent * tangent) * 0.7978845608 * (
            1.0 + 3.0 * 0.044715 * square
        )
        out_o[rows, :] = (mixed + dot(actb, w_down[...])).astype(BF)
        dpreb = (dot(g, w_down[...], NT) * slope).astype(BF)
        dpre[rows, :] = dpreb
        dh2 = dot(dpreb, w_up[...], NT)
        dm = g.astype(F32) + norm_back(dh2, normed2, inverse2, gain_mlp)
        dmix[rows, :] = dm
        dmb = dm.astype(BF)
        dmixb[rows, :] = dmb
        downs[rows, :] = dot(dmb, w_out[...], NT).astype(BF)
        return jnp.sum(dh2 * normed2, 0, keepdims=True)

    stay = pl.ds(0, STAY)
    away = pl.ds(STAY, HALO)
    own_stay = jnp.concatenate([heads[0:WIN, :], back[0 : STAY - WIN]], 0)
    gain_term_m = mlp(stay, own_stay)
    arrive(ex[1])
    gain_term_m = gain_term_m + mlp(away, own[...])
    start(ex[2])

    plan_ab, plan_d = plans

    def stage1(which, plan, src, r1):
        def one(k, fn):
            target = wrap(m1 + k, g1)
            copy = pltpu.make_async_remote_copy(
                src_ref=src.at[pl.ds(pl.multiple_of(target * plan.r, 16), plan.r)],
                dst_ref=r1.at[k],
                send_sem=red_send.at[which, 0, k],
                recv_sem=red_recv.at[which, 0, k],
                device_id=peer1(target),
                device_id_type=MESH,
            )
            pl.when(target < plan.own)(functools.partial(fn, copy))
        return one

    def stage2(which, plan, s1, r2):
        def one(k, fn):
            target = wrap(u + k, g2)
            copy = pltpu.make_async_remote_copy(
                src_ref=s1.at[target],
                dst_ref=r2.at[k],
                send_sem=red_send.at[which, 1, k],
                recv_sem=red_recv.at[which, 1, k],
                device_id=peer2(target),
                device_id_type=MESH,
            )
            pl.when((target < plan.t) & (m1 < plan.own))(functools.partial(fn, copy))
        return one

    def spread2(which, plan, fin):
        def one(k, fn, source=None):
            source = u if source is None else source
            copy = pltpu.make_async_remote_copy(
                src_ref=fin.at[source],
                dst_ref=fin.at[source],
                send_sem=red_send.at[which, 2, k],
                recv_sem=red_recv.at[which, 2, k],
                device_id=peer2(wrap(u + k, g2)),
                device_id_type=MESH,
            )
            pl.when((source < plan.t) & (m1 < plan.own))(functools.partial(fn, copy))
        return one

    def spread1(which, plan, fin, gat):
        def one(k, fn, source=None):
            source = m1 if source is None else source
            copy = pltpu.make_async_remote_copy(
                src_ref=fin,
                dst_ref=gat.at[source],
                send_sem=red_send.at[which, 3, k],
                recv_sem=red_recv.at[which, 3, k],
                device_id=peer1(wrap(m1 + k, g1)),
                device_id_type=MESH,
            )
            pl.when(source < plan.own)(functools.partial(fn, copy))
        return one

    def each(n, one, fn, back=None):
        def step(k, _):
            if back is None:
                one(k, fn)
            else:
                one(k, fn, wrap(back - k, n))
            return 0

        lax.fori_loop(1, n, step, 0)

    def go(copy):
        copy.start()

    def got(copy):
        copy.wait_recv()

    def sent(copy):
        copy.wait_send()

    def wait_r1(which, plan, r1):
        def step(k, _):
            pltpu.make_async_remote_copy(
                src_ref=r1.at[k], dst_ref=r1.at[k],
                send_sem=red_send.at[which, 0, k], recv_sem=red_recv.at[which, 0, k],
                device_id=peer1(wrap(m1 + k, g1)), device_id_type=MESH,
            ).wait_recv()
            return 0

        lax.fori_loop(1, g1, step, 0)

    def wait_r2(which, plan, r2):
        def step(k, _):
            pltpu.make_async_remote_copy(
                src_ref=r2.at[k], dst_ref=r2.at[k],
                send_sem=red_send.at[which, 1, k], recv_sem=red_recv.at[which, 1, k],
                device_id=peer2(wrap(u + k, g2)), device_id_type=MESH,
            ).wait_recv()
            return 0

        lax.fori_loop(1, g2, step, 0)

    def reduce1(which, plan, src, r1, s1, r2):
        @pl.when(m1 < plan.own)
        def _():
            wait_r1(which, plan, r1)
            for j in range(plan.t):
                cols = slice(j * plan.lanes, (j + 1) * plan.lanes)
                total = src[pl.ds(pl.multiple_of(m1 * plan.r, 16), plan.r), cols].astype(F32)
                for k in range(1, g1):
                    total = total + r1[k, :, cols].astype(F32)
                s1[j] = total
        each(g2, stage2(which, plan, s1, r2), go)

    def reduce2(which, plan, s1, r2, fin):
        @pl.when((m1 < plan.own) & (u < plan.t))
        def _():
            wait_r2(which, plan, r2)
            total = s1[u]
            for k in range(1, g2):
                total = total + r2[k]
            fin[u] = total.astype(BF)
        each(g2, spread2(which, plan, fin), go)

    def gather2(which, plan, fin, gat):
        each(g2, spread2(which, plan, fin), got, u)
        @pl.when(m1 < plan.own)
        def _():
            gat[m1] = fin[...]
        each(g1, spread1(which, plan, fin, gat), go)

    def gather1(which, plan, fin, gat):
        each(g1, spread1(which, plan, fin, gat), got, m1)

    def drain(which, plan, src, r1, s1, r2, fin, gat):
        each(g1, stage1(which, plan, src, r1), sent)
        each(g2, stage2(which, plan, s1, r2), sent)
        each(g2, spread2(which, plan, fin), sent)
        each(g1, spread1(which, plan, fin, gat), sent)

    ab_src[0:C, :] = dot(g_o[...], act[...], TN).astype(BF)
    ab_src[C : 2 * C, :] = dot(h2[...], dpre[...], TN).astype(BF)
    each(g1, stage1(0, plan_ab, ab_src, ab_r1), go)

    def backward(w, do):
        rows = pl.ds(w * WIN, WIN)
        dom = jnp.concatenate(
            [
                jnp.where((lane[:, :C] >= 32 * h) & (lane[:, :C] < 32 * h + 32), do, 0.0).astype(BF)
                for h in range(HEADS)
            ],
            0,
        )
        prob = probs[w]
        dprob = dot(qkv[rows, 512:704], dom, NT)
        dscore = (prob * (dprob - jnp.sum(dprob * prob, 0, keepdims=True))).astype(BF)
        dv = dot(prob.astype(BF), dom).astype(BF)
        dk = (dot(dscore, qm[w, :, 0:C]) * SCALE).astype(BF)
        key_t = dot(eye, qkv[rows, 256:448], NT).astype(BF)
        dq = gather_heads(dot(key_t, dscore) * SCALE)
        gsum[0, rows, :] = dq
        gsum[1, rows, :] = dk
        gsum[2, rows, :] = dv
        return (
            dot(dq, wpad[:, 0:C], NT) + dot(dk, wpad[:, 256:448], NT) + dot(dv, wpad[:, 512:704], NT)
        ).astype(BF)

    dsource0 = backward(0, downs[0:WIN, :])
    own_all = jnp.concatenate([own_stay, own[...]], 0)
    grad_out = dot(own_all, dmixb[...], TN)

    arrive(ex[2])
    home = jnp.concatenate([downs[WIN:STAY, :], downs_h[...]], 0)
    do_win = dot(to_win[...], home).astype(BF)
    sources = []
    for w in range(1, 4):
        sources.append(backward(w, do_win[(w - 1) * WIN : w * WIN]))
        if w == 1:
            reduce1(0, plan_ab, ab_src, ab_r1, ab_s1, ab_r2)
        if w == 3:
            reduce2(0, plan_ab, ab_s1, ab_r2, ab_fin)
    back = dot(from_win[...], jnp.concatenate(sources, 0)).astype(BF)
    dsh_h[...] = back[STAY - WIN :]
    start(ex[3])

    d_src[0:C, :] = jnp.concatenate(
        [dot(t_win[...], gsum[i], TN) for i in range(3)] + [grad_out], 1
    ).astype(BF)
    dsource = jnp.concatenate([dsource0, back], 0).astype(F32)
    gain_term_a = jnp.sum(dsource * normed1[...], 0, keepdims=True)
    d_src[C:, :] = jnp.zeros((plan_d.rows - C, FF), BF)
    gains = jnp.concatenate([gain_term_a, gain_term_m, jnp.zeros((1, 384), F32)], 1)
    first = lax.broadcasted_iota(jnp.int32, (16, FF), 0) == 0
    d_src[C : C + 16, :] = jnp.where(first, jnp.broadcast_to(gains, (16, FF)), 0.0).astype(BF)
    each(g1, stage1(1, plan_d, d_src, d_r1), go)

    def finish(rows, dshift):
        normed, inverse = norm(x_o[rows, :].astype(F32))
        dx = norm_back(dshift.astype(F32), normed, inverse, gain_attn)
        gf_o[rows, :] = (dmix[rows, :] + dx).astype(BF)

    gather2(0, plan_ab, ab_fin, gat_ab)
    finish(stay, dsource[:STAY])
    arrive(ex[3])
    finish(away, dsh[...])

    reduce1(1, plan_d, d_src, d_r1, d_s1, d_r2)
    reduce2(1, plan_d, d_s1, d_r2, d_fin)
    gather2(1, plan_d, d_fin, gat_d)
    gather1(0, plan_ab, ab_fin, gat_ab)
    gather1(1, plan_d, d_fin, gat_d)
    for copies in ex:
        for copy in copies:
            copy.wait_send()
    drain(0, plan_ab, ab_src, ab_r1, ab_s1, ab_r2, ab_fin, gat_ab)
    drain(1, plan_d, d_src, d_r1, d_s1, d_r2, d_fin, gat_d)


def final(
    plans, out_o, gf_o, gat_ab, gat_d, from_order,
    output, grad_field, grad_qkv, grad_out, grad_up, grad_down, grad_ga, grad_gm,
):
    plan_ab, plan_d = plans
    output[...] = dot(from_order[...], out_o[...]).astype(BF)
    grad_field[...] = dot(from_order[...], gf_o[...]).astype(BF)

    def whole(plan, gat):
        return jnp.concatenate(
            [
                jnp.concatenate([gat[o, t].astype(F32) for t in range(plan.t)], 1)
                for o in range(plan.own)
            ],
            0,
        )

    ab = whole(plan_ab, gat_ab)
    grad_down[...] = ab[:C].T
    grad_up[...] = ab[C : 2 * C]
    d = whole(plan_d, gat_d)
    grad_qkv[...] = d[:C, : 3 * C]
    grad_out[...] = d[:C, 3 * C :]
    grad_ga[...] = d[C : C + 1, :C]
    grad_gm[...] = d[C : C + 1, C : 2 * C]


def body(nlon, nlat, field, region, w_qkv, w_out, w_up, w_down, gain_attn, gain_mlp, grad_next):
    consts, from_order = tables()
    xg = 4 if nlon >= 16 else 1
    g1, g2 = xg * nlat, nlon // xg
    plan_ab, plan_d = Plan(2 * C, g1, g2), Plan(C + 16, g1, g2)
    plans = (plan_ab, plan_d)
    vmem = pl.BlockSpec(memory_space=pltpu.VMEM)
    smem = pl.BlockSpec(memory_space=pltpu.SMEM)
    V = pltpu.VMEM

    def pair(shape_of, kind):
        return [V(shape_of(p), kind) for p in plans]

    shapes = (
        jax.ShapeDtypeStruct((ALL, C), BF),
        jax.ShapeDtypeStruct((ALL, C), BF),
        jax.ShapeDtypeStruct((plan_ab.own, plan_ab.t, plan_ab.r, plan_ab.lanes), BF),
        jax.ShapeDtypeStruct((plan_d.own, plan_d.t, plan_d.r, plan_d.lanes), BF),
    )
    scratch = (
        [
            V((ALL, C), BF), V((HALO, C), BF),
            V((HALO, C), BF), V((HALO, C), BF),
            V((ALL, C), BF), V((HALO, C), BF),
            V((HALO, C), BF), V((HALO, C), BF),
            V((ALL, C), BF), V((ALL, C), BF), V((ALL, C), F32), V((4 * WIN, C), BF),
            V((C, FF), BF), V((4 * WIN, FF), BF), V((4, HQ, 256), BF), V((4, WIN, HQ), F32),
            V((4 * WIN, C), BF),
            V((ALL, C), BF), V((ALL, FF), BF), V((ALL, FF), BF), V((ALL, C), F32), V((ALL, C), BF),
            V((3, 4 * WIN, C), BF),
        ]
        + pair(lambda p: (p.rows, FF), BF)
        + pair(lambda p: (g1, p.r, FF), BF)
        + pair(lambda p: (p.t, p.r, p.lanes), F32)
        + pair(lambda p: (g2, p.r, p.lanes), F32)
        + pair(lambda p: (p.t, p.r, p.lanes), BF)
        + [
            pltpu.SemaphoreType.DMA((4, 3)),
            pltpu.SemaphoreType.DMA((4, 3)),
            pltpu.SemaphoreType.DMA((2, 4, 16)),
            pltpu.SemaphoreType.DMA((2, 4, 16)),
        ]
    )
    mids = pl.pallas_call(
        functools.partial(kernel, nlon, nlat, xg, plans),
        out_shape=shapes,
        in_specs=[vmem, vmem, smem] + [vmem] * 11,
        out_specs=[vmem] * 4,
        scratch_shapes=scratch,
        compiler_params=pltpu.CompilerParams(
            collective_id=0, has_side_effects=True, vmem_limit_bytes=50 << 20
        ),
        name="block",
    )(
        field.reshape(TOK, C), grad_next.reshape(TOK, C), region, w_qkv, w_out, w_up, w_down,
        gain_attn.reshape(1, C), gain_mlp.reshape(1, C), *[jnp.asarray(a) for a in consts],
    )
    outs = pl.pallas_call(
        functools.partial(final, plans),
        out_shape=(
            jax.ShapeDtypeStruct((TOK, C), BF),
            jax.ShapeDtypeStruct((TOK, C), BF),
            jax.ShapeDtypeStruct((C, 3 * C), F32),
            jax.ShapeDtypeStruct((C, C), F32),
            jax.ShapeDtypeStruct((C, FF), F32),
            jax.ShapeDtypeStruct((FF, C), F32),
            jax.ShapeDtypeStruct((1, C), F32),
            jax.ShapeDtypeStruct((1, C), F32),
        ),
        in_specs=[vmem] * 5,
        out_specs=[vmem] * 8,
        compiler_params=pltpu.CompilerParams(vmem_limit_bytes=50 << 20),
        name="final",
    )(*mids, jnp.asarray(from_order))
    output, grad_field, grad_qkv, grad_out, grad_up, grad_down, grad_ga, grad_gm = outs
    return (
        output.reshape(field.shape), grad_field.reshape(field.shape),
        grad_qkv, grad_out, grad_up, grad_down, grad_ga.reshape(C), grad_gm.reshape(C),
    )


def solution(mesh):
    grid = P(None, "lat", "lon", None)
    return jax.shard_map(
        functools.partial(body, mesh.shape["lon"], mesh.shape["lat"]),
        mesh=mesh,
        in_specs=(grid, P(), P(), P(), P(), P(), P(), P(), grid),
        out_specs=(grid, grid, P(), P(), P(), P(), P(), P()),
        check_vma=False,
    )
```

```python
import functools

import jax
import jax.numpy as jnp
import ml_dtypes
import numpy as np
from jax import lax
from jax.experimental import pallas as pl
from jax.experimental.pallas import tpu as pltpu
from jax.sharding import PartitionSpec as P

C = 192
HEADS = 6
FF = 768
HALF = 384
ROWS = 12
COLS = 24
TOK = 2 * ROWS * COLS
SCALE = 32.0 ** -0.5
LOG2E = 1.4426950408889634
F32 = jnp.float32
BF = jnp.bfloat16
MESH = pl.DeviceIdType.MESH

NQ = (144,) + (72,) * 4 + (40,) * 4
NK = (144,) + (144,) * 4 + (160,) * 4
QAT = tuple(int(v) for v in np.cumsum((0,) + NQ))
KAT = tuple(int(v) for v in np.cumsum((0,) + NK))
NQS, NKS = QAT[-1], KAT[-1]
WAY = ((0, -1), (0, 1), (-1, 0), (1, 0), (-1, -1), (-1, 1), (1, -1), (1, 1))
MAT = (0, 160, 320, 480, 640, 688, 736, 784)
MROWS = (160,) * 4 + (48,) * 4
HALO = 832
PARTS = (
    (),
    ((0, 72),),
    ((160, 72),),
    ((320, 72),),
    ((480, 72),),
    ((112, 40), (320 + 112, 40), (640, 40)),
    ((160 + 112, 40), (320 + 72, 40), (688, 40)),
    ((72, 40), (480 + 112, 40), (736, 40)),
    ((160 + 72, 40), (480 + 72, 40), (784, 40)),
)
BANDS = 18


def tables():
    def piece(rows, cols, size=None):
        got = [(l * ROWS * COLS + r * COLS + c, r) for l in range(2) for r in rows for c in cols]
        return got + [(-1, None)] * ((size or len(got)) - len(got))

    top, mid, bot = range(0, 3), range(3, 9), range(9, 12)
    left, cen, rig = range(0, 6), range(6, 18), range(18, 24)
    own = [
        piece(mid, cen),
        piece(mid, rig), piece(mid, left), piece(bot, cen), piece(top, cen),
        piece(bot, rig, 40), piece(bot, left, 40), piece(top, rig, 40), piece(top, left, 40),
    ]
    sent = [
        piece(mid, side) + piece(top, side, 40) + piece(bot, side, 48) for side in (left, rig)
    ] + [
        piece(rows, cen) + piece(rows, left, 40) + piece(rows, rig, 48) for rows in (top, bot)
    ] + [
        piece(top, left, 48), piece(top, rig, 48), piece(bot, left, 48), piece(bot, rig, 48),
    ]
    shift = (0, 0, ROWS, -ROWS, ROWS, ROWS, -ROWS, -ROWS)
    flat_own = sum(own, [])
    flat_sent = sum(sent, [])
    moved = sum(
        [[(i, None if r is None else r + s) for i, r in part] for part, s in zip(sent, shift)], []
    )
    assert len(flat_own) == NQS and len(flat_sent) == HALO

    def hot(tokens):
        out = np.zeros((len(tokens), TOK), np.float32)
        for at, (index, _) in enumerate(tokens):
            if index >= 0:
                out[at, index] = 1
        return out

    keys = []
    for w in range(9):
        keys += own[w]
        for start, size in PARTS[w]:
            keys += moved[start : start + size]
    row_of = np.zeros((NKS, 32), np.float32)
    for at, (_, row) in enumerate(keys):
        row_of[at, BANDS if row is None else row + 3] = 1
    to_own, to_sent = hot(flat_own), hot(flat_sent)
    kind = ml_dtypes.bfloat16
    return [
        np.ascontiguousarray(a).astype(kind)
        for a in (np.concatenate([to_own, to_sent]), to_own.T, to_own @ to_sent.T, row_of)
    ]


def dot(a, b, dims=((1,), (0,))):
    return lax.dot_general(a, b, (dims, ((), ())), preferred_element_type=F32)


NT = ((1,), (1,))
TN = ((0,), (0,))


def norm(x):
    mean = jnp.mean(x, -1, keepdims=True)
    centred = x - mean
    inverse = lax.rsqrt(jnp.mean(centred * centred, -1, keepdims=True) + 1e-05)
    return centred * inverse, inverse


def norm_back(d, normed, inverse, gain):
    dn = d * gain
    return inverse * (
        dn - jnp.mean(dn, -1, keepdims=True) - normed * jnp.mean(dn * normed, -1, keepdims=True)
    )


class Plan:
    def __init__(self, rows, g1, g2):
        self.r = 16 * -(-rows // (16 * g1))
        self.own = -(-rows // self.r)
        self.rows = self.own * self.r
        self.piece = self.r // 2
        self.across = 3 if g2 >= 6 else 1
        self.pieces = 2 * self.across
        self.lanes = HALF // self.across


def kernel(
    sizes, plans,
    field_in, grad_in, region, wqkv_in, wout_in, wup_in, wdown_in, gaina_in, gainm_in,
    gather_in, to_nat_in, collect_in, row_of_in,
    output, grad_field, gat_ab, gat_d,
    field, grad, w_qkv, w_out, w_up, w_down, gain_a, gain_m, gather, to_nat, collect, row_of,
    msg, halo_x, back_src, back_dst, back_f,
    x_q, g_q, h1_q, norm_q, norm_h, t_norm, t_win, wpad, qf, kx, vx, closed,
    qm, p0, p1, p2, tile0, tile1, tile2, heads, own_b,
    h2, act, dpre, dmix, dmixb, downs, dq_all, dk_all, dv_all, dsq, out_q,
    ab_src, d_src, ab_rc, d_rc, ab_s0, d_s0, ab_r1, d_r1, ab_s1, d_s1, ab_r2, d_r2,
    ab_fin, d_fin, ab_sh, d_sh,
    in_sem, halo_send, halo_recv, core_send, core_recv, red_send, red_recv,
):
    nz, ny, nx, nlat = sizes
    nlon = nz * ny * nx
    g1, g2 = ny * (nlat // 2) * nx, nz
    lon = lax.axis_index("lon")
    lat = lax.axis_index("lat")
    core = lax.rem(lat, 2)
    x_at, y_at, z_at = lax.rem(lon, nx), lax.rem(lax.div(lon, nx), ny), lax.div(lon, nx * ny)
    m1 = (y_at * (nlat // 2) + lax.div(lat, 2)) * nx + x_at
    plan_ab, plan_d = plans

    def wrap(i, n):
        return lax.rem(i + n, n)

    def at(dlat, dlon):
        return {"lon": wrap(lon + dlon, nlon), "lat": wrap(lat + dlat, nlat)}

    def peer1(m):
        y = lax.div(m, nx)
        return {
            "lon": (z_at * ny + lax.div(y, nlat // 2)) * nx + lax.rem(m, nx),
            "lat": lax.rem(y, nlat // 2) * 2 + core,
        }

    def peer2(v):
        return {"lon": v * (nx * ny) + lax.rem(lon, nx * ny), "lat": lat}

    sibling = {"lon": lon, "lat": lat + 1 - 2 * core}

    loads = [
        pltpu.make_async_copy(src, dst, in_sem.at[i])
        for i, (src, dst) in enumerate(
            [
                (field_in, field), (gather_in, gather), (row_of_in, row_of), (gaina_in, gain_a),
                (wqkv_in, w_qkv), (grad_in, grad), (wout_in, w_out), (gainm_in, gain_m),
                (wup_in, w_up), (wdown_in, w_down), (to_nat_in, to_nat), (collect_in, collect),
            ]
        )
    ]
    for load in loads:
        load.start()

    barrier = pltpu.get_barrier_semaphore()

    def greet(device):
        pl.semaphore_signal(barrier, inc=1, device_id=device, device_id_type=MESH)

    def greet1(k, _):
        greet(peer1(wrap(m1 + k, g1)))
        return 0

    def greet2(k, _):
        greet(peer2(wrap(z_at + k, g2)))
        return 0

    for way in WAY:
        greet(at(*way))
    greet(sibling)
    lax.fori_loop(1, g1, greet1, 0)
    lax.fori_loop(1, g2, greet2, 0)

    def halo(which, src, dst, sign):
        return [
            pltpu.make_async_remote_copy(
                src_ref=src.at[pl.ds(MAT[i], MROWS[i])],
                dst_ref=dst.at[pl.ds(MAT[i], MROWS[i])],
                send_sem=halo_send.at[which, i],
                recv_sem=halo_recv.at[which, i],
                device_id=at(sign * WAY[i][0], sign * WAY[i][1]),
                device_id_type=MESH,
            )
            for i in range(8)
        ]

    there = halo(0, msg, halo_x, 1)
    back = halo(1, back_src, back_dst, -1)

    lane = lax.broadcasted_iota(jnp.int32, (1, 256), 1)
    for n, tile in ((144, tile0), (72, tile1), (40, tile2)):
        rows = lax.broadcasted_iota(jnp.int32, (n, HEADS * n), 0)
        cols = lax.broadcasted_iota(jnp.int32, (n, HEADS * n), 1)
        hit = jnp.zeros((n, HEADS * n), F32)
        for h in range(HEADS):
            hit = jnp.where(cols == rows + n * h, 1.0, hit)
        tile[...] = hit.astype(BF)
    eye = (
        lax.broadcasted_iota(jnp.int32, (C, C), 0) == lax.broadcasted_iota(jnp.int32, (C, C), 1)
    ).astype(F32).astype(BF)

    loads[0].wait()
    loads[1].wait()
    moved = dot(gather[...], field[...])
    x_q[...] = moved[:NQS]
    msg[...] = moved[NQS:].astype(BF)
    pl.semaphore_wait(barrier, 9 + (g1 - 1) + (g2 - 1))
    for copy in there:
        copy.start()

    loads[2].wait()
    slot = lax.broadcasted_iota(jnp.int32, (32, 256), 0)
    value = jnp.where(slot == BANDS, 3, -1)
    for j in range(BANDS):
        band = region[wrap(lat * ROWS + j - 3, nlat * ROWS)]
        value = jnp.where(slot == j, band, value)
    column = lax.broadcasted_iota(jnp.int32, (32, 256), 1) - C
    band_hot = jnp.where((column >= 0) & (value == column), 1.0, 0.0).astype(BF)
    member = dot(row_of[...], band_hot)
    closed[...] = jnp.where((lane >= C) & (lane < C + 4), (member - 1.0) * 1e30, 0.0)

    for load in loads[3:5]:
        load.wait()
    wpad[...] = jnp.zeros_like(wpad)
    for i in range(3):
        wpad[:, 256 * i : 256 * i + C] = w_qkv[:, C * i : C * i + C]
    gain_attn = gain_a[...]

    normed, inverse1 = norm(x_q[...])
    norm_q[...] = normed
    h1_q[...] = (normed * gain_attn).astype(BF)
    qf[...] = dot(h1_q[...], wpad[:, 0:256]).astype(BF).astype(F32)

    def keys_of(first, last):
        rows = pl.ds(KAT[first], KAT[last] - KAT[first])
        t_win[rows, :] = (t_norm[rows, :] * gain_attn).astype(BF)
        both = dot(t_win[rows, :], wpad[:, 256:768])
        kx[rows, :] = (both[:, 0:256] + member[KAT[first] : KAT[last]]).astype(BF)
        vx[rows, :] = both[:, 256 : 256 + C].astype(BF)

    def kept(w):
        if w == 0:
            return p0, tile0
        return (p1.at[w - 1], tile1) if w < 5 else (p2.at[w - 5], tile2)

    def gather_heads(full, tile):
        n = full.shape[1] // HEADS
        at_lane = lax.broadcasted_iota(jnp.int32, (1, HEADS * n), 1)
        parts = [
            jnp.where(
                (at_lane >= n * h) & (at_lane < n * h + n), full[32 * h : 32 * h + 32], 0.0
            )
            for h in range(HEADS)
        ]
        return dot(tile[...], jnp.concatenate(parts, 0).astype(BF), NT)

    def by_head(inside, outside, width):
        at_lane = lane[:, :width]
        return jnp.concatenate(
            [
                jnp.where((at_lane >= 32 * h) & (at_lane < 32 * h + 32), inside, outside)
                for h in range(HEADS)
            ],
            0,
        ).astype(BF)

    def rows_of(w):
        return pl.ds(QAT[w], NQ[w]), pl.ds(KAT[w], NK[w]), pl.ds(HEADS * QAT[w], HEADS * NQ[w])

    def forward(w):
        q_rows, k_rows, m_rows = rows_of(w)
        keep, tile = kept(w)
        qm[m_rows, :] = by_head(qf[q_rows, :], closed[pl.ds(KAT[w], NQ[w]), :], 256)
        scores = dot(kx[k_rows, :], qm[m_rows, :], NT) * (SCALE * LOG2E)
        top = jnp.max(scores, 0, keepdims=True)
        expo = jnp.exp2(scores - top)
        prob = expo * (1.0 / jnp.sum(expo, 0, keepdims=True))
        keep[...] = prob
        value_t = dot(eye, vx[k_rows, :], NT).astype(BF)
        heads[q_rows, :] = gather_heads(dot(value_t, prob.astype(BF)), tile)

    def backward(w):
        q_rows, k_rows, m_rows = rows_of(w)
        keep, tile = kept(w)
        do = by_head(downs[q_rows, :], 0.0, C)
        prob = keep[...]
        dprob = dot(vx[k_rows, :], do, NT)
        dscore = (prob * (dprob - jnp.sum(dprob * prob, 0, keepdims=True))).astype(BF)
        dv_all[k_rows, :] = dot(prob.astype(BF), do).astype(BF)
        dk_all[k_rows, :] = (dot(dscore, qm[m_rows, 0:C]) * SCALE).astype(BF)
        key_t = dot(eye, kx[k_rows, 0:C], NT).astype(BF)
        dq_all[q_rows, :] = gather_heads(dot(key_t, dscore) * SCALE, tile)

    def mlp(rows):
        x = x_q[rows, :]
        g = g_q[rows, :]
        owned = heads[rows, :].astype(BF)
        own_b[rows, :] = owned
        mixed = x + dot(owned, w_out[...])
        normed2, inverse2 = norm(mixed)
        gain_mlp = gain_m[...]
        h2b = (normed2 * gain_mlp).astype(BF)
        h2[rows, :] = h2b
        pre = dot(h2b, w_up[...])
        square = pre * pre
        tangent = jnp.tanh(0.7978845608 * pre * (1.0 + 0.044715 * square))
        half = 0.5 * (1.0 + tangent)
        actb = (pre * half).astype(BF)
        act[rows, :] = actb
        slope = half + 0.5 * pre * (1.0 - tangent * tangent) * 0.7978845608 * (
            1.0 + 3.0 * 0.044715 * square
        )
        out_q[rows, :] = (mixed + dot(actb, w_down[...], NT)).astype(BF)
        dpreb = (dot(g, w_down[...]) * slope).astype(BF)
        dpre[rows, :] = dpreb
        dh2 = dot(dpreb, w_up[...], NT)
        dm = g.astype(F32) + norm_back(dh2, normed2, inverse2, gain_mlp)
        dmix[rows, :] = dm
        dmb = dm.astype(BF)
        dmixb[rows, :] = dmb
        downs[rows, :] = dot(dmb, w_out[...], NT).astype(BF).astype(F32)
        return jnp.sum(dh2 * normed2, 0, keepdims=True)

    t_norm[0:144, :] = normed[0:144]
    keys_of(0, 1)
    forward(0)
    for load in loads[5:10]:
        load.wait()
    g_q[...] = dot(gather[0:NQS, :], grad[...]).astype(BF)
    term_m = mlp(pl.ds(0, 144))
    backward(0)

    for copy in there:
        copy.wait_recv()
    norm_h[...] = norm(halo_x[...].astype(F32))[0]
    for w in range(1, 9):
        t_norm[pl.ds(KAT[w], NQ[w]), :] = norm_q[pl.ds(QAT[w], NQ[w]), :]
        to = KAT[w] + NQ[w]
        for start, size in PARTS[w]:
            t_norm[pl.ds(to, size), :] = norm_h[pl.ds(start, size), :]
            to += size
    keys_of(1, 9)
    for w in range(1, 9):
        forward(w)
    term_m = term_m + mlp(pl.ds(144, NQS - 144))

    def core_copy(which, stage, src, dst):
        return pltpu.make_async_remote_copy(
            src_ref=src, dst_ref=dst,
            send_sem=core_send.at[which, stage], recv_sem=core_recv.at[which, stage],
            device_id=sibling, device_id_type=MESH,
        )

    def remote(which, stage, k, src, dst, device):
        return pltpu.make_async_remote_copy(
            src_ref=src, dst_ref=dst,
            send_sem=red_send.at[which, stage, k], recv_sem=red_recv.at[which, stage, k],
            device_id=device, device_id_type=MESH,
        )

    def each(n, one, fn, back=None):
        def step(k, _):
            one(k, fn) if back is None else one(k, fn, wrap(back - k, n))
            return 0

        lax.fori_loop(1, n, step, 0)

    def go(copy):
        copy.start()

    def got(copy):
        copy.wait_recv()

    def sent(copy):
        copy.wait_send()

    class Chain:
        def __init__(self, which, plan, src, rc, s0, r1, s1, r2, fin, sh, gat):
            self.which, self.plan = which, plan
            self.src, self.rc, self.s0, self.r1 = src, rc, s0, r1
            self.s1, self.r2, self.fin, self.sh, self.gat = s1, r2, fin, sh, gat
            self.mine = m1 < plan.own
            self.first = core_copy(which, 0, src.at[1 - core], rc)
            self.last = core_copy(which, 1, gat.at[core], gat.at[core])

        def a2a1(self, k, fn):
            target = wrap(m1 + k, g1)
            start = pl.multiple_of(target * self.plan.r, 16)
            copy = remote(
                self.which, 0, k, self.s0.at[pl.ds(start, self.plan.r)], self.r1.at[k],
                peer1(target),
            )
            pl.when(target < self.plan.own)(functools.partial(fn, copy))

        def come1(self, k, fn):
            fn(remote(self.which, 0, k, self.r1.at[k], self.r1.at[k], peer1(wrap(m1 + k, g1))))

        def a2a2(self, k, fn):
            target = wrap(z_at + k, g2)
            copy = remote(self.which, 1, k, self.s1.at[target], self.r2.at[k], peer2(target))
            pl.when(self.mine & (target < self.plan.pieces))(functools.partial(fn, copy))

        def come2(self, k, fn):
            fn(remote(self.which, 1, k, self.r2.at[k], self.r2.at[k], peer2(wrap(z_at + k, g2))))

        def all2(self, k, fn, source=None):
            source = z_at if source is None else source
            copy = remote(
                self.which, 2, k, self.fin.at[source], self.fin.at[source],
                peer2(wrap(z_at + k, g2)),
            )
            pl.when(self.mine & (source < self.plan.pieces))(functools.partial(fn, copy))

        def all1(self, k, fn, source=None):
            source = m1 if source is None else source
            copy = remote(
                self.which, 3, k, self.sh, self.gat.at[core, source], peer1(wrap(m1 + k, g1))
            )
            pl.when(source < self.plan.own)(functools.partial(fn, copy))

        def begin(self):
            self.first.start()

        def pair(self):
            self.first.wait_recv()
            self.s0[...] = (self.src[core] + self.rc[...]).astype(BF)
            each(g1, self.a2a1, go)

        def plane(self):
            plan = self.plan

            @pl.when(self.mine)
            def _():
                each(g1, self.come1, got)
                start = pl.multiple_of(m1 * plan.r, 16)
                total = self.s0[pl.ds(start, plan.r), :].astype(F32)
                for k in range(1, g1):
                    total = total + self.r1[k].astype(F32)
                for j in range(plan.pieces):
                    i, t = j // plan.across, j % plan.across
                    self.s1[j] = total[
                        i * plan.piece : (i + 1) * plan.piece, t * plan.lanes : (t + 1) * plan.lanes
                    ]

            each(g2, self.a2a2, go)

        def line(self):
            @pl.when(self.mine & (z_at < self.plan.pieces))
            def _():
                each(g2, self.come2, got)
                total = self.s1[z_at]
                for k in range(1, g2):
                    total = total + self.r2[k]
                self.fin[z_at] = total

            each(g2, self.all2, go)

        def spread(self):
            each(g2, self.all2, got, z_at)

            @pl.when(self.mine)
            def _():
                across = self.plan.across
                rows = [
                    jnp.concatenate([self.fin[across * i + t] for t in range(across)], 1)
                    for i in range(2)
                ]
                shard = jnp.concatenate(rows, 0).astype(BF)
                self.sh[...] = shard
                self.gat[core, m1] = shard

            each(g1, self.all1, go)

        def collect(self):
            each(g1, self.all1, got, m1)
            self.last.start()

        def end(self):
            self.last.wait_recv()

        def drain(self):
            self.first.wait_send()
            each(g1, self.a2a1, sent)
            each(g2, self.a2a2, sent)
            each(g2, self.all2, sent)
            each(g1, self.all1, sent)
            self.last.wait_send()

    ab = Chain(0, plan_ab, ab_src, ab_rc, ab_s0, ab_r1, ab_s1, ab_r2, ab_fin, ab_sh, gat_ab)
    dd = Chain(1, plan_d, d_src, d_rc, d_s0, d_r1, d_s1, d_r2, d_fin, d_sh, gat_d)

    down_term = dot(g_q[...], act[...], TN)
    up_term = dot(h2[...], dpre[...], TN)
    for i in range(2):
        cols = slice(i * HALF, (i + 1) * HALF)
        ab_src[i, 0:C, :] = down_term[:, cols]
        ab_src[i, C : 2 * C, :] = up_term[:, cols]
        if plan_ab.rows > 2 * C:
            ab_src[i, 2 * C :, :] = jnp.zeros((plan_ab.rows - 2 * C, HALF), F32)
    ab.begin()

    for w in range(1, 9):
        backward(w)
        if w == 4:
            ab.pair()

    dsource = dot(dk_all[...], wpad[:, 256 : 256 + C], NT) + dot(dv_all[...], wpad[:, 512 : 512 + C], NT)
    dq_b = dq_all[...].astype(BF)
    dq_source = dot(dq_b, wpad[:, 0:C], NT)
    back_f[...] = jnp.zeros_like(back_f)
    for w in range(9):
        dsq[pl.ds(QAT[w], NQ[w]), :] = (
            dsource[KAT[w] : KAT[w] + NQ[w]] + dq_source[QAT[w] : QAT[w + 1]]
        )
        to = KAT[w] + NQ[w]
        for start, size in PARTS[w]:
            back_f[pl.ds(start, size), :] = dsource[to : to + size]
            to += size
    back_src[...] = back_f[...].astype(BF)
    for copy in back:
        copy.start()

    term_a = jnp.sum(dsource * t_norm[...], 0, keepdims=True) + jnp.sum(
        dq_source * norm_q[...], 0, keepdims=True
    )
    d_term = jnp.concatenate(
        [
            dot(h1_q[...], dq_b, TN), dot(t_win[...], dk_all[...], TN),
            dot(t_win[...], dv_all[...], TN), dot(own_b[...], dmixb[...], TN),
        ],
        1,
    )
    gains = jnp.concatenate([term_a, term_m], 1)
    first_row = lax.broadcasted_iota(jnp.int32, (16, HALF), 0) == 0
    for i in range(2):
        d_src[i, 0:C, :] = d_term[:, i * HALF : (i + 1) * HALF]
        if plan_d.rows > C + 16:
            d_src[i, C + 16 :, :] = jnp.zeros((plan_d.rows - C - 16, HALF), F32)
    d_src[0, C : C + 16, :] = jnp.where(first_row, jnp.broadcast_to(gains, (16, HALF)), 0.0)
    d_src[1, C : C + 16, :] = jnp.zeros((16, HALF), F32)
    dd.begin()

    ab.plane()
    dd.pair()
    loads[10].wait()
    loads[11].wait()
    output[...] = dot(to_nat[...], out_q[...]).astype(BF)
    for copy in back:
        copy.wait_recv()
    dshift = (dsq[...] + dot(collect[...], back_dst[...])).astype(BF).astype(F32)
    gf = dmix[...] + norm_back(dshift, norm_q[...], inverse1, gain_attn)
    grad_field[...] = dot(to_nat[...], gf.astype(BF)).astype(BF)
    ab.line()
    dd.plane()
    ab.spread()
    dd.line()
    ab.collect()
    dd.spread()
    dd.collect()
    ab.end()
    dd.end()
    for copy in there + back:
        copy.wait_send()
    ab.drain()
    dd.drain()


def final(
    plans, out_n, gf_n, gat_ab, gat_d,
    output, grad_field, grad_qkv, grad_out, grad_up, grad_down_t, grad_ga, grad_gm,
):
    output[...] = out_n[...]
    grad_field[...] = gf_n[...]

    def whole(plan, gat):
        halves = [gat[i].astype(F32).reshape(plan.rows, HALF) for i in range(2)]
        return jnp.concatenate(halves, 1)

    ab = whole(plans[0], gat_ab)
    grad_down_t[...] = ab[:C]
    grad_up[...] = ab[C : 2 * C]
    d = whole(plans[1], gat_d)
    grad_qkv[...] = d[:C, : 3 * C]
    grad_out[...] = d[:C, 3 * C :]
    grad_ga[...] = d[C : C + 1, :C]
    grad_gm[...] = d[C : C + 1, C : 2 * C]


def body(nlon, nlat, field, region, w_qkv, w_out, w_up, w_down, gain_attn, gain_mlp, grad_next):
    sizes = (nlon // 8, 2, 4, nlat) if nlon >= 16 else (nlon // 2, 1, 2, nlat)
    nz, ny, nx, _ = sizes
    g1, g2 = ny * (nlat // 2) * nx, nz
    plans = (Plan(2 * C, g1, g2), Plan(C + 16, g1, g2))
    vmem = pl.BlockSpec(memory_space=pltpu.VMEM)
    smem = pl.BlockSpec(memory_space=pltpu.SMEM)
    hbm = pl.BlockSpec(memory_space=pltpu.HBM)
    V = pltpu.VMEM
    consts = [jnp.asarray(a) for a in tables()]
    operands = [
        field.reshape(TOK, C), grad_next.reshape(TOK, C), region, w_qkv, w_out, w_up, w_down.T,
        gain_attn.reshape(1, C), gain_mlp.reshape(1, C), *consts,
    ]

    def pair(shape_of, kind):
        return [V(shape_of(p), kind) for p in plans]

    shapes = [jax.ShapeDtypeStruct((TOK, C), BF)] * 2 + [
        jax.ShapeDtypeStruct((2, p.own, p.r, HALF), BF) for p in plans
    ]
    scratch = (
        [V(a.shape, a.dtype) for i, a in enumerate(operands) if i != 2]
        + [V((HALO, C), BF)] * 4 + [V((HALO, C), F32)]
        + [
            V((NQS, C), F32), V((NQS, C), BF), V((NQS, C), BF), V((NQS, C), F32),
            V((HALO, C), F32), V((NKS, C), F32), V((NKS, C), BF), V((C, FF), BF),
            V((NQS, 256), F32), V((NKS, 256), BF), V((NKS, C), BF), V((NKS, 256), F32),
            V((HEADS * NQS, 256), BF),
            V((144, HEADS * 144), F32), V((4, 144, HEADS * 72), F32), V((4, 160, HEADS * 40), F32),
            V((144, HEADS * 144), BF), V((72, HEADS * 72), BF), V((40, HEADS * 40), BF),
            V((NQS, C), F32), V((NQS, C), BF),
            V((NQS, C), BF), V((NQS, FF), BF), V((NQS, FF), BF), V((NQS, C), F32),
            V((NQS, C), BF), V((NQS, C), F32), V((NQS, C), F32),
            V((NKS, C), BF), V((NKS, C), BF), V((NQS, C), F32), V((NQS, C), BF),
        ]
        + pair(lambda p: (2, p.rows, HALF), F32)
        + pair(lambda p: (p.rows, HALF), F32)
        + pair(lambda p: (p.rows, HALF), BF)
        + pair(lambda p: (g1, p.r, HALF), BF)
        + pair(lambda p: (p.pieces, p.piece, p.lanes), F32)
        + pair(lambda p: (g2, p.piece, p.lanes), F32)
        + pair(lambda p: (p.pieces, p.piece, p.lanes), F32)
        + pair(lambda p: (p.r, HALF), BF)
        + [
            pltpu.SemaphoreType.DMA((12,)),
            pltpu.SemaphoreType.DMA((2, 8)),
            pltpu.SemaphoreType.DMA((2, 8)),
            pltpu.SemaphoreType.DMA((2, 2)),
            pltpu.SemaphoreType.DMA((2, 2)),
            pltpu.SemaphoreType.DMA((2, 4, 16)),
            pltpu.SemaphoreType.DMA((2, 4, 16)),
        ]
    )
    mids = pl.pallas_call(
        functools.partial(kernel, sizes, plans),
        out_shape=shapes,
        in_specs=[smem if i == 2 else hbm for i in range(len(operands))],
        out_specs=[vmem] * 4,
        scratch_shapes=scratch,
        compiler_params=pltpu.CompilerParams(
            collective_id=0, has_side_effects=True, vmem_limit_bytes=54 << 20
        ),
        name="block",
    )(*operands)
    outs = pl.pallas_call(
        functools.partial(final, plans),
        out_shape=(
            jax.ShapeDtypeStruct((TOK, C), BF),
            jax.ShapeDtypeStruct((TOK, C), BF),
            jax.ShapeDtypeStruct((C, 3 * C), F32),
            jax.ShapeDtypeStruct((C, C), F32),
            jax.ShapeDtypeStruct((C, FF), F32),
            jax.ShapeDtypeStruct((C, FF), F32),
            jax.ShapeDtypeStruct((1, C), F32),
            jax.ShapeDtypeStruct((1, C), F32),
        ),
        in_specs=[vmem] * 4,
        out_specs=[vmem] * 8,
        compiler_params=pltpu.CompilerParams(vmem_limit_bytes=40 << 20),
        name="final",
    )(*mids)
    output, grad_field, grad_qkv, grad_out, grad_up, grad_down_t, grad_ga, grad_gm = outs
    return (
        output.reshape(field.shape), grad_field.reshape(field.shape),
        grad_qkv, grad_out, grad_up, grad_down_t.T, grad_ga.reshape(C), grad_gm.reshape(C),
    )


def solution(mesh):
    grid = P(None, "lat", "lon", None)
    return jax.shard_map(
        functools.partial(body, mesh.shape["lon"], mesh.shape["lat"]),
        mesh=mesh,
        in_specs=(grid, P(), P(), P(), P(), P(), P(), P(), grid),
        out_specs=(grid, grid, P(), P(), P(), P(), P(), P()),
        check_vma=False,
    )
```

```python
import functools

import jax
import jax.numpy as jnp
import ml_dtypes
import numpy as np
from jax import lax
from jax.experimental import pallas as pl
from jax.experimental.pallas import tpu as pltpu
from jax.sharding import PartitionSpec as P

C = 192
HEADS = 6
FF = 768
HALF = 384
ROWS = 12
COLS = 24
TOK = 2 * ROWS * COLS
SCALE = 32.0 ** -0.5
LOG2E = 1.4426950408889634
F32 = jnp.float32
BF = jnp.bfloat16
MESH = pl.DeviceIdType.MESH
VLIM = 54 << 20

NQ = (144,) + (72,) * 4 + (40,) * 4
NK = (144,) + (144,) * 4 + (160,) * 4
QAT = tuple(int(v) for v in np.cumsum((0,) + NQ))
KAT = tuple(int(v) for v in np.cumsum((0,) + NK))
NQS, NKS = QAT[-1], KAT[-1]
WAY = ((0, -1), (0, 1), (-1, 0), (1, 0), (-1, -1), (-1, 1), (1, -1), (1, 1))
MAT = (0, 160, 320, 480, 640, 688, 736, 784)
MROWS = (160,) * 4 + (48,) * 4
HALO = 832
PARTS = (
    (),
    ((0, 72),),
    ((160, 72),),
    ((320, 72),),
    ((480, 72),),
    ((112, 40), (320 + 112, 40), (640, 40)),
    ((160 + 112, 40), (320 + 72, 40), (688, 40)),
    ((72, 40), (480 + 112, 40), (736, 40)),
    ((160 + 72, 40), (480 + 72, 40), (784, 40)),
)
BANDS = 18


def tables():
    def piece(rows, cols, size=None):
        got = [(l * ROWS * COLS + r * COLS + c, r) for l in range(2) for r in rows for c in cols]
        return got + [(-1, None)] * ((size or len(got)) - len(got))

    top, mid, bot = range(0, 3), range(3, 9), range(9, 12)
    left, cen, rig = range(0, 6), range(6, 18), range(18, 24)
    own = [
        piece(mid, cen),
        piece(mid, rig), piece(mid, left), piece(bot, cen), piece(top, cen),
        piece(bot, rig, 40), piece(bot, left, 40), piece(top, rig, 40), piece(top, left, 40),
    ]
    sent = [
        piece(mid, side) + piece(top, side, 40) + piece(bot, side, 48) for side in (left, rig)
    ] + [
        piece(rows, cen) + piece(rows, left, 40) + piece(rows, rig, 48) for rows in (top, bot)
    ] + [
        piece(top, left, 48), piece(top, rig, 48), piece(bot, left, 48), piece(bot, rig, 48),
    ]
    shift = (0, 0, ROWS, -ROWS, ROWS, ROWS, -ROWS, -ROWS)
    flat_own = sum(own, [])
    flat_sent = sum(sent, [])
    moved = sum(
        [[(i, None if r is None else r + s) for i, r in part] for part, s in zip(sent, shift)], []
    )
    assert len(flat_own) == NQS and len(flat_sent) == HALO

    def hot(tokens):
        out = np.zeros((len(tokens), TOK), np.float32)
        for at, (index, _) in enumerate(tokens):
            if index >= 0:
                out[at, index] = 1
        return out

    keys = []
    for w in range(9):
        keys += own[w]
        for start, size in PARTS[w]:
            keys += moved[start : start + size]
    row_of = np.zeros((NKS, 32), np.float32)
    for at, (_, row) in enumerate(keys):
        row_of[at, BANDS if row is None else row + 3] = 1
    to_own, to_sent = hot(flat_own), hot(flat_sent)
    kind = ml_dtypes.bfloat16
    return [
        np.ascontiguousarray(a).astype(kind)
        for a in (np.concatenate([to_own, to_sent]), to_own.T, to_own @ to_sent.T, row_of)
    ]


def dot(a, b, dims=((1,), (0,))):
    return lax.dot_general(a, b, (dims, ((), ())), preferred_element_type=F32)


NT = ((1,), (1,))
TN = ((0,), (0,))


def norm(x):
    mean = jnp.mean(x, -1, keepdims=True)
    centred = x - mean
    inverse = lax.rsqrt(jnp.mean(centred * centred, -1, keepdims=True) + 1e-05)
    return centred * inverse, inverse


def norm_back(d, normed, inverse, gain):
    dn = d * gain
    return inverse * (
        dn - jnp.mean(dn, -1, keepdims=True) - normed * jnp.mean(dn * normed, -1, keepdims=True)
    )


class Plan:
    def __init__(self, rows, g1, g2):
        self.r = 16 * -(-rows // (16 * g1))
        self.own = -(-rows // self.r)
        self.rows = self.own * self.r
        self.piece = self.r // 2
        self.across = 3 if g2 >= 6 else 1
        self.pieces = 2 * self.across
        self.lanes = HALF // self.across


def kernel(
    sizes, plans,
    field_in, grad_in, region, wqkv_in, wout_in, wup_in, wdown_in, gaina_in, gainm_in,
    gather_in, to_nat_in, collect_in, row_of_in,
    output_hbm, grad_field_hbm, gat_ab_hbm, gat_d_hbm,
    output, grad_field, gat_ab, gat_d,
    field, grad, w_qkv, w_out, w_up, w_down, gain_a, gain_m, gather, to_nat, collect, row_of,
    msg, halo_x, back_src, back_dst, back_f,
    x_q, g_q, h1_q, norm_q, norm_h, t_norm, t_win, wpad, qf, kx, vx, closed,
    qm, p0, p1, p2, tile0, tile1, tile2, heads, own_b,
    h2, act, dpre, dmix, dmixb, downs, dq_all, dk_all, dv_all, dsq, out_q,
    ab_src, d_src, ab_rc, d_rc, ab_s0, d_s0, ab_r1, d_r1, ab_s1, d_s1, ab_r2, d_r2,
    ab_fin, d_fin, ab_sh, d_sh,
    in_sem, out_sem, halo_send, halo_recv, core_send, core_recv, red_send, red_recv,
):
    nz, ny, nx, nlat = sizes
    nlon = nz * ny * nx
    g1, g2 = ny * (nlat // 2) * nx, nz
    lon = lax.axis_index("lon")
    lat = lax.axis_index("lat")
    core = lax.rem(lat, 2)
    x_at, y_at, z_at = lax.rem(lon, nx), lax.rem(lax.div(lon, nx), ny), lax.div(lon, nx * ny)
    m1 = (y_at * (nlat // 2) + lax.div(lat, 2)) * nx + x_at
    plan_ab, plan_d = plans

    def wrap(i, n):
        return lax.rem(i + n, n)

    def at(dlat, dlon):
        return {"lon": wrap(lon + dlon, nlon), "lat": wrap(lat + dlat, nlat)}

    def peer1(m):
        y = lax.div(m, nx)
        return {
            "lon": (z_at * ny + lax.div(y, nlat // 2)) * nx + lax.rem(m, nx),
            "lat": lax.rem(y, nlat // 2) * 2 + core,
        }

    def peer2(v):
        return {"lon": v * (nx * ny) + lax.rem(lon, nx * ny), "lat": lat}

    sibling = {"lon": lon, "lat": lat + 1 - 2 * core}

    loads = [
        pltpu.make_async_copy(src, dst, in_sem.at[i])
        for i, (src, dst) in enumerate(
            [
                (field_in, field), (gather_in, gather), (row_of_in, row_of), (gaina_in, gain_a),
                (wqkv_in, w_qkv), (grad_in, grad), (wout_in, w_out), (gainm_in, gain_m),
                (wup_in, w_up), (wdown_in, w_down), (to_nat_in, to_nat), (collect_in, collect),
            ]
        )
    ]
    for load in loads[:2]:
        load.start()
    stores = [
        pltpu.make_async_copy(src, dst, out_sem.at[i])
        for i, (src, dst) in enumerate(
            [
                (output, output_hbm), (grad_field, grad_field_hbm),
                (gat_ab.at[core], gat_ab_hbm.at[core]), (gat_d.at[core], gat_d_hbm.at[core]),
                (gat_ab.at[1 - core], gat_ab_hbm.at[1 - core]),
                (gat_d.at[1 - core], gat_d_hbm.at[1 - core]),
            ]
        )
    ]

    barrier = pltpu.get_barrier_semaphore()

    def greet(device):
        pl.semaphore_signal(barrier, inc=1, device_id=device, device_id_type=MESH)

    def others(n, fn):
        def step(j, _):
            half = lax.div(j, 2)
            fn(n // 2 + jnp.where(lax.rem(j, 2) == 1, half, -half))
            return 0

        lax.fori_loop(1, n, step, 0)

    for way in reversed(WAY):
        greet(at(*way))
    others(g2, lambda k: greet(peer2(wrap(z_at + k, g2))))
    others(g1, lambda k: greet(peer1(wrap(m1 + k, g1))))
    greet(sibling)
    for load in loads[2:]:
        load.start()

    def halo(which, src, dst, sign):
        return [
            pltpu.make_async_remote_copy(
                src_ref=src.at[pl.ds(MAT[i], MROWS[i])],
                dst_ref=dst.at[pl.ds(MAT[i], MROWS[i])],
                send_sem=halo_send.at[which, i],
                recv_sem=halo_recv.at[which, i],
                device_id=at(sign * WAY[i][0], sign * WAY[i][1]),
                device_id_type=MESH,
            )
            for i in range(8)
        ]

    there = halo(0, msg, halo_x, 1)
    back = halo(1, back_src, back_dst, -1)

    lane = lax.broadcasted_iota(jnp.int32, (1, 256), 1)
    for n, tile in ((144, tile0), (72, tile1), (40, tile2)):
        rows = lax.broadcasted_iota(jnp.int32, (n, HEADS * n), 0)
        cols = lax.broadcasted_iota(jnp.int32, (n, HEADS * n), 1)
        hit = jnp.zeros((n, HEADS * n), F32)
        for h in range(HEADS):
            hit = jnp.where(cols == rows + n * h, 1.0, hit)
        tile[...] = hit.astype(BF)
    eye = (
        lax.broadcasted_iota(jnp.int32, (C, C), 0) == lax.broadcasted_iota(jnp.int32, (C, C), 1)
    ).astype(F32).astype(BF)

    loads[0].wait()
    loads[1].wait()
    moved = dot(gather[...], field[...])
    x_q[...] = moved[:NQS]
    msg[...] = moved[NQS:].astype(BF)
    pl.semaphore_wait(barrier, 9 + (g1 - 1) + (g2 - 1))
    for copy in reversed(there):
        copy.start()

    loads[2].wait()
    slot = lax.broadcasted_iota(jnp.int32, (32, 256), 0)
    value = jnp.where(slot == BANDS, 3, -1)
    for j in range(BANDS):
        band = region[wrap(lat * ROWS + j - 3, nlat * ROWS)]
        value = jnp.where(slot == j, band, value)
    column = lax.broadcasted_iota(jnp.int32, (32, 256), 1) - C
    band_hot = jnp.where((column >= 0) & (value == column), 1.0, 0.0).astype(BF)
    member = dot(row_of[...], band_hot)
    closed[...] = jnp.where((lane >= C) & (lane < C + 4), (member - 1.0) * 1e30, 0.0)

    for load in loads[3:5]:
        load.wait()
    wpad[...] = jnp.zeros_like(wpad)
    for i in range(3):
        wpad[:, 256 * i : 256 * i + C] = w_qkv[:, C * i : C * i + C]
    gain_attn = gain_a[...]

    normed, inverse1 = norm(x_q[...])
    norm_q[...] = normed
    h1_q[...] = (normed * gain_attn).astype(BF)
    qf[...] = dot(h1_q[...], wpad[:, 0:256]).astype(BF).astype(F32)

    def keys_of(first, last):
        rows = pl.ds(KAT[first], KAT[last] - KAT[first])
        t_win[rows, :] = (t_norm[rows, :] * gain_attn).astype(BF)
        both = dot(t_win[rows, :], wpad[:, 256:768])
        kx[rows, :] = (both[:, 0:256] + member[KAT[first] : KAT[last]]).astype(BF)
        vx[rows, :] = both[:, 256 : 256 + C].astype(BF)

    def kept(w):
        if w == 0:
            return p0, tile0
        return (p1.at[w - 1], tile1) if w < 5 else (p2.at[w - 5], tile2)

    def gather_heads(full, tile):
        n = full.shape[1] // HEADS
        at_lane = lax.broadcasted_iota(jnp.int32, (1, HEADS * n), 1)
        parts = [
            jnp.where(
                (at_lane >= n * h) & (at_lane < n * h + n), full[32 * h : 32 * h + 32], 0.0
            )
            for h in range(HEADS)
        ]
        return dot(tile[...], jnp.concatenate(parts, 0).astype(BF), NT)

    def by_head(inside, outside, width):
        at_lane = lane[:, :width]
        return jnp.concatenate(
            [
                jnp.where((at_lane >= 32 * h) & (at_lane < 32 * h + 32), inside, outside)
                for h in range(HEADS)
            ],
            0,
        ).astype(BF)

    def rows_of(w):
        return pl.ds(QAT[w], NQ[w]), pl.ds(KAT[w], NK[w]), pl.ds(HEADS * QAT[w], HEADS * NQ[w])

    def forward(w):
        q_rows, k_rows, m_rows = rows_of(w)
        keep, tile = kept(w)
        qm[m_rows, :] = by_head(qf[q_rows, :], closed[pl.ds(KAT[w], NQ[w]), :], 256)
        scores = dot(kx[k_rows, :], qm[m_rows, :], NT) * (SCALE * LOG2E)
        top = jnp.max(scores, 0, keepdims=True)
        expo = jnp.exp2(scores - top)
        prob = expo * (1.0 / jnp.sum(expo, 0, keepdims=True))
        keep[...] = prob
        value_t = dot(eye, vx[k_rows, :], NT).astype(BF)
        heads[q_rows, :] = gather_heads(dot(value_t, prob.astype(BF)), tile)

    def backward(w):
        q_rows, k_rows, m_rows = rows_of(w)
        keep, tile = kept(w)
        do = by_head(downs[q_rows, :], 0.0, C)
        prob = keep[...]
        dprob = dot(vx[k_rows, :], do, NT)
        dscore = (prob * (dprob - jnp.sum(dprob * prob, 0, keepdims=True))).astype(BF)
        dv_all[k_rows, :] = dot(prob.astype(BF), do).astype(BF)
        dk_all[k_rows, :] = (dot(dscore, qm[m_rows, 0:C]) * SCALE).astype(BF)
        key_t = dot(eye, kx[k_rows, 0:C], NT).astype(BF)
        dq_all[q_rows, :] = gather_heads(dot(key_t, dscore) * SCALE, tile)

    def mlp(rows):
        x = x_q[rows, :]
        g = g_q[rows, :]
        owned = heads[rows, :].astype(BF)
        own_b[rows, :] = owned
        mixed = x + dot(owned, w_out[...])
        normed2, inverse2 = norm(mixed)
        gain_mlp = gain_m[...]
        h2b = (normed2 * gain_mlp).astype(BF)
        h2[rows, :] = h2b
        pre = dot(h2b, w_up[...])
        square = pre * pre
        tangent = jnp.tanh(0.7978845608 * pre * (1.0 + 0.044715 * square))
        half = 0.5 * (1.0 + tangent)
        actb = (pre * half).astype(BF)
        act[rows, :] = actb
        slope = half + 0.5 * pre * (1.0 - tangent * tangent) * 0.7978845608 * (
            1.0 + 3.0 * 0.044715 * square
        )
        out_q[rows, :] = (mixed + dot(actb, w_down[...], NT)).astype(BF)
        dpreb = (dot(g, w_down[...]) * slope).astype(BF)
        dpre[rows, :] = dpreb
        dh2 = dot(dpreb, w_up[...], NT)
        dm = g.astype(F32) + norm_back(dh2, normed2, inverse2, gain_mlp)
        dmix[rows, :] = dm
        dmb = dm.astype(BF)
        dmixb[rows, :] = dmb
        downs[rows, :] = dot(dmb, w_out[...], NT).astype(BF).astype(F32)
        return jnp.sum(dh2 * normed2, 0, keepdims=True)

    t_norm[0:144, :] = normed[0:144]
    keys_of(0, 1)
    forward(0)
    for load in loads[5:10]:
        load.wait()
    g_q[...] = dot(gather[0:NQS, :], grad[...]).astype(BF)
    term_m = mlp(pl.ds(0, 144))
    backward(0)

    for copy in there:
        copy.wait_recv()
    norm_h[...] = norm(halo_x[...].astype(F32))[0]
    for w in range(1, 9):
        t_norm[pl.ds(KAT[w], NQ[w]), :] = norm_q[pl.ds(QAT[w], NQ[w]), :]
        to = KAT[w] + NQ[w]
        for start, size in PARTS[w]:
            t_norm[pl.ds(to, size), :] = norm_h[pl.ds(start, size), :]
            to += size
    keys_of(1, 9)
    for w in range(1, 9):
        forward(w)
    term_m = term_m + mlp(pl.ds(144, NQS - 144))

    def core_copy(which, stage, src, dst):
        return pltpu.make_async_remote_copy(
            src_ref=src, dst_ref=dst,
            send_sem=core_send.at[which, stage], recv_sem=core_recv.at[which, stage],
            device_id=sibling, device_id_type=MESH,
        )

    def remote(which, stage, k, src, dst, device):
        return pltpu.make_async_remote_copy(
            src_ref=src, dst_ref=dst,
            send_sem=red_send.at[which, stage, k], recv_sem=red_recv.at[which, stage, k],
            device_id=device, device_id_type=MESH,
        )

    def each(n, one, fn, back=None):
        others(n, lambda k: one(k, fn) if back is None else one(k, fn, wrap(back - k, n)))

    def go(copy):
        copy.start()

    def got(copy):
        copy.wait_recv()

    def sent(copy):
        copy.wait_send()

    class Chain:
        def __init__(self, which, plan, src, rc, s0, r1, s1, r2, fin, sh, gat):
            self.which, self.plan = which, plan
            self.src, self.rc, self.s0, self.r1 = src, rc, s0, r1
            self.s1, self.r2, self.fin, self.sh, self.gat = s1, r2, fin, sh, gat
            self.mine = m1 < plan.own
            self.first = core_copy(which, 0, src.at[1 - core], rc)
            self.last = core_copy(which, 1, gat.at[core], gat.at[core])

        def a2a1(self, k, fn):
            target = wrap(m1 + k, g1)
            start = pl.multiple_of(target * self.plan.r, 16)
            copy = remote(
                self.which, 0, k, self.s0.at[pl.ds(start, self.plan.r)], self.r1.at[k],
                peer1(target),
            )
            pl.when(target < self.plan.own)(functools.partial(fn, copy))

        def come1(self, k, fn):
            fn(remote(self.which, 0, k, self.r1.at[k], self.r1.at[k], peer1(wrap(m1 + k, g1))))

        def a2a2(self, k, fn):
            target = wrap(z_at + k, g2)
            copy = remote(self.which, 1, k, self.s1.at[target], self.r2.at[k], peer2(target))
            pl.when(self.mine & (target < self.plan.pieces))(functools.partial(fn, copy))

        def come2(self, k, fn):
            fn(remote(self.which, 1, k, self.r2.at[k], self.r2.at[k], peer2(wrap(z_at + k, g2))))

        def all2(self, k, fn, source=None):
            source = z_at if source is None else source
            copy = remote(
                self.which, 2, k, self.fin.at[source], self.fin.at[source],
                peer2(wrap(z_at + k, g2)),
            )
            pl.when(self.mine & (source < self.plan.pieces))(functools.partial(fn, copy))

        def all1(self, k, fn, source=None):
            source = m1 if source is None else source
            copy = remote(
                self.which, 3, k, self.sh, self.gat.at[core, source], peer1(wrap(m1 + k, g1))
            )
            pl.when(source < self.plan.own)(functools.partial(fn, copy))

        def begin(self):
            self.first.start()

        def pair(self):
            self.first.wait_recv()
            self.s0[...] = (self.src[core] + self.rc[...]).astype(BF)
            each(g1, self.a2a1, go)

        def plane(self):
            plan = self.plan

            @pl.when(self.mine)
            def _():
                each(g1, self.come1, got)
                start = pl.multiple_of(m1 * plan.r, 16)
                total = self.s0[pl.ds(start, plan.r), :].astype(F32)
                for k in range(1, g1):
                    total = total + self.r1[k].astype(F32)
                for j in range(plan.pieces):
                    i, t = j // plan.across, j % plan.across
                    self.s1[j] = total[
                        i * plan.piece : (i + 1) * plan.piece, t * plan.lanes : (t + 1) * plan.lanes
                    ]

            each(g2, self.a2a2, go)

        def line(self):
            @pl.when(self.mine & (z_at < self.plan.pieces))
            def _():
                each(g2, self.come2, got)
                total = self.s1[z_at]
                for k in range(1, g2):
                    total = total + self.r2[k]
                self.fin[z_at] = total

            each(g2, self.all2, go)

        def spread(self):
            each(g2, self.all2, got, z_at)

            @pl.when(self.mine)
            def _():
                across = self.plan.across
                rows = [
                    jnp.concatenate([self.fin[across * i + t] for t in range(across)], 1)
                    for i in range(2)
                ]
                shard = jnp.concatenate(rows, 0).astype(BF)
                self.sh[...] = shard
                self.gat[core, m1] = shard

            each(g1, self.all1, go)

        def collect(self):
            each(g1, self.all1, got, m1)
            self.last.start()

        def end(self):
            self.last.wait_recv()

        def drain(self):
            self.first.wait_send()
            each(g1, self.a2a1, sent)
            each(g2, self.a2a2, sent)

        def drain_late(self):
            each(g2, self.all2, sent)
            each(g1, self.all1, sent)

    ab = Chain(0, plan_ab, ab_src, ab_rc, ab_s0, ab_r1, ab_s1, ab_r2, ab_fin, ab_sh, gat_ab)
    dd = Chain(1, plan_d, d_src, d_rc, d_s0, d_r1, d_s1, d_r2, d_fin, d_sh, gat_d)

    down_term = dot(g_q[...], act[...], TN)
    up_term = dot(h2[...], dpre[...], TN)
    for i in range(2):
        cols = slice(i * HALF, (i + 1) * HALF)
        ab_src[i, 0:C, :] = down_term[:, cols]
        ab_src[i, C : 2 * C, :] = up_term[:, cols]
        if plan_ab.rows > 2 * C:
            ab_src[i, 2 * C :, :] = jnp.zeros((plan_ab.rows - 2 * C, HALF), F32)
    ab.begin()

    for w in range(1, 9):
        backward(w)
        if w == 4:
            ab.pair()

    dsource = dot(dk_all[...], wpad[:, 256 : 256 + C], NT) + dot(dv_all[...], wpad[:, 512 : 512 + C], NT)
    dq_b = dq_all[...].astype(BF)
    dq_source = dot(dq_b, wpad[:, 0:C], NT)
    back_f[...] = jnp.zeros_like(back_f)
    for w in range(9):
        dsq[pl.ds(QAT[w], NQ[w]), :] = (
            dsource[KAT[w] : KAT[w] + NQ[w]] + dq_source[QAT[w] : QAT[w + 1]]
        )
        to = KAT[w] + NQ[w]
        for start, size in PARTS[w]:
            back_f[pl.ds(start, size), :] = dsource[to : to + size]
            to += size
    back_src[...] = back_f[...].astype(BF)
    for copy in reversed(back):
        copy.start()

    term_a = jnp.sum(dsource * t_norm[...], 0, keepdims=True) + jnp.sum(
        dq_source * norm_q[...], 0, keepdims=True
    )
    d_term = jnp.concatenate(
        [
            dot(h1_q[...], dq_b, TN), dot(t_win[...], dk_all[...], TN),
            dot(t_win[...], dv_all[...], TN), dot(own_b[...], dmixb[...], TN),
        ],
        1,
    )
    gains = jnp.concatenate([term_a, term_m], 1)
    first_row = lax.broadcasted_iota(jnp.int32, (16, HALF), 0) == 0
    for i in range(2):
        d_src[i, 0:C, :] = d_term[:, i * HALF : (i + 1) * HALF]
        if plan_d.rows > C + 16:
            d_src[i, C + 16 :, :] = jnp.zeros((plan_d.rows - C - 16, HALF), F32)
    d_src[0, C : C + 16, :] = jnp.where(first_row, jnp.broadcast_to(gains, (16, HALF)), 0.0)
    d_src[1, C : C + 16, :] = jnp.zeros((16, HALF), F32)
    dd.begin()

    dd.pair()
    loads[10].wait()
    loads[11].wait()
    output[...] = dot(to_nat[...], out_q[...]).astype(BF)
    stores[0].start()
    ab.plane()
    dd.plane()
    for copy in back:
        copy.wait_recv()
    dshift = (dsq[...] + dot(collect[...], back_dst[...])).astype(BF).astype(F32)
    gf = dmix[...] + norm_back(dshift, norm_q[...], inverse1, gain_attn)
    grad_field[...] = dot(to_nat[...], gf.astype(BF)).astype(BF)
    stores[1].start()
    ab.line()
    dd.line()
    ab.spread()
    dd.spread()
    for copy in there + back:
        copy.wait_send()
    ab.drain()
    dd.drain()
    ab.collect()
    stores[2].start()
    dd.collect()
    stores[3].start()
    ab.drain_late()
    dd.drain_late()
    ab.end()
    stores[4].start()
    dd.end()
    stores[5].start()
    ab.last.wait_send()
    dd.last.wait_send()
    for store in stores:
        store.wait()


def final(plans, out_n, gf_n, gat_ab_in, gat_d_in, *refs):
    outs = refs[:8]
    out_v8, gf_v, gat_ab, gat_d, qkv_v, out_v, up_v, down_v, ga_v, gm_v, in_sem, out_sem = refs[8:]
    loads = [
        pltpu.make_async_copy(src, dst, in_sem.at[i])
        for i, (src, dst) in enumerate(
            [(gat_d_in, gat_d), (gat_ab_in, gat_ab), (out_n, out_v8), (gf_n, gf_v)]
        )
    ]
    for load in loads:
        load.start()
    stores = [
        pltpu.make_async_copy(src, dst, out_sem.at[i])
        for i, (src, dst) in enumerate(
            zip((out_v8, gf_v, qkv_v, out_v, up_v, down_v, ga_v, gm_v), outs)
        )
    ]

    def whole(plan, gat):
        halves = [gat[i].astype(F32).reshape(plan.rows, HALF) for i in range(2)]
        return jnp.concatenate(halves, 1)

    loads[0].wait()
    d = whole(plans[1], gat_d)
    qkv_v[...] = d[:C, : 3 * C]
    out_v[...] = d[:C, 3 * C :]
    ga_v[...] = d[C : C + 1, :C]
    gm_v[...] = d[C : C + 1, C : 2 * C]
    for at in (2, 3, 6, 7):
        stores[at].start()
    for at in range(2):
        loads[2 + at].wait()
        stores[at].start()
    loads[1].wait()
    ab = whole(plans[0], gat_ab)
    down_v[...] = ab[:C]
    up_v[...] = ab[C : 2 * C]
    stores[4].start()
    stores[5].start()
    for store in stores:
        store.wait()


def body(nlon, nlat, field, region, w_qkv, w_out, w_up, w_down, gain_attn, gain_mlp, grad_next):
    sizes = (nlon // 8, 2, 4, nlat) if nlon >= 16 else (nlon // 2, 1, 2, nlat)
    nz, ny, nx, _ = sizes
    g1, g2 = ny * (nlat // 2) * nx, nz
    plans = (Plan(2 * C, g1, g2), Plan(C + 16, g1, g2))
    vmem = pl.BlockSpec(memory_space=pltpu.VMEM)
    smem = pl.BlockSpec(memory_space=pltpu.SMEM)
    hbm = pl.BlockSpec(memory_space=pltpu.HBM)
    V = pltpu.VMEM
    consts = [jnp.asarray(a) for a in tables()]
    operands = [
        field.reshape(TOK, C), grad_next.reshape(TOK, C), region, w_qkv, w_out, w_up, w_down.T,
        gain_attn.reshape(1, C), gain_mlp.reshape(1, C), *consts,
    ]

    def pair(shape_of, kind):
        return [V(shape_of(p), kind) for p in plans]

    shapes = [jax.ShapeDtypeStruct((TOK, C), BF)] * 2 + [
        jax.ShapeDtypeStruct((2, p.own, p.r, HALF), BF) for p in plans
    ]
    scratch = (
        [V(a.shape, a.dtype) for a in shapes]
        + [V(a.shape, a.dtype) for i, a in enumerate(operands) if i != 2]
        + [V((HALO, C), BF)] * 4 + [V((HALO, C), F32)]
        + [
            V((NQS, C), F32), V((NQS, C), BF), V((NQS, C), BF), V((NQS, C), F32),
            V((HALO, C), F32), V((NKS, C), F32), V((NKS, C), BF), V((C, FF), BF),
            V((NQS, 256), F32), V((NKS, 256), BF), V((NKS, C), BF), V((NKS, 256), F32),
            V((HEADS * NQS, 256), BF),
            V((144, HEADS * 144), F32), V((4, 144, HEADS * 72), F32), V((4, 160, HEADS * 40), F32),
            V((144, HEADS * 144), BF), V((72, HEADS * 72), BF), V((40, HEADS * 40), BF),
            V((NQS, C), F32), V((NQS, C), BF),
            V((NQS, C), BF), V((NQS, FF), BF), V((NQS, FF), BF), V((NQS, C), F32),
            V((NQS, C), BF), V((NQS, C), F32), V((NQS, C), F32),
            V((NKS, C), BF), V((NKS, C), BF), V((NQS, C), F32), V((NQS, C), BF),
        ]
        + pair(lambda p: (2, p.rows, HALF), F32)
        + pair(lambda p: (p.rows, HALF), F32)
        + pair(lambda p: (p.rows, HALF), BF)
        + pair(lambda p: (g1, p.r, HALF), BF)
        + pair(lambda p: (p.pieces, p.piece, p.lanes), F32)
        + pair(lambda p: (g2, p.piece, p.lanes), F32)
        + pair(lambda p: (p.pieces, p.piece, p.lanes), F32)
        + pair(lambda p: (p.r, HALF), BF)
        + [
            pltpu.SemaphoreType.DMA((12,)),
            pltpu.SemaphoreType.DMA((6,)),
            pltpu.SemaphoreType.DMA((2, 8)),
            pltpu.SemaphoreType.DMA((2, 8)),
            pltpu.SemaphoreType.DMA((2, 2)),
            pltpu.SemaphoreType.DMA((2, 2)),
            pltpu.SemaphoreType.DMA((2, 4, 16)),
            pltpu.SemaphoreType.DMA((2, 4, 16)),
        ]
    )
    mids = pl.pallas_call(
        functools.partial(kernel, sizes, plans),
        out_shape=shapes,
        in_specs=[smem if i == 2 else hbm for i in range(len(operands))],
        out_specs=[hbm] * 4,
        scratch_shapes=scratch,
        compiler_params=pltpu.CompilerParams(
            collective_id=0, has_side_effects=True, vmem_limit_bytes=VLIM
        ),
        name="block",
    )(*operands)
    results = [
        jax.ShapeDtypeStruct((TOK, C), BF),
        jax.ShapeDtypeStruct((TOK, C), BF),
        jax.ShapeDtypeStruct((C, 3 * C), F32),
        jax.ShapeDtypeStruct((C, C), F32),
        jax.ShapeDtypeStruct((C, FF), F32),
        jax.ShapeDtypeStruct((C, FF), F32),
        jax.ShapeDtypeStruct((1, C), F32),
        jax.ShapeDtypeStruct((1, C), F32),
    ]
    outs = pl.pallas_call(
        functools.partial(final, plans),
        out_shape=results,
        in_specs=[hbm] * 4,
        out_specs=[hbm] * 8,
        scratch_shapes=[V(a.shape, a.dtype) for a in shapes + results[2:]]
        + [pltpu.SemaphoreType.DMA((4,)), pltpu.SemaphoreType.DMA((8,))],
        compiler_params=pltpu.CompilerParams(vmem_limit_bytes=VLIM),
        name="final",
    )(*mids)
    output, grad_field, grad_qkv, grad_out, grad_up, grad_down_t, grad_ga, grad_gm = outs
    return (
        output.reshape(field.shape), grad_field.reshape(field.shape),
        grad_qkv, grad_out, grad_up, grad_down_t.T, grad_ga.reshape(C), grad_gm.reshape(C),
    )


def solution(mesh):
    grid = P(None, "lat", "lon", None)
    return jax.shard_map(
        functools.partial(body, mesh.shape["lon"], mesh.shape["lat"]),
        mesh=mesh,
        in_specs=(grid, P(), P(), P(), P(), P(), P(), P(), grid),
        out_specs=(grid, grid, P(), P(), P(), P(), P(), P()),
        check_vma=False,
    )
```

```python
import functools

import jax
import jax.numpy as jnp
import ml_dtypes
import numpy as np
from jax import lax
from jax.experimental import pallas as pl
from jax.experimental.pallas import tpu as pltpu
from jax.sharding import PartitionSpec as P

C = 192
HEADS = 6
FF = 768
HALF = 384
ROWS = 12
COLS = 24
TOK = 2 * ROWS * COLS
SCALE = 32.0 ** -0.5
LOG2E = 1.4426950408889634
F32 = jnp.float32
BF = jnp.bfloat16
MESH = pl.DeviceIdType.MESH
VLIM = 54 << 20

NQ = (144,) + (72,) * 4 + (40,) * 4
NK = (144,) + (144,) * 4 + (160,) * 4
QAT = tuple(int(v) for v in np.cumsum((0,) + NQ))
KAT = tuple(int(v) for v in np.cumsum((0,) + NK))
NQS, NKS = QAT[-1], KAT[-1]
WAY = ((0, -1), (0, 1), (-1, 0), (1, 0), (-1, -1), (-1, 1), (1, -1), (1, 1))
MAT = (0, 160, 320, 480, 640, 688, 736, 784)
MROWS = (160,) * 4 + (48,) * 4
HALO = 832
PARTS = (
    (),
    ((0, 72),),
    ((160, 72),),
    ((320, 72),),
    ((480, 72),),
    ((112, 40), (320 + 112, 40), (640, 40)),
    ((160 + 112, 40), (320 + 72, 40), (688, 40)),
    ((72, 40), (480 + 112, 40), (736, 40)),
    ((160 + 72, 40), (480 + 72, 40), (784, 40)),
)
BANDS = 18


def tables():
    def piece(rows, cols, size=None):
        got = [(l * ROWS * COLS + r * COLS + c, r) for l in range(2) for r in rows for c in cols]
        return got + [(-1, None)] * ((size or len(got)) - len(got))

    top, mid, bot = range(0, 3), range(3, 9), range(9, 12)
    left, cen, rig = range(0, 6), range(6, 18), range(18, 24)
    own = [
        piece(mid, cen),
        piece(mid, rig), piece(mid, left), piece(bot, cen), piece(top, cen),
        piece(bot, rig, 40), piece(bot, left, 40), piece(top, rig, 40), piece(top, left, 40),
    ]
    sent = [
        piece(mid, side) + piece(top, side, 40) + piece(bot, side, 48) for side in (left, rig)
    ] + [
        piece(rows, cen) + piece(rows, left, 40) + piece(rows, rig, 48) for rows in (top, bot)
    ] + [
        piece(top, left, 48), piece(top, rig, 48), piece(bot, left, 48), piece(bot, rig, 48),
    ]
    shift = (0, 0, ROWS, -ROWS, ROWS, ROWS, -ROWS, -ROWS)
    flat_own = sum(own, [])
    flat_sent = sum(sent, [])
    moved = sum(
        [[(i, None if r is None else r + s) for i, r in part] for part, s in zip(sent, shift)], []
    )
    assert len(flat_own) == NQS and len(flat_sent) == HALO

    def hot(tokens):
        out = np.zeros((len(tokens), TOK), np.float32)
        for at, (index, _) in enumerate(tokens):
            if index >= 0:
                out[at, index] = 1
        return out

    keys = []
    for w in range(9):
        keys += own[w]
        for start, size in PARTS[w]:
            keys += moved[start : start + size]
    row_of = np.zeros((NKS, 32), np.float32)
    for at, (_, row) in enumerate(keys):
        row_of[at, BANDS if row is None else row + 3] = 1
    to_own, to_sent = hot(flat_own), hot(flat_sent)
    kind = ml_dtypes.bfloat16
    return [
        np.ascontiguousarray(a).astype(kind)
        for a in (np.concatenate([to_own, to_sent]), to_own.T, to_own @ to_sent.T, row_of)
    ]


def dot(a, b, dims=((1,), (0,))):
    return lax.dot_general(a, b, (dims, ((), ())), preferred_element_type=F32)


NT = ((1,), (1,))
TN = ((0,), (0,))


def norm(x):
    mean = jnp.mean(x, -1, keepdims=True)
    centred = x - mean
    inverse = lax.rsqrt(jnp.mean(centred * centred, -1, keepdims=True) + 1e-05)
    return centred * inverse, inverse


def norm_back(d, normed, inverse, gain):
    dn = d * gain
    return inverse * (
        dn - jnp.mean(dn, -1, keepdims=True) - normed * jnp.mean(dn * normed, -1, keepdims=True)
    )


class Plan:
    def __init__(self, rows, g1, g2):
        self.r = [16 * -(-n // (16 * g1)) for n in rows]
        self.own = max(-(-n // r) for n, r in zip(rows, self.r))
        self.rows = [self.own * r for r in self.r]
        self.at = [0, self.r[0]]
        self.both = sum(self.r)
        self.across = 3 if g2 >= 6 else 1
        self.pieces = 2 * self.across
        self.lanes = HALF // self.across


def kernel(
    sizes, plan,
    field_in, grad_in, region_in, wqkv_in, wout_in, wup_in, wdown_in, gaina_in, gainm_in,
    gather_in, to_nat_in, collect_in, row_of_in,
    output_hbm, grad_field_hbm, gat_hbm,
    output, grad_field, gat,
    field, grad, region, w_qkv, w_out, w_up, w_down, gain_a, gain_m, gather, to_nat, collect, row_of,
    msg, halo_x, back_src, back_dst, back_f,
    x_q, g_q, h1_q, norm_q, norm_h, t_norm, t_win, wpad, qf, kx, vx, closed,
    qm, p0, p1, p2, tile0, tile1, tile2, heads, own_b,
    h2, act, dpre, dmix, dmixb, downs, dq_all, dk_all, dv_all, dsq, out_q,
    ab_src, d_src, ab_rc, d_rc, ab_s0, d_s0, ab_r1, d_r1, s1, r2, fin, sh,
    in_sem, out_sem, halo_send, halo_recv, core_send, core_recv, red_send, red_recv,
):
    nz, ny, nx, nlat = sizes
    nlon = nz * ny * nx
    g1, g2 = ny * (nlat // 2) * nx, nz
    lon = lax.axis_index("lon")
    lat = lax.axis_index("lat")
    core = lax.rem(lat, 2)
    x_at, y_at, z_at = lax.rem(lon, nx), lax.rem(lax.div(lon, nx), ny), lax.div(lon, nx * ny)
    m1 = (y_at * (nlat // 2) + lax.div(lat, 2)) * nx + x_at
    mine = m1 < plan.own

    def wrap(i, n):
        return lax.rem(i + n, n)

    def at(dlat, dlon):
        return {"lon": wrap(lon + dlon, nlon), "lat": wrap(lat + dlat, nlat)}

    def peer1(m):
        y = lax.div(m, nx)
        return {
            "lon": (z_at * ny + lax.div(y, nlat // 2)) * nx + lax.rem(m, nx),
            "lat": lax.rem(y, nlat // 2) * 2 + core,
        }

    def peer2(v):
        return {"lon": v * (nx * ny) + lax.rem(lon, nx * ny), "lat": lat}

    sibling = {"lon": lon, "lat": lat + 1 - 2 * core}

    loads = [
        pltpu.make_async_copy(src, dst, in_sem.at[i])
        for i, (src, dst) in enumerate(
            [
                (field_in, field), (gather_in, gather), (row_of_in, row_of), (gaina_in, gain_a),
                (wqkv_in, w_qkv), (grad_in, grad), (wout_in, w_out), (gainm_in, gain_m),
                (wup_in, w_up), (wdown_in, w_down), (to_nat_in, to_nat), (collect_in, collect),
                (region_in, region),
            ]
        )
    ]
    loads[0].start()
    loads[1].start()
    loads[12].start()
    stores = [
        pltpu.make_async_copy(src, dst, out_sem.at[i])
        for i, (src, dst) in enumerate(
            [
                (output, output_hbm), (grad_field, grad_field_hbm),
                (gat.at[core], gat_hbm.at[core]), (gat.at[1 - core], gat_hbm.at[1 - core]),
            ]
        )
    ]

    barrier = pltpu.get_barrier_semaphore()

    def greet(device):
        pl.semaphore_signal(barrier, inc=1, device_id=device, device_id_type=MESH)

    def others(n, fn):
        def step(j, _):
            half = lax.div(j, 2)
            fn(n // 2 + jnp.where(lax.rem(j, 2) == 1, half, -half))
            return 0

        lax.fori_loop(1, n, step, 0)

    for way in reversed(WAY):
        greet(at(*way))
    others(g2, lambda k: greet(peer2(wrap(z_at + k, g2))))
    others(g1, lambda k: greet(peer1(wrap(m1 + k, g1))))
    greet(sibling)
    for load in loads[2:12]:
        load.start()

    def halo(which, src, dst, sign):
        return [
            pltpu.make_async_remote_copy(
                src_ref=src.at[pl.ds(MAT[i], MROWS[i])],
                dst_ref=dst.at[pl.ds(MAT[i], MROWS[i])],
                send_sem=halo_send.at[which, i],
                recv_sem=halo_recv.at[which, i],
                device_id=at(sign * WAY[i][0], sign * WAY[i][1]),
                device_id_type=MESH,
            )
            for i in range(8)
        ]

    there = halo(0, msg, halo_x, 1)
    back = halo(1, back_src, back_dst, -1)

    lane = lax.broadcasted_iota(jnp.int32, (1, 256), 1)
    for n, tile in ((144, tile0), (72, tile1), (40, tile2)):
        rows = lax.broadcasted_iota(jnp.int32, (n, HEADS * n), 0)
        cols = lax.broadcasted_iota(jnp.int32, (n, HEADS * n), 1)
        hit = jnp.zeros((n, HEADS * n), F32)
        for h in range(HEADS):
            hit = jnp.where(cols == rows + n * h, 1.0, hit)
        tile[...] = hit.astype(BF)
    eye = (
        lax.broadcasted_iota(jnp.int32, (C, C), 0) == lax.broadcasted_iota(jnp.int32, (C, C), 1)
    ).astype(F32).astype(BF)

    loads[0].wait()
    loads[1].wait()
    moved = dot(gather[...], field[...])
    x_q[...] = moved[:NQS]
    msg[...] = moved[NQS:].astype(BF)
    pl.semaphore_wait(barrier, 9 + (g1 - 1) + (g2 - 1))
    for copy in reversed(there):
        copy.start()

    loads[2].wait()
    loads[12].wait()
    slot = lax.broadcasted_iota(jnp.int32, (32, 256), 0)
    value = jnp.where(slot == BANDS, 3, -1)
    for j in range(BANDS):
        band = region[wrap(lat * ROWS + j - 3, nlat * ROWS)]
        value = jnp.where(slot == j, band, value)
    column = lax.broadcasted_iota(jnp.int32, (32, 256), 1) - C
    band_hot = jnp.where((column >= 0) & (value == column), 1.0, 0.0).astype(BF)
    member = dot(row_of[...], band_hot)
    closed[...] = jnp.where((lane >= C) & (lane < C + 4), (member - 1.0) * 1e30, 0.0)

    for load in loads[3:5]:
        load.wait()
    wpad[...] = jnp.zeros_like(wpad)
    for i in range(3):
        wpad[:, 256 * i : 256 * i + C] = w_qkv[:, C * i : C * i + C]
    gain_attn = gain_a[...]

    normed, inverse1 = norm(x_q[...])
    norm_q[...] = normed
    h1_q[...] = (normed * gain_attn).astype(BF)
    qf[...] = dot(h1_q[...], wpad[:, 0:256]).astype(BF).astype(F32)

    def keys_of(first, last):
        rows = pl.ds(KAT[first], KAT[last] - KAT[first])
        t_win[rows, :] = (t_norm[rows, :] * gain_attn).astype(BF)
        both = dot(t_win[rows, :], wpad[:, 256:768])
        kx[rows, :] = (both[:, 0:256] + member[KAT[first] : KAT[last]]).astype(BF)
        vx[rows, :] = both[:, 256 : 256 + C].astype(BF)

    def kept(w):
        if w == 0:
            return p0, tile0
        return (p1.at[w - 1], tile1) if w < 5 else (p2.at[w - 5], tile2)

    def gather_heads(full, tile):
        n = full.shape[1] // HEADS
        at_lane = lax.broadcasted_iota(jnp.int32, (1, HEADS * n), 1)
        parts = [
            jnp.where(
                (at_lane >= n * h) & (at_lane < n * h + n), full[32 * h : 32 * h + 32], 0.0
            )
            for h in range(HEADS)
        ]
        return dot(tile[...], jnp.concatenate(parts, 0).astype(BF), NT)

    def by_head(inside, outside, width):
        at_lane = lane[:, :width]
        return jnp.concatenate(
            [
                jnp.where((at_lane >= 32 * h) & (at_lane < 32 * h + 32), inside, outside)
                for h in range(HEADS)
            ],
            0,
        ).astype(BF)

    def rows_of(w):
        return pl.ds(QAT[w], NQ[w]), pl.ds(KAT[w], NK[w]), pl.ds(HEADS * QAT[w], HEADS * NQ[w])

    def forward(w):
        q_rows, k_rows, m_rows = rows_of(w)
        keep, tile = kept(w)
        qm[m_rows, :] = by_head(qf[q_rows, :], closed[pl.ds(KAT[w], NQ[w]), :], 256)
        scores = dot(kx[k_rows, :], qm[m_rows, :], NT) * (SCALE * LOG2E)
        top = jnp.max(scores, 0, keepdims=True)
        expo = jnp.exp2(scores - top)
        prob = expo * (1.0 / jnp.sum(expo, 0, keepdims=True))
        keep[...] = prob
        value_t = dot(eye, vx[k_rows, :], NT).astype(BF)
        heads[q_rows, :] = gather_heads(dot(value_t, prob.astype(BF)), tile)

    def backward(w):
        q_rows, k_rows, m_rows = rows_of(w)
        keep, tile = kept(w)
        do = by_head(downs[q_rows, :], 0.0, C)
        prob = keep[...]
        dprob = dot(vx[k_rows, :], do, NT)
        dscore = (prob * (dprob - jnp.sum(dprob * prob, 0, keepdims=True))).astype(BF)
        dv_all[k_rows, :] = dot(prob.astype(BF), do).astype(BF)
        dk_all[k_rows, :] = (dot(dscore, qm[m_rows, 0:C]) * SCALE).astype(BF)
        key_t = dot(eye, kx[k_rows, 0:C], NT).astype(BF)
        dq_all[q_rows, :] = gather_heads(dot(key_t, dscore) * SCALE, tile)

    def mlp(rows):
        x = x_q[rows, :]
        g = g_q[rows, :]
        owned = heads[rows, :].astype(BF)
        own_b[rows, :] = owned
        mixed = x + dot(owned, w_out[...])
        normed2, inverse2 = norm(mixed)
        gain_mlp = gain_m[...]
        h2b = (normed2 * gain_mlp).astype(BF)
        h2[rows, :] = h2b
        pre = dot(h2b, w_up[...])
        square = pre * pre
        tangent = jnp.tanh(0.7978845608 * pre * (1.0 + 0.044715 * square))
        half = 0.5 * (1.0 + tangent)
        actb = (pre * half).astype(BF)
        act[rows, :] = actb
        slope = half + 0.5 * pre * (1.0 - tangent * tangent) * 0.7978845608 * (
            1.0 + 3.0 * 0.044715 * square
        )
        out_q[rows, :] = (mixed + dot(actb, w_down[...], NT)).astype(BF)
        dpreb = (dot(g, w_down[...]) * slope).astype(BF)
        dpre[rows, :] = dpreb
        dh2 = dot(dpreb, w_up[...], NT)
        dm = g.astype(F32) + norm_back(dh2, normed2, inverse2, gain_mlp)
        dmix[rows, :] = dm
        dmb = dm.astype(BF)
        dmixb[rows, :] = dmb
        downs[rows, :] = dot(dmb, w_out[...], NT).astype(BF).astype(F32)
        return jnp.sum(dh2 * normed2, 0, keepdims=True)

    t_norm[0:144, :] = normed[0:144]
    keys_of(0, 1)
    forward(0)
    for load in loads[5:10]:
        load.wait()
    g_q[...] = dot(gather[0:NQS, :], grad[...]).astype(BF)
    term_m = mlp(pl.ds(0, 144))
    backward(0)

    def gather_keys(first, last):
        for w in range(first, last):
            t_norm[pl.ds(KAT[w], NQ[w]), :] = norm_q[pl.ds(QAT[w], NQ[w]), :]
            to = KAT[w] + NQ[w]
            for start, size in PARTS[w]:
                t_norm[pl.ds(to, size), :] = norm_h[pl.ds(start, size), :]
                to += size
        keys_of(first, last)
        for w in range(first, last):
            forward(w)

    for first, last in ((0, 4), (4, 8)):
        for copy in there[first:last]:
            copy.wait_recv()
        rows = pl.ds(MAT[first], sum(MROWS[first:last]))
        norm_h[rows, :] = norm(halo_x[rows, :].astype(F32))[0]
        gather_keys(first + 1, last + 1)
    term_m = term_m + mlp(pl.ds(144, NQS - 144))

    def core_copy(which, src, dst):
        return pltpu.make_async_remote_copy(
            src_ref=src, dst_ref=dst,
            send_sem=core_send.at[which], recv_sem=core_recv.at[which],
            device_id=sibling, device_id_type=MESH,
        )

    def remote(stage, k, src, dst, device):
        return pltpu.make_async_remote_copy(
            src_ref=src, dst_ref=dst,
            send_sem=red_send.at[stage, k], recv_sem=red_recv.at[stage, k],
            device_id=device, device_id_type=MESH,
        )

    def each(n, one, fn, back=None):
        others(n, lambda k: one(k, fn) if back is None else one(k, fn, wrap(back - k, n)))

    def go(copy):
        copy.start()

    def got(copy):
        copy.wait_recv()

    def sent(copy):
        copy.wait_send()

    class Chain:
        def __init__(self, which, src, rc, s0, r1):
            self.which, self.r, self.at = which, plan.r[which], plan.at[which] // 2
            self.src, self.rc, self.s0, self.r1 = src, rc, s0, r1
            self.first = core_copy(which, src.at[1 - core], rc)

        def a2a1(self, k, fn):
            target = wrap(m1 + k, g1)
            start = pl.multiple_of(target * self.r, 16)
            copy = remote(
                self.which, k, self.s0.at[pl.ds(start, self.r)], self.r1.at[k], peer1(target)
            )
            pl.when(target < plan.own)(functools.partial(fn, copy))

        def come1(self, k, fn):
            fn(remote(self.which, k, self.r1.at[k], self.r1.at[k], peer1(wrap(m1 + k, g1))))

        def begin(self):
            self.first.start()

        def pair(self):
            self.first.wait_recv()
            self.s0[...] = (self.src[core] + self.rc[...]).astype(BF)
            each(g1, self.a2a1, go)

        def plane(self):
            half = self.r // 2

            @pl.when(mine)
            def _():
                each(g1, self.come1, got)
                start = pl.multiple_of(m1 * self.r, 16)
                total = self.s0[pl.ds(start, self.r), :].astype(F32)
                for k in range(1, g1):
                    total = total + self.r1[k].astype(F32)
                for j in range(plan.pieces):
                    i, t = j // plan.across, j % plan.across
                    s1[j, self.at : self.at + half, :] = total[
                        i * half : (i + 1) * half, t * plan.lanes : (t + 1) * plan.lanes
                    ]

        def drain(self):
            self.first.wait_send()
            each(g1, self.a2a1, sent)

    def a2a2(k, fn):
        target = wrap(z_at + k, g2)
        copy = remote(2, k, s1.at[target], r2.at[k], peer2(target))
        pl.when(mine & (target < plan.pieces))(functools.partial(fn, copy))

    def come2(k, fn):
        fn(remote(2, k, r2.at[k], r2.at[k], peer2(wrap(z_at + k, g2))))

    def all2(k, fn, source=None):
        source = z_at if source is None else source
        copy = remote(3, k, fin.at[source], fin.at[source], peer2(wrap(z_at + k, g2)))
        pl.when(mine & (source < plan.pieces))(functools.partial(fn, copy))

    def all1(k, fn, source=None):
        source = m1 if source is None else source
        copy = remote(4, k, sh, gat.at[core, source], peer1(wrap(m1 + k, g1)))
        pl.when(source < plan.own)(functools.partial(fn, copy))

    last = core_copy(2, gat.at[core], gat.at[core])

    def line():
        @pl.when(mine & (z_at < plan.pieces))
        def _():
            each(g2, come2, got)
            total = s1[z_at]
            for k in range(1, g2):
                total = total + r2[k]
            fin[z_at] = total

        each(g2, all2, go)

    def spread():
        each(g2, all2, got, z_at)

        @pl.when(mine)
        def _():
            halves = [
                jnp.concatenate([fin[plan.across * i + t] for t in range(plan.across)], 1)
                for i in range(2)
            ]
            cut = plan.r[0] // 2
            rows = [half[:cut] for half in halves] + [half[cut:] for half in halves]
            shard = jnp.concatenate(rows, 0).astype(BF)
            sh[...] = shard
            gat[core, m1] = shard

        each(g1, all1, go)

    ab = Chain(0, ab_src, ab_rc, ab_s0, ab_r1)
    dd = Chain(1, d_src, d_rc, d_s0, d_r1)

    down_term = dot(g_q[...], act[...], TN)
    up_term = dot(h2[...], dpre[...], TN)
    for i in range(2):
        cols = slice(i * HALF, (i + 1) * HALF)
        ab_src[i, 0:C, :] = down_term[:, cols]
        ab_src[i, C : 2 * C, :] = up_term[:, cols]
        if plan.rows[0] > 2 * C:
            ab_src[i, 2 * C :, :] = jnp.zeros((plan.rows[0] - 2 * C, HALF), F32)
    ab.begin()

    for w in range(1, 9):
        backward(w)
        if w == 4:
            ab.pair()

    dsource = dot(dk_all[...], wpad[:, 256 : 256 + C], NT) + dot(dv_all[...], wpad[:, 512 : 512 + C], NT)
    dq_b = dq_all[...].astype(BF)
    dq_source = dot(dq_b, wpad[:, 0:C], NT)
    back_f[...] = jnp.zeros_like(back_f)
    for w in range(9):
        dsq[pl.ds(QAT[w], NQ[w]), :] = (
            dsource[KAT[w] : KAT[w] + NQ[w]] + dq_source[QAT[w] : QAT[w + 1]]
        )
        to = KAT[w] + NQ[w]
        for start, size in PARTS[w]:
            back_f[pl.ds(start, size), :] = dsource[to : to + size]
            to += size
    back_src[...] = back_f[...].astype(BF)
    for copy in reversed(back):
        copy.start()

    term_a = jnp.sum(dsource * t_norm[...], 0, keepdims=True) + jnp.sum(
        dq_source * norm_q[...], 0, keepdims=True
    )
    d_term = jnp.concatenate(
        [
            dot(h1_q[...], dq_b, TN), dot(t_win[...], dk_all[...], TN),
            dot(t_win[...], dv_all[...], TN), dot(own_b[...], dmixb[...], TN),
        ],
        1,
    )
    gains = jnp.concatenate([term_a, term_m], 1)
    first_row = lax.broadcasted_iota(jnp.int32, (16, HALF), 0) == 0
    for i in range(2):
        d_src[i, 0:C, :] = d_term[:, i * HALF : (i + 1) * HALF]
        if plan.rows[1] > C + 16:
            d_src[i, C + 16 :, :] = jnp.zeros((plan.rows[1] - C - 16, HALF), F32)
    d_src[0, C : C + 16, :] = jnp.where(first_row, jnp.broadcast_to(gains, (16, HALF)), 0.0)
    d_src[1, C : C + 16, :] = jnp.zeros((16, HALF), F32)
    dd.begin()

    dd.pair()
    loads[10].wait()
    loads[11].wait()
    output[...] = dot(to_nat[...], out_q[...]).astype(BF)
    stores[0].start()
    ab.plane()
    dd.plane()
    each(g2, a2a2, go)
    for copy in back:
        copy.wait_recv()
    dshift = (dsq[...] + dot(collect[...], back_dst[...])).astype(BF).astype(F32)
    gf = dmix[...] + norm_back(dshift, norm_q[...], inverse1, gain_attn)
    grad_field[...] = dot(to_nat[...], gf.astype(BF)).astype(BF)
    stores[1].start()
    for copy in there + back:
        copy.wait_send()
    line()
    ab.drain()
    dd.drain()
    spread()
    each(g2, a2a2, sent)
    each(g2, all2, sent)
    each(g1, all1, got, m1)
    last.start()
    stores[2].start()
    each(g1, all1, sent)
    last.wait_recv()
    stores[3].start()
    last.wait_send()
    for store in stores:
        store.wait()


def final(plan, out_n, gf_n, gat_in, *refs):
    outs = refs[:8]
    out_v8, gf_v, gat, qkv_v, out_v, up_v, down_v, ga_v, gm_v, in_sem, out_sem = refs[8:]
    loads = [
        pltpu.make_async_copy(src, dst, in_sem.at[i])
        for i, (src, dst) in enumerate(
            [(gat_in, gat), (out_n, out_v8), (gf_n, gf_v)]
        )
    ]
    for load in loads:
        load.start()
    stores = [
        pltpu.make_async_copy(src, dst, out_sem.at[i])
        for i, (src, dst) in enumerate(
            zip((out_v8, gf_v, qkv_v, out_v, up_v, down_v, ga_v, gm_v), outs)
        )
    ]

    def whole(which):
        rows = slice(plan.at[which], plan.at[which] + plan.r[which])
        halves = [
            gat[i, :, rows, :].astype(F32).reshape(plan.rows[which], HALF) for i in range(2)
        ]
        return jnp.concatenate(halves, 1)

    loads[0].wait()
    d = whole(1)
    qkv_v[...] = d[:C, : 3 * C]
    out_v[...] = d[:C, 3 * C :]
    ga_v[...] = d[C : C + 1, :C]
    gm_v[...] = d[C : C + 1, C : 2 * C]
    for at in (2, 3, 6, 7):
        stores[at].start()
    for at in range(2):
        loads[1 + at].wait()
        stores[at].start()
    ab = whole(0)
    down_v[...] = ab[:C]
    up_v[...] = ab[C : 2 * C]
    stores[4].start()
    stores[5].start()
    for store in stores:
        store.wait()


def body(nlon, nlat, field, region, w_qkv, w_out, w_up, w_down, gain_attn, gain_mlp, grad_next):
    sizes = (nlon // 8, 2, 4, nlat) if nlon >= 16 else (nlon // 2, 1, 2, nlat)
    nz, ny, nx, _ = sizes
    g1, g2 = ny * (nlat // 2) * nx, nz
    plan = Plan((2 * C, C + 16), g1, g2)
    hbm = pl.BlockSpec(memory_space=pltpu.HBM)
    V = pltpu.VMEM
    consts = [jnp.asarray(a) for a in tables()]
    operands = [
        field.reshape(TOK, C), grad_next.reshape(TOK, C), region, w_qkv, w_out, w_up, w_down.T,
        gain_attn.reshape(1, C), gain_mlp.reshape(1, C), *consts,
    ]

    def pair(shape_of, kind):
        return [V(shape_of(i), kind) for i in range(2)]

    shapes = [jax.ShapeDtypeStruct((TOK, C), BF)] * 2 + [
        jax.ShapeDtypeStruct((2, plan.own, plan.both, HALF), BF)
    ]
    piece = (plan.both // 2, plan.lanes)
    scratch = (
        [V(a.shape, a.dtype) for a in shapes]
        + [(pltpu.SMEM if i == 2 else V)(a.shape, a.dtype) for i, a in enumerate(operands)]
        + [V((HALO, C), BF)] * 4 + [V((HALO, C), F32)]
        + [
            V((NQS, C), F32), V((NQS, C), BF), V((NQS, C), BF), V((NQS, C), F32),
            V((HALO, C), F32), V((NKS, C), F32), V((NKS, C), BF), V((C, FF), BF),
            V((NQS, 256), F32), V((NKS, 256), BF), V((NKS, C), BF), V((NKS, 256), F32),
            V((HEADS * NQS, 256), BF),
            V((144, HEADS * 144), F32), V((4, 144, HEADS * 72), F32), V((4, 160, HEADS * 40), F32),
            V((144, HEADS * 144), BF), V((72, HEADS * 72), BF), V((40, HEADS * 40), BF),
            V((NQS, C), F32), V((NQS, C), BF),
            V((NQS, C), BF), V((NQS, FF), BF), V((NQS, FF), BF), V((NQS, C), F32),
            V((NQS, C), BF), V((NQS, C), F32), V((NQS, C), F32),
            V((NKS, C), BF), V((NKS, C), BF), V((NQS, C), F32), V((NQS, C), BF),
        ]
        + pair(lambda i: (2, plan.rows[i], HALF), F32)
        + pair(lambda i: (plan.rows[i], HALF), F32)
        + pair(lambda i: (plan.rows[i], HALF), BF)
        + pair(lambda i: (g1, plan.r[i], HALF), BF)
        + [
            V((plan.pieces, *piece), F32), V((g2, *piece), F32), V((plan.pieces, *piece), F32),
            V((plan.both, HALF), BF),
        ]
        + [
            pltpu.SemaphoreType.DMA((13,)),
            pltpu.SemaphoreType.DMA((4,)),
            pltpu.SemaphoreType.DMA((2, 8)),
            pltpu.SemaphoreType.DMA((2, 8)),
            pltpu.SemaphoreType.DMA((3,)),
            pltpu.SemaphoreType.DMA((3,)),
            pltpu.SemaphoreType.DMA((5, 16)),
            pltpu.SemaphoreType.DMA((5, 16)),
        ]
    )
    mids = pl.pallas_call(
        functools.partial(kernel, sizes, plan),
        out_shape=shapes,
        in_specs=[hbm] * len(operands),
        out_specs=[hbm] * 3,
        scratch_shapes=scratch,
        compiler_params=pltpu.CompilerParams(
            collective_id=0, has_side_effects=True, vmem_limit_bytes=VLIM
        ),
        name="block",
    )(*operands)
    results = [
        jax.ShapeDtypeStruct((TOK, C), BF),
        jax.ShapeDtypeStruct((TOK, C), BF),
        jax.ShapeDtypeStruct((C, 3 * C), F32),
        jax.ShapeDtypeStruct((C, C), F32),
        jax.ShapeDtypeStruct((C, FF), F32),
        jax.ShapeDtypeStruct((C, FF), F32),
        jax.ShapeDtypeStruct((1, C), F32),
        jax.ShapeDtypeStruct((1, C), F32),
    ]
    outs = pl.pallas_call(
        functools.partial(final, plan),
        out_shape=results,
        in_specs=[hbm] * 3,
        out_specs=[hbm] * 8,
        scratch_shapes=[V(a.shape, a.dtype) for a in shapes + results[2:]]
        + [pltpu.SemaphoreType.DMA((3,)), pltpu.SemaphoreType.DMA((8,))],
        compiler_params=pltpu.CompilerParams(vmem_limit_bytes=VLIM),
        name="final",
    )(*mids)
    output, grad_field, grad_qkv, grad_out, grad_up, grad_down_t, grad_ga, grad_gm = outs
    return (
        output.reshape(field.shape), grad_field.reshape(field.shape),
        grad_qkv, grad_out, grad_up, grad_down_t.T, grad_ga.reshape(C), grad_gm.reshape(C),
    )


def solution(mesh):
    grid = P(None, "lat", "lon", None)
    return jax.shard_map(
        functools.partial(body, mesh.shape["lon"], mesh.shape["lat"]),
        mesh=mesh,
        in_specs=(grid, P(), P(), P(), P(), P(), P(), P(), grid),
        out_specs=(grid, grid, P(), P(), P(), P(), P(), P()),
        check_vma=False,
    )
```

```python
import functools

import jax
import jax.numpy as jnp
import ml_dtypes
import numpy as np
from jax import lax
from jax.experimental import pallas as pl
from jax.experimental.pallas import tpu as pltpu
from jax.sharding import PartitionSpec as P

C = 192
HEADS = 6
FF = 768
HALF = 384
ROWS = 12
COLS = 24
TOK = 2 * ROWS * COLS
SCALE = 32.0 ** -0.5
LOG2E = 1.4426950408889634
F32 = jnp.float32
BF = jnp.bfloat16
MESH = pl.DeviceIdType.MESH
VLIM = 54 << 20

NQ = (144,) + (72,) * 4 + (40,) * 4
NK = (144,) + (144,) * 4 + (160,) * 4
QAT = tuple(int(v) for v in np.cumsum((0,) + NQ))
KAT = tuple(int(v) for v in np.cumsum((0,) + NK))
NQS, NKS = QAT[-1], KAT[-1]
WAY = ((0, -1), (0, 1), (-1, 0), (1, 0), (-1, -1), (-1, 1), (1, -1), (1, 1))
MAT = (0, 160, 320, 480, 640, 688, 736, 784)
MROWS = (160,) * 4 + (48,) * 4
HALO = 832
PARTS = (
    (),
    ((0, 72),),
    ((160, 72),),
    ((320, 72),),
    ((480, 72),),
    ((112, 40), (320 + 112, 40), (640, 40)),
    ((160 + 112, 40), (320 + 72, 40), (688, 40)),
    ((72, 40), (480 + 112, 40), (736, 40)),
    ((160 + 72, 40), (480 + 72, 40), (784, 40)),
)
BANDS = 18


def tables():
    def piece(rows, cols, size=None):
        got = [(l * ROWS * COLS + r * COLS + c, r) for l in range(2) for r in rows for c in cols]
        return got + [(-1, None)] * ((size or len(got)) - len(got))

    top, mid, bot = range(0, 3), range(3, 9), range(9, 12)
    left, cen, rig = range(0, 6), range(6, 18), range(18, 24)
    own = [
        piece(mid, cen),
        piece(mid, rig), piece(mid, left), piece(bot, cen), piece(top, cen),
        piece(bot, rig, 40), piece(bot, left, 40), piece(top, rig, 40), piece(top, left, 40),
    ]
    sent = [
        piece(mid, side) + piece(top, side, 40) + piece(bot, side, 48) for side in (left, rig)
    ] + [
        piece(rows, cen) + piece(rows, left, 40) + piece(rows, rig, 48) for rows in (top, bot)
    ] + [
        piece(top, left, 48), piece(top, rig, 48), piece(bot, left, 48), piece(bot, rig, 48),
    ]
    shift = (0, 0, ROWS, -ROWS, ROWS, ROWS, -ROWS, -ROWS)
    flat_own = sum(own, [])
    flat_sent = sum(sent, [])
    moved = sum(
        [[(i, None if r is None else r + s) for i, r in part] for part, s in zip(sent, shift)], []
    )
    assert len(flat_own) == NQS and len(flat_sent) == HALO

    def hot(tokens):
        out = np.zeros((len(tokens), TOK), np.float32)
        for at, (index, _) in enumerate(tokens):
            if index >= 0:
                out[at, index] = 1
        return out

    keys = []
    for w in range(9):
        keys += own[w]
        for start, size in PARTS[w]:
            keys += moved[start : start + size]
    row_of = np.zeros((NKS, 32), np.float32)
    for at, (_, row) in enumerate(keys):
        row_of[at, BANDS if row is None else row + 3] = 1
    to_own, to_sent = hot(flat_own), hot(flat_sent)
    kind = ml_dtypes.bfloat16
    return [
        np.ascontiguousarray(a).astype(kind)
        for a in (np.concatenate([to_own, to_sent]), to_own.T, to_own @ to_sent.T, row_of)
    ]


def dot(a, b, dims=((1,), (0,))):
    return lax.dot_general(a, b, (dims, ((), ())), preferred_element_type=F32)


NT = ((1,), (1,))
TN = ((0,), (0,))


def norm(x):
    mean = jnp.mean(x, -1, keepdims=True)
    centred = x - mean
    inverse = lax.rsqrt(jnp.mean(centred * centred, -1, keepdims=True) + 1e-05)
    return centred * inverse, inverse


def norm_back(d, normed, inverse, gain):
    dn = d * gain
    return inverse * (
        dn - jnp.mean(dn, -1, keepdims=True) - normed * jnp.mean(dn * normed, -1, keepdims=True)
    )


class Plan:
    def __init__(self, rows, g1, g2):
        self.r = 16 * -(-rows // (16 * g1))
        self.own = -(-rows // self.r)
        self.rows = self.own * self.r
        self.piece = self.r // 2
        self.across = 3 if g2 >= 6 else 1
        self.pieces = 2 * self.across
        self.lanes = HALF // self.across


def kernel(
    sizes, plans,
    field_in, grad_in, region_in, wqkv_in, wout_in, wup_in, wdown_in, gaina_in, gainm_in,
    gather_in, to_nat_in, collect_in, row_of_in,
    output_hbm, grad_field_hbm, gat_ab_hbm, gat_d_hbm,
    output, grad_field, gat_ab, gat_d,
    field, grad, region, w_qkv, w_out, w_up, w_down, gain_a, gain_m, gather, to_nat, collect, row_of,
    msg, halo_x, back_src, back_dst, back_f,
    x_q, g_q, h1_q, norm_q, norm_h, t_norm, t_win, wpad, qf, kx, vx, closed,
    qm, p0, p1, p2, tile0, tile1, tile2, heads, own_b,
    h2, act, dpre, dmix, dmixb, downs, dq_all, dk_all, dv_all, dsq, out_q,
    ab_src, d_src, ab_rc, d_rc, ab_s0, d_s0, ab_r1, d_r1, ab_s1, d_s1, ab_r2, d_r2,
    ab_fin, d_fin, ab_sh, d_sh,
    in_sem, out_sem, halo_send, halo_recv, core_send, core_recv, red_send, red_recv,
):
    nz, ny, nx, nlat = sizes
    nlon = nz * ny * nx
    g1, g2 = ny * (nlat // 2) * nx, nz
    lon = lax.axis_index("lon")
    lat = lax.axis_index("lat")
    core = lax.rem(lat, 2)
    x_at, y_at, z_at = lax.rem(lon, nx), lax.rem(lax.div(lon, nx), ny), lax.div(lon, nx * ny)
    m1 = (y_at * (nlat // 2) + lax.div(lat, 2)) * nx + x_at
    plan_ab, plan_d = plans

    def wrap(i, n):
        return lax.rem(i + n, n)

    def at(dlat, dlon):
        return {"lon": wrap(lon + dlon, nlon), "lat": wrap(lat + dlat, nlat)}

    def peer1(m):
        y = lax.div(m, nx)
        return {
            "lon": (z_at * ny + lax.div(y, nlat // 2)) * nx + lax.rem(m, nx),
            "lat": lax.rem(y, nlat // 2) * 2 + core,
        }

    def peer2(v):
        return {"lon": v * (nx * ny) + lax.rem(lon, nx * ny), "lat": lat}

    sibling = {"lon": lon, "lat": lat + 1 - 2 * core}

    loads = [
        pltpu.make_async_copy(src, dst, in_sem.at[i])
        for i, (src, dst) in enumerate(
            [
                (field_in, field), (gather_in, gather), (row_of_in, row_of), (gaina_in, gain_a),
                (wqkv_in, w_qkv), (grad_in, grad), (wout_in, w_out), (gainm_in, gain_m),
                (wup_in, w_up), (wdown_in, w_down), (to_nat_in, to_nat), (collect_in, collect),
                (region_in, region),
            ]
        )
    ]
    loads[0].start()
    loads[1].start()
    loads[12].start()
    stores = [
        pltpu.make_async_copy(src, dst, out_sem.at[i])
        for i, (src, dst) in enumerate(
            [
                (output, output_hbm), (grad_field, grad_field_hbm),
                (gat_ab.at[core], gat_ab_hbm.at[core]), (gat_d.at[core], gat_d_hbm.at[core]),
                (gat_ab.at[1 - core], gat_ab_hbm.at[1 - core]),
                (gat_d.at[1 - core], gat_d_hbm.at[1 - core]),
            ]
        )
    ]

    barrier = pltpu.get_barrier_semaphore()

    def greet(device):
        pl.semaphore_signal(barrier, inc=1, device_id=device, device_id_type=MESH)

    def others(n, fn):
        def step(j, _):
            half = lax.div(j, 2)
            fn(n // 2 + jnp.where(lax.rem(j, 2) == 1, half, -half))
            return 0

        lax.fori_loop(1, n, step, 0)

    for way in reversed(WAY):
        greet(at(*way))
    others(g2, lambda k: greet(peer2(wrap(z_at + k, g2))))
    others(g1, lambda k: greet(peer1(wrap(m1 + k, g1))))
    greet(sibling)
    for load in loads[2:12]:
        load.start()

    def halo(which, src, dst, sign):
        return [
            pltpu.make_async_remote_copy(
                src_ref=src.at[pl.ds(MAT[i], MROWS[i])],
                dst_ref=dst.at[pl.ds(MAT[i], MROWS[i])],
                send_sem=halo_send.at[which, i],
                recv_sem=halo_recv.at[which, i],
                device_id=at(sign * WAY[i][0], sign * WAY[i][1]),
                device_id_type=MESH,
            )
            for i in range(8)
        ]

    there = halo(0, msg, halo_x, 1)
    back = halo(1, back_src, back_dst, -1)

    lane = lax.broadcasted_iota(jnp.int32, (1, 256), 1)
    for n, tile in ((144, tile0), (72, tile1), (40, tile2)):
        rows = lax.broadcasted_iota(jnp.int32, (n, HEADS * n), 0)
        cols = lax.broadcasted_iota(jnp.int32, (n, HEADS * n), 1)
        hit = jnp.zeros((n, HEADS * n), F32)
        for h in range(HEADS):
            hit = jnp.where(cols == rows + n * h, 1.0, hit)
        tile[...] = hit.astype(BF)
    eye = (
        lax.broadcasted_iota(jnp.int32, (C, C), 0) == lax.broadcasted_iota(jnp.int32, (C, C), 1)
    ).astype(F32).astype(BF)

    loads[0].wait()
    loads[1].wait()
    msg[...] = dot(gather[NQS:, :], field[...]).astype(BF)
    pl.semaphore_wait(barrier, 9 + (g1 - 1) + (g2 - 1))
    for copy in reversed(there):
        copy.start()
    x_q[...] = dot(gather[0:NQS, :], field[...])

    loads[2].wait()
    loads[12].wait()
    slot = lax.broadcasted_iota(jnp.int32, (32, 256), 0)
    value = jnp.where(slot == BANDS, 3, -1)
    for j in range(BANDS):
        band = region[wrap(lat * ROWS + j - 3, nlat * ROWS)]
        value = jnp.where(slot == j, band, value)
    column = lax.broadcasted_iota(jnp.int32, (32, 256), 1) - C
    band_hot = jnp.where((column >= 0) & (value == column), 1.0, 0.0).astype(BF)
    member = dot(row_of[...], band_hot)
    closed[...] = jnp.where((lane >= C) & (lane < C + 4), (member - 1.0) * 1e30, 0.0)

    for load in loads[3:5]:
        load.wait()
    wpad[...] = jnp.zeros_like(wpad)
    for i in range(3):
        wpad[:, 256 * i : 256 * i + C] = w_qkv[:, C * i : C * i + C]
    gain_attn = gain_a[...]

    normed, inverse1 = norm(x_q[...])
    norm_q[...] = normed
    h1_q[...] = (normed * gain_attn).astype(BF)
    qf[...] = dot(h1_q[...], wpad[:, 0:256]).astype(BF).astype(F32)

    def keys_of(first, last):
        rows = pl.ds(KAT[first], KAT[last] - KAT[first])
        t_win[rows, :] = (t_norm[rows, :] * gain_attn).astype(BF)
        both = dot(t_win[rows, :], wpad[:, 256:768])
        kx[rows, :] = (both[:, 0:256] + member[KAT[first] : KAT[last]]).astype(BF)
        vx[rows, :] = both[:, 256 : 256 + C].astype(BF)

    def kept(w):
        if w == 0:
            return p0, tile0
        return (p1.at[w - 1], tile1) if w < 5 else (p2.at[w - 5], tile2)

    def gather_heads(full, tile):
        n = full.shape[1] // HEADS
        at_lane = lax.broadcasted_iota(jnp.int32, (1, HEADS * n), 1)
        parts = [
            jnp.where(
                (at_lane >= n * h) & (at_lane < n * h + n), full[32 * h : 32 * h + 32], 0.0
            )
            for h in range(HEADS)
        ]
        return dot(tile[...], jnp.concatenate(parts, 0).astype(BF), NT)

    def by_head(inside, outside, width):
        at_lane = lane[:, :width]
        return jnp.concatenate(
            [
                jnp.where((at_lane >= 32 * h) & (at_lane < 32 * h + 32), inside, outside)
                for h in range(HEADS)
            ],
            0,
        ).astype(BF)

    def rows_of(w):
        return pl.ds(QAT[w], NQ[w]), pl.ds(KAT[w], NK[w]), pl.ds(HEADS * QAT[w], HEADS * NQ[w])

    def forward(w):
        q_rows, k_rows, m_rows = rows_of(w)
        keep, tile = kept(w)
        qm[m_rows, :] = by_head(qf[q_rows, :], closed[pl.ds(KAT[w], NQ[w]), :], 256)
        scores = dot(kx[k_rows, :], qm[m_rows, :], NT) * (SCALE * LOG2E)
        top = jnp.max(scores, 0, keepdims=True)
        expo = jnp.exp2(scores - top)
        prob = expo * (1.0 / jnp.sum(expo, 0, keepdims=True))
        keep[...] = prob
        value_t = dot(eye, vx[k_rows, :], NT).astype(BF)
        heads[q_rows, :] = gather_heads(dot(value_t, prob.astype(BF)), tile)

    def backward(w):
        q_rows, k_rows, m_rows = rows_of(w)
        keep, tile = kept(w)
        do = by_head(downs[q_rows, :], 0.0, C)
        prob = keep[...]
        dprob = dot(vx[k_rows, :], do, NT)
        dscore = (prob * (dprob - jnp.sum(dprob * prob, 0, keepdims=True))).astype(BF)
        dv_all[k_rows, :] = dot(prob.astype(BF), do).astype(BF)
        dk_all[k_rows, :] = (dot(dscore, qm[m_rows, 0:C]) * SCALE).astype(BF)
        key_t = dot(eye, kx[k_rows, 0:C], NT).astype(BF)
        dq_all[q_rows, :] = gather_heads(dot(key_t, dscore) * SCALE, tile)

    def mlp(rows):
        x = x_q[rows, :]
        g = g_q[rows, :]
        owned = heads[rows, :].astype(BF)
        own_b[rows, :] = owned
        mixed = x + dot(owned, w_out[...])
        normed2, inverse2 = norm(mixed)
        gain_mlp = gain_m[...]
        h2b = (normed2 * gain_mlp).astype(BF)
        h2[rows, :] = h2b
        pre = dot(h2b, w_up[...])
        square = pre * pre
        tangent = jnp.tanh(0.7978845608 * pre * (1.0 + 0.044715 * square))
        half = 0.5 * (1.0 + tangent)
        actb = (pre * half).astype(BF)
        act[rows, :] = actb
        slope = half + 0.5 * pre * (1.0 - tangent * tangent) * 0.7978845608 * (
            1.0 + 3.0 * 0.044715 * square
        )
        out_q[rows, :] = (mixed + dot(actb, w_down[...], NT)).astype(BF)
        dpreb = (dot(g, w_down[...]) * slope).astype(BF)
        dpre[rows, :] = dpreb
        dh2 = dot(dpreb, w_up[...], NT)
        dm = g.astype(F32) + norm_back(dh2, normed2, inverse2, gain_mlp)
        dmix[rows, :] = dm
        dmb = dm.astype(BF)
        dmixb[rows, :] = dmb
        downs[rows, :] = dot(dmb, w_out[...], NT).astype(BF).astype(F32)
        return jnp.sum(dh2 * normed2, 0, keepdims=True)

    t_norm[0:144, :] = normed[0:144]
    keys_of(0, 1)
    forward(0)
    for load in loads[5:10]:
        load.wait()
    g_q[...] = dot(gather[0:NQS, :], grad[...]).astype(BF)
    term_m = mlp(pl.ds(0, 144))
    backward(0)

    for copy in there:
        copy.wait_recv()
    norm_h[...] = norm(halo_x[...].astype(F32))[0]
    for w in range(1, 9):
        t_norm[pl.ds(KAT[w], NQ[w]), :] = norm_q[pl.ds(QAT[w], NQ[w]), :]
        to = KAT[w] + NQ[w]
        for start, size in PARTS[w]:
            t_norm[pl.ds(to, size), :] = norm_h[pl.ds(start, size), :]
            to += size
    keys_of(1, 9)
    for w in range(1, 9):
        forward(w)
    term_m = term_m + mlp(pl.ds(144, NQS - 144))

    def core_copy(which, stage, src, dst):
        return pltpu.make_async_remote_copy(
            src_ref=src, dst_ref=dst,
            send_sem=core_send.at[which, stage], recv_sem=core_recv.at[which, stage],
            device_id=sibling, device_id_type=MESH,
        )

    def remote(which, stage, k, src, dst, device):
        return pltpu.make_async_remote_copy(
            src_ref=src, dst_ref=dst,
            send_sem=red_send.at[which, stage, k], recv_sem=red_recv.at[which, stage, k],
            device_id=device, device_id_type=MESH,
        )

    def each(n, one, fn, back=None):
        others(n, lambda k: one(k, fn) if back is None else one(k, fn, wrap(back - k, n)))

    def go(copy):
        copy.start()

    def got(copy):
        copy.wait_recv()

    def sent(copy):
        copy.wait_send()

    class Chain:
        def __init__(self, which, plan, src, rc, s0, r1, s1, r2, fin, sh, gat):
            self.which, self.plan = which, plan
            self.src, self.rc, self.s0, self.r1 = src, rc, s0, r1
            self.s1, self.r2, self.fin, self.sh, self.gat = s1, r2, fin, sh, gat
            self.mine = m1 < plan.own
            self.first = core_copy(which, 0, src.at[1 - core], rc)
            self.last = core_copy(which, 1, gat.at[core], gat.at[core])

        def a2a1(self, k, fn):
            target = wrap(m1 + k, g1)
            start = pl.multiple_of(target * self.plan.r, 16)
            copy = remote(
                self.which, 0, k, self.s0.at[pl.ds(start, self.plan.r)], self.r1.at[k],
                peer1(target),
            )
            pl.when(target < self.plan.own)(functools.partial(fn, copy))

        def come1(self, k, fn):
            fn(remote(self.which, 0, k, self.r1.at[k], self.r1.at[k], peer1(wrap(m1 + k, g1))))

        def a2a2(self, k, fn):
            target = wrap(z_at + k, g2)
            copy = remote(self.which, 1, k, self.s1.at[target], self.r2.at[k], peer2(target))
            pl.when(self.mine & (target < self.plan.pieces))(functools.partial(fn, copy))

        def come2(self, k, fn):
            fn(remote(self.which, 1, k, self.r2.at[k], self.r2.at[k], peer2(wrap(z_at + k, g2))))

        def all2(self, k, fn, source=None):
            source = z_at if source is None else source
            copy = remote(
                self.which, 2, k, self.fin.at[source], self.fin.at[source],
                peer2(wrap(z_at + k, g2)),
            )
            pl.when(self.mine & (source < self.plan.pieces))(functools.partial(fn, copy))

        def all1(self, k, fn, source=None):
            source = m1 if source is None else source
            copy = remote(
                self.which, 3, k, self.sh, self.gat.at[core, source], peer1(wrap(m1 + k, g1))
            )
            pl.when(source < self.plan.own)(functools.partial(fn, copy))

        def begin(self):
            self.first.start()

        def pair(self):
            self.first.wait_recv()
            self.s0[...] = (self.src[core] + self.rc[...]).astype(BF)
            each(g1, self.a2a1, go)

        def plane(self):
            plan = self.plan

            @pl.when(self.mine)
            def _():
                each(g1, self.come1, got)
                start = pl.multiple_of(m1 * plan.r, 16)
                total = self.s0[pl.ds(start, plan.r), :].astype(F32)
                for k in range(1, g1):
                    total = total + self.r1[k].astype(F32)
                for j in range(plan.pieces):
                    i, t = j // plan.across, j % plan.across
                    self.s1[j] = total[
                        i * plan.piece : (i + 1) * plan.piece, t * plan.lanes : (t + 1) * plan.lanes
                    ]

            each(g2, self.a2a2, go)

        def line(self):
            @pl.when(self.mine & (z_at < self.plan.pieces))
            def _():
                each(g2, self.come2, got)
                total = self.s1[z_at]
                for k in range(1, g2):
                    total = total + self.r2[k]
                self.fin[z_at] = total

            each(g2, self.all2, go)

        def spread(self):
            each(g2, self.all2, got, z_at)

            @pl.when(self.mine)
            def _():
                across = self.plan.across
                rows = [
                    jnp.concatenate([self.fin[across * i + t] for t in range(across)], 1)
                    for i in range(2)
                ]
                shard = jnp.concatenate(rows, 0).astype(BF)
                self.sh[...] = shard
                self.gat[core, m1] = shard

            each(g1, self.all1, go)

        def collect(self):
            each(g1, self.all1, got, m1)
            self.last.start()

        def end(self):
            self.last.wait_recv()

        def drain(self):
            self.first.wait_send()
            each(g1, self.a2a1, sent)
            each(g2, self.a2a2, sent)

        def drain_late(self):
            each(g2, self.all2, sent)
            each(g1, self.all1, sent)

    ab = Chain(0, plan_ab, ab_src, ab_rc, ab_s0, ab_r1, ab_s1, ab_r2, ab_fin, ab_sh, gat_ab)
    dd = Chain(1, plan_d, d_src, d_rc, d_s0, d_r1, d_s1, d_r2, d_fin, d_sh, gat_d)

    down_term = dot(g_q[...], act[...], TN)
    up_term = dot(h2[...], dpre[...], TN)
    for i in range(2):
        cols = slice(i * HALF, (i + 1) * HALF)
        ab_src[i, 0:C, :] = down_term[:, cols]
        ab_src[i, C : 2 * C, :] = up_term[:, cols]
        if plan_ab.rows > 2 * C:
            ab_src[i, 2 * C :, :] = jnp.zeros((plan_ab.rows - 2 * C, HALF), F32)
    ab.begin()

    for w in range(1, 9):
        backward(w)
        if w == 4:
            ab.pair()

    dq_b = dq_all[...].astype(BF)
    d_term = jnp.concatenate(
        [
            dot(h1_q[...], dq_b, TN), dot(t_win[...], dk_all[...], TN),
            dot(t_win[...], dv_all[...], TN), dot(own_b[...], dmixb[...], TN),
        ],
        1,
    )
    weighted = jnp.sum(d_term[:, : 3 * C] * w_qkv[...].astype(F32), 1, keepdims=True)
    term_a = jnp.broadcast_to(weighted, (C, 128)).T[0:1] / gain_attn
    gains = jnp.concatenate([term_a, term_m], 1)
    first_row = lax.broadcasted_iota(jnp.int32, (16, HALF), 0) == 0
    for i in range(2):
        d_src[i, 0:C, :] = d_term[:, i * HALF : (i + 1) * HALF]
        if plan_d.rows > C + 16:
            d_src[i, C + 16 :, :] = jnp.zeros((plan_d.rows - C - 16, HALF), F32)
    d_src[0, C : C + 16, :] = jnp.where(first_row, jnp.broadcast_to(gains, (16, HALF)), 0.0)
    d_src[1, C : C + 16, :] = jnp.zeros((16, HALF), F32)
    dd.begin()

    dsource = dot(dk_all[...], wpad[:, 256 : 256 + C], NT) + dot(dv_all[...], wpad[:, 512 : 512 + C], NT)
    dq_source = dot(dq_b, wpad[:, 0:C], NT)
    back_f[...] = jnp.zeros_like(back_f)
    for w in range(9):
        dsq[pl.ds(QAT[w], NQ[w]), :] = (
            dsource[KAT[w] : KAT[w] + NQ[w]] + dq_source[QAT[w] : QAT[w + 1]]
        )
        to = KAT[w] + NQ[w]
        for start, size in PARTS[w]:
            back_f[pl.ds(start, size), :] = dsource[to : to + size]
            to += size
    back_src[...] = back_f[...].astype(BF)
    for copy in reversed(back):
        copy.start()

    dd.pair()
    loads[10].wait()
    loads[11].wait()
    output[...] = dot(to_nat[...], out_q[...]).astype(BF)
    stores[0].start()
    ab.plane()
    dd.plane()
    for copy in back:
        copy.wait_recv()
    dshift = (dsq[...] + dot(collect[...], back_dst[...])).astype(BF).astype(F32)
    gf = dmix[...] + norm_back(dshift, norm_q[...], inverse1, gain_attn)
    grad_field[...] = dot(to_nat[...], gf.astype(BF)).astype(BF)
    stores[1].start()
    ab.line()
    dd.line()
    ab.spread()
    dd.spread()
    for copy in there + back:
        copy.wait_send()
    ab.drain()
    dd.drain()
    ab.collect()
    stores[2].start()
    dd.collect()
    stores[3].start()
    ab.drain_late()
    dd.drain_late()
    ab.end()
    stores[4].start()
    dd.end()
    stores[5].start()
    ab.last.wait_send()
    dd.last.wait_send()
    for store in stores:
        store.wait()


def final(plans, out_n, gf_n, gat_ab_in, gat_d_in, *refs):
    outs = refs[:8]
    out_v8, gf_v, gat_ab, gat_d, qkv_v, out_v, up_v, down_v, ga_v, gm_v, in_sem, out_sem = refs[8:]
    loads = [
        pltpu.make_async_copy(src, dst, in_sem.at[i])
        for i, (src, dst) in enumerate(
            [(gat_d_in, gat_d), (gat_ab_in, gat_ab), (out_n, out_v8), (gf_n, gf_v)]
        )
    ]
    for load in loads:
        load.start()
    stores = [
        pltpu.make_async_copy(src, dst, out_sem.at[i])
        for i, (src, dst) in enumerate(
            zip((out_v8, gf_v, qkv_v, out_v, up_v, down_v, ga_v, gm_v), outs)
        )
    ]

    def whole(plan, gat):
        halves = [gat[i].astype(F32).reshape(plan.rows, HALF) for i in range(2)]
        return jnp.concatenate(halves, 1)

    loads[0].wait()
    d = whole(plans[1], gat_d)
    qkv_v[...] = d[:C, : 3 * C]
    out_v[...] = d[:C, 3 * C :]
    ga_v[...] = d[C : C + 1, :C]
    gm_v[...] = d[C : C + 1, C : 2 * C]
    for at in (2, 3, 6, 7):
        stores[at].start()
    for at in range(2):
        loads[2 + at].wait()
        stores[at].start()
    loads[1].wait()
    ab = whole(plans[0], gat_ab)
    down_v[...] = ab[:C]
    up_v[...] = ab[C : 2 * C]
    stores[4].start()
    stores[5].start()
    for store in stores:
        store.wait()


def body(nlon, nlat, field, region, w_qkv, w_out, w_up, w_down, gain_attn, gain_mlp, grad_next):
    sizes = (nlon // 8, 2, 4, nlat) if nlon >= 16 else (nlon // 2, 1, 2, nlat)
    nz, ny, nx, _ = sizes
    g1, g2 = ny * (nlat // 2) * nx, nz
    plans = (Plan(2 * C, g1, g2), Plan(C + 16, g1, g2))
    hbm = pl.BlockSpec(memory_space=pltpu.HBM)
    V = pltpu.VMEM
    consts = [jnp.asarray(a) for a in tables()]
    operands = [
        field.reshape(TOK, C), grad_next.reshape(TOK, C), region, w_qkv, w_out, w_up, w_down.T,
        gain_attn.reshape(1, C), gain_mlp.reshape(1, C), *consts,
    ]

    def pair(shape_of, kind):
        return [V(shape_of(p), kind) for p in plans]

    shapes = [jax.ShapeDtypeStruct((TOK, C), BF)] * 2 + [
        jax.ShapeDtypeStruct((2, p.own, p.r, HALF), BF) for p in plans
    ]
    scratch = (
        [V(a.shape, a.dtype) for a in shapes]
        + [(pltpu.SMEM if i == 2 else V)(a.shape, a.dtype) for i, a in enumerate(operands)]
        + [V((HALO, C), BF)] * 4 + [V((HALO, C), F32)]
        + [
            V((NQS, C), F32), V((NQS, C), BF), V((NQS, C), BF), V((NQS, C), F32),
            V((HALO, C), F32), V((NKS, C), F32), V((NKS, C), BF), V((C, FF), BF),
            V((NQS, 256), F32), V((NKS, 256), BF), V((NKS, C), BF), V((NKS, 256), F32),
            V((HEADS * NQS, 256), BF),
            V((144, HEADS * 144), F32), V((4, 144, HEADS * 72), F32), V((4, 160, HEADS * 40), F32),
            V((144, HEADS * 144), BF), V((72, HEADS * 72), BF), V((40, HEADS * 40), BF),
            V((NQS, C), F32), V((NQS, C), BF),
            V((NQS, C), BF), V((NQS, FF), BF), V((NQS, FF), BF), V((NQS, C), F32),
            V((NQS, C), BF), V((NQS, C), F32), V((NQS, C), F32),
            V((NKS, C), BF), V((NKS, C), BF), V((NQS, C), F32), V((NQS, C), BF),
        ]
        + pair(lambda p: (2, p.rows, HALF), F32)
        + pair(lambda p: (p.rows, HALF), F32)
        + pair(lambda p: (p.rows, HALF), BF)
        + pair(lambda p: (g1, p.r, HALF), BF)
        + pair(lambda p: (p.pieces, p.piece, p.lanes), F32)
        + pair(lambda p: (g2, p.piece, p.lanes), F32)
        + pair(lambda p: (p.pieces, p.piece, p.lanes), F32)
        + pair(lambda p: (p.r, HALF), BF)
        + [
            pltpu.SemaphoreType.DMA((13,)),
            pltpu.SemaphoreType.DMA((6,)),
            pltpu.SemaphoreType.DMA((2, 8)),
            pltpu.SemaphoreType.DMA((2, 8)),
            pltpu.SemaphoreType.DMA((2, 2)),
            pltpu.SemaphoreType.DMA((2, 2)),
            pltpu.SemaphoreType.DMA((2, 4, 16)),
            pltpu.SemaphoreType.DMA((2, 4, 16)),
        ]
    )
    mids = pl.pallas_call(
        functools.partial(kernel, sizes, plans),
        out_shape=shapes,
        in_specs=[hbm] * len(operands),
        out_specs=[hbm] * 4,
        scratch_shapes=scratch,
        compiler_params=pltpu.CompilerParams(
            collective_id=0, has_side_effects=True, vmem_limit_bytes=VLIM
        ),
        name="block",
    )(*operands)
    results = [
        jax.ShapeDtypeStruct((TOK, C), BF),
        jax.ShapeDtypeStruct((TOK, C), BF),
        jax.ShapeDtypeStruct((C, 3 * C), F32),
        jax.ShapeDtypeStruct((C, C), F32),
        jax.ShapeDtypeStruct((C, FF), F32),
        jax.ShapeDtypeStruct((C, FF), F32),
        jax.ShapeDtypeStruct((1, C), F32),
        jax.ShapeDtypeStruct((1, C), F32),
    ]
    outs = pl.pallas_call(
        functools.partial(final, plans),
        out_shape=results,
        in_specs=[hbm] * 4,
        out_specs=[hbm] * 8,
        scratch_shapes=[V(a.shape, a.dtype) for a in shapes + results[2:]]
        + [pltpu.SemaphoreType.DMA((4,)), pltpu.SemaphoreType.DMA((8,))],
        compiler_params=pltpu.CompilerParams(vmem_limit_bytes=VLIM),
        name="final",
    )(*mids)
    output, grad_field, grad_qkv, grad_out, grad_up, grad_down_t, grad_ga, grad_gm = outs
    return (
        output.reshape(field.shape), grad_field.reshape(field.shape),
        grad_qkv, grad_out, grad_up, grad_down_t.T, grad_ga.reshape(C), grad_gm.reshape(C),
    )


def solution(mesh):
    grid = P(None, "lat", "lon", None)
    return jax.shard_map(
        functools.partial(body, mesh.shape["lon"], mesh.shape["lat"]),
        mesh=mesh,
        in_specs=(grid, P(), P(), P(), P(), P(), P(), P(), grid),
        out_specs=(grid, grid, P(), P(), P(), P(), P(), P()),
        check_vma=False,
    )
```

```python
import functools

import jax
import jax.numpy as jnp
import ml_dtypes
import numpy as np
from jax import lax
from jax.experimental import pallas as pl
from jax.experimental.pallas import tpu as pltpu
from jax.sharding import PartitionSpec as P

C = 192
HEADS = 6
FF = 768
HALF = 384
ROWS = 12
COLS = 24
TOK = 2 * ROWS * COLS
SCALE = 32.0 ** -0.5
LOG2E = 1.4426950408889634
F32 = jnp.float32
BF = jnp.bfloat16
MESH = pl.DeviceIdType.MESH
VLIM = 54 << 20

NQ = (144,) + (72,) * 4 + (40,) * 4
NK = (144,) + (144,) * 4 + (160,) * 4
QAT = tuple(int(v) for v in np.cumsum((0,) + NQ))
KAT = tuple(int(v) for v in np.cumsum((0,) + NK))
NQS, NKS = QAT[-1], KAT[-1]
WAY = ((0, -1), (0, 1), (-1, 0), (1, 0), (-1, -1), (-1, 1), (1, -1), (1, 1))
MAT = (0, 160, 320, 480, 640, 688, 736, 784)
MROWS = (160,) * 4 + (48,) * 4
HALO = 832
PARTS = (
    (),
    ((0, 72),),
    ((160, 72),),
    ((320, 72),),
    ((480, 72),),
    ((112, 40), (320 + 112, 40), (640, 40)),
    ((160 + 112, 40), (320 + 72, 40), (688, 40)),
    ((72, 40), (480 + 112, 40), (736, 40)),
    ((160 + 72, 40), (480 + 72, 40), (784, 40)),
)
BANDS = 18


def tables():
    def piece(rows, cols, size=None):
        got = [(l * ROWS * COLS + r * COLS + c, r) for l in range(2) for r in rows for c in cols]
        return got + [(-1, None)] * ((size or len(got)) - len(got))

    top, mid, bot = range(0, 3), range(3, 9), range(9, 12)
    left, cen, rig = range(0, 6), range(6, 18), range(18, 24)
    own = [
        piece(mid, cen),
        piece(mid, rig), piece(mid, left), piece(bot, cen), piece(top, cen),
        piece(bot, rig, 40), piece(bot, left, 40), piece(top, rig, 40), piece(top, left, 40),
    ]
    sent = [
        piece(mid, side) + piece(top, side, 40) + piece(bot, side, 48) for side in (left, rig)
    ] + [
        piece(rows, cen) + piece(rows, left, 40) + piece(rows, rig, 48) for rows in (top, bot)
    ] + [
        piece(top, left, 48), piece(top, rig, 48), piece(bot, left, 48), piece(bot, rig, 48),
    ]
    shift = (0, 0, ROWS, -ROWS, ROWS, ROWS, -ROWS, -ROWS)
    flat_own = sum(own, [])
    flat_sent = sum(sent, [])
    moved = sum(
        [[(i, None if r is None else r + s) for i, r in part] for part, s in zip(sent, shift)], []
    )
    assert len(flat_own) == NQS and len(flat_sent) == HALO

    def hot(tokens):
        out = np.zeros((len(tokens), TOK), np.float32)
        for at, (index, _) in enumerate(tokens):
            if index >= 0:
                out[at, index] = 1
        return out

    keys = []
    for w in range(9):
        keys += own[w]
        for start, size in PARTS[w]:
            keys += moved[start : start + size]
    row_of = np.zeros((NKS, 32), np.float32)
    for at, (_, row) in enumerate(keys):
        row_of[at, BANDS if row is None else row + 3] = 1
    to_own, to_sent = hot(flat_own), hot(flat_sent)
    kind = ml_dtypes.bfloat16
    return [
        np.ascontiguousarray(a).astype(kind)
        for a in (np.concatenate([to_own, to_sent]), to_own.T, to_own @ to_sent.T, row_of)
    ]


def dot(a, b, dims=((1,), (0,))):
    return lax.dot_general(a, b, (dims, ((), ())), preferred_element_type=F32)


NT = ((1,), (1,))
TN = ((0,), (0,))


def norm(x):
    mean = jnp.mean(x, -1, keepdims=True)
    centred = x - mean
    inverse = lax.rsqrt(jnp.mean(centred * centred, -1, keepdims=True) + 1e-05)
    return centred * inverse, inverse


def norm_back(d, normed, inverse, gain):
    dn = d * gain
    return inverse * (
        dn - jnp.mean(dn, -1, keepdims=True) - normed * jnp.mean(dn * normed, -1, keepdims=True)
    )


class Plan:
    def __init__(self, rows, g1, g2):
        self.r = 16 * -(-rows // (16 * g1))
        self.own = -(-rows // self.r)
        self.rows = self.own * self.r
        self.piece = self.r // 2
        self.across = 3 if g2 >= 6 else 1
        self.pieces = 2 * self.across
        self.lanes = HALF // self.across


def kernel(
    sizes, plans,
    field_in, grad_in, region_in, wqkv_in, wout_in, wup_in, wdown_in, gaina_in, gainm_in,
    gather_in, to_nat_in, collect_in, row_of_in,
    output_hbm, grad_field_hbm, gat_ab_hbm, gat_d_hbm,
    output, grad_field, gat_ab, gat_d,
    field, grad, region, w_qkv, w_out, w_up, w_down, gain_a, gain_m, gather, to_nat, collect, row_of,
    msg, halo_x, back_src, back_dst, back_f,
    x_q, g_q, h1_q, norm_q, norm_h, t_norm, t_win, wpad, qf, kx, vx, closed,
    qm, p0, p1, p2, tile0, tile1, tile2, heads, own_b,
    h2, act, dpre, dmix, dmixb, downs, dq_all, dk_all, dv_all, dsq, out_q,
    ab_src, d_src, ab_rc, d_rc, ab_s0, d_s0, ab_r1, d_r1, ab_s1, d_s1, ab_r2, d_r2,
    ab_fin, d_fin, ab_sh, d_sh,
    in_sem, out_sem, halo_send, halo_recv, core_send, core_recv, red_send, red_recv,
):
    nz, ny, nx, nlat = sizes
    nlon = nz * ny * nx
    g1, g2 = ny * (nlat // 2) * nx, nz
    lon = lax.axis_index("lon")
    lat = lax.axis_index("lat")
    core = lax.rem(lat, 2)
    x_at, y_at, z_at = lax.rem(lon, nx), lax.rem(lax.div(lon, nx), ny), lax.div(lon, nx * ny)
    m1 = (y_at * (nlat // 2) + lax.div(lat, 2)) * nx + x_at
    plan_ab, plan_d = plans

    def wrap(i, n):
        return lax.rem(i + n, n)

    def at(dlat, dlon):
        return {"lon": wrap(lon + dlon, nlon), "lat": wrap(lat + dlat, nlat)}

    def peer1(m):
        y = lax.div(m, nx)
        return {
            "lon": (z_at * ny + lax.div(y, nlat // 2)) * nx + lax.rem(m, nx),
            "lat": lax.rem(y, nlat // 2) * 2 + core,
        }

    def peer2(v):
        return {"lon": v * (nx * ny) + lax.rem(lon, nx * ny), "lat": lat}

    sibling = {"lon": lon, "lat": lat + 1 - 2 * core}

    loads = [
        pltpu.make_async_copy(src, dst, in_sem.at[i])
        for i, (src, dst) in enumerate(
            [
                (field_in, field), (gather_in, gather), (row_of_in, row_of), (gaina_in, gain_a),
                (wqkv_in, w_qkv), (grad_in, grad), (wout_in, w_out), (gainm_in, gain_m),
                (wup_in, w_up), (wdown_in, w_down), (to_nat_in, to_nat), (collect_in, collect),
                (region_in, region),
            ]
        )
    ]
    loads[0].start()
    loads[1].start()
    loads[12].start()
    stores = [
        pltpu.make_async_copy(src, dst, out_sem.at[i])
        for i, (src, dst) in enumerate(
            [
                (output, output_hbm), (grad_field, grad_field_hbm),
                (gat_ab.at[core], gat_ab_hbm.at[core]), (gat_d.at[core], gat_d_hbm.at[core]),
                (gat_ab.at[1 - core], gat_ab_hbm.at[1 - core]),
                (gat_d.at[1 - core], gat_d_hbm.at[1 - core]),
            ]
        )
    ]

    barrier = pltpu.get_barrier_semaphore()

    def greet(device):
        pl.semaphore_signal(barrier, inc=1, device_id=device, device_id_type=MESH)

    def others(n, fn):
        def step(j, _):
            half = lax.div(j, 2)
            fn(n // 2 + jnp.where(lax.rem(j, 2) == 1, half, -half))
            return 0

        lax.fori_loop(1, n, step, 0)

    for way in reversed(WAY):
        greet(at(*way))
    others(g2, lambda k: greet(peer2(wrap(z_at + k, g2))))
    others(g1, lambda k: greet(peer1(wrap(m1 + k, g1))))
    greet(sibling)
    for load in loads[2:12]:
        load.start()

    def halo(which, src, dst, sign):
        return [
            pltpu.make_async_remote_copy(
                src_ref=src.at[pl.ds(MAT[i], MROWS[i])],
                dst_ref=dst.at[pl.ds(MAT[i], MROWS[i])],
                send_sem=halo_send.at[which, i],
                recv_sem=halo_recv.at[which, i],
                device_id=at(sign * WAY[i][0], sign * WAY[i][1]),
                device_id_type=MESH,
            )
            for i in range(8)
        ]

    there = halo(0, msg, halo_x, 1)
    back = halo(1, back_src, back_dst, -1)

    lane = lax.broadcasted_iota(jnp.int32, (1, 256), 1)
    for n, tile in ((144, tile0), (72, tile1), (40, tile2)):
        rows = lax.broadcasted_iota(jnp.int32, (n, HEADS * n), 0)
        cols = lax.broadcasted_iota(jnp.int32, (n, HEADS * n), 1)
        hit = jnp.zeros((n, HEADS * n), F32)
        for h in range(HEADS):
            hit = jnp.where(cols == rows + n * h, 1.0, hit)
        tile[...] = hit.astype(BF)
    eye = (
        lax.broadcasted_iota(jnp.int32, (C, C), 0) == lax.broadcasted_iota(jnp.int32, (C, C), 1)
    ).astype(F32).astype(BF)

    loads[0].wait()
    loads[1].wait()
    moved = dot(gather[...], field[...])
    x_q[...] = moved[:NQS]
    msg[...] = moved[NQS:].astype(BF)
    pl.semaphore_wait(barrier, 9 + (g1 - 1) + (g2 - 1))
    for copy in reversed(there):
        copy.start()

    loads[2].wait()
    loads[12].wait()
    slot = lax.broadcasted_iota(jnp.int32, (32, 256), 0)
    value = jnp.where(slot == BANDS, 3, -1)
    for j in range(BANDS):
        band = region[wrap(lat * ROWS + j - 3, nlat * ROWS)]
        value = jnp.where(slot == j, band, value)
    column = lax.broadcasted_iota(jnp.int32, (32, 256), 1) - C
    band_hot = jnp.where((column >= 0) & (value == column), 1.0, 0.0).astype(BF)
    member = dot(row_of[...], band_hot)
    closed[...] = jnp.where((lane >= C) & (lane < C + 4), (member - 1.0) * 1e30, 0.0)

    for load in loads[3:5]:
        load.wait()
    wpad[...] = jnp.zeros_like(wpad)
    for i in range(3):
        wpad[:, 256 * i : 256 * i + C] = w_qkv[:, C * i : C * i + C]
    gain_attn = gain_a[...]

    normed, inverse1 = norm(x_q[...])
    norm_q[...] = normed
    h1_q[...] = (normed * gain_attn).astype(BF)
    qf[...] = dot(h1_q[...], wpad[:, 0:256]).astype(BF).astype(F32)

    def keys_of(first, last):
        rows = pl.ds(KAT[first], KAT[last] - KAT[first])
        t_win[rows, :] = (t_norm[rows, :] * gain_attn).astype(BF)
        both = dot(t_win[rows, :], wpad[:, 256:768])
        kx[rows, :] = (both[:, 0:256] + member[KAT[first] : KAT[last]]).astype(BF)
        vx[rows, :] = both[:, 256 : 256 + C].astype(BF)

    def kept(w):
        if w == 0:
            return p0, tile0
        return (p1.at[w - 1], tile1) if w < 5 else (p2.at[w - 5], tile2)

    def gather_heads(full, tile):
        n = full.shape[1] // HEADS
        at_lane = lax.broadcasted_iota(jnp.int32, (1, HEADS * n), 1)
        parts = [
            jnp.where(
                (at_lane >= n * h) & (at_lane < n * h + n), full[32 * h : 32 * h + 32], 0.0
            )
            for h in range(HEADS)
        ]
        return dot(tile[...], jnp.concatenate(parts, 0).astype(BF), NT)

    def by_head(inside, outside, width):
        at_lane = lane[:, :width]
        return jnp.concatenate(
            [
                jnp.where((at_lane >= 32 * h) & (at_lane < 32 * h + 32), inside, outside)
                for h in range(HEADS)
            ],
            0,
        ).astype(BF)

    def rows_of(w):
        return pl.ds(QAT[w], NQ[w]), pl.ds(KAT[w], NK[w]), pl.ds(HEADS * QAT[w], HEADS * NQ[w])

    def forward(w):
        q_rows, k_rows, m_rows = rows_of(w)
        keep, tile = kept(w)
        qm[m_rows, :] = by_head(qf[q_rows, :], closed[pl.ds(KAT[w], NQ[w]), :], 256)
        scores = dot(kx[k_rows, :], qm[m_rows, :], NT) * (SCALE * LOG2E)
        top = jnp.max(scores, 0, keepdims=True)
        expo = jnp.exp2(scores - top)
        prob = expo * (1.0 / jnp.sum(expo, 0, keepdims=True))
        keep[...] = prob
        value_t = dot(eye, vx[k_rows, :], NT).astype(BF)
        heads[q_rows, :] = gather_heads(dot(value_t, prob.astype(BF)), tile)

    def backward(w):
        q_rows, k_rows, m_rows = rows_of(w)
        keep, tile = kept(w)
        do = by_head(downs[q_rows, :], 0.0, C)
        prob = keep[...]
        dprob = dot(vx[k_rows, :], do, NT)
        dscore = (prob * (dprob - jnp.sum(dprob * prob, 0, keepdims=True))).astype(BF)
        dv_all[k_rows, :] = dot(prob.astype(BF), do).astype(BF)
        dk_all[k_rows, :] = (dot(dscore, qm[m_rows, 0:C]) * SCALE).astype(BF)
        key_t = dot(eye, kx[k_rows, 0:C], NT).astype(BF)
        dq_all[q_rows, :] = gather_heads(dot(key_t, dscore) * SCALE, tile)

    def mlp(rows):
        x = x_q[rows, :]
        g = g_q[rows, :]
        owned = heads[rows, :].astype(BF)
        own_b[rows, :] = owned
        mixed = x + dot(owned, w_out[...])
        normed2, inverse2 = norm(mixed)
        gain_mlp = gain_m[...]
        h2b = (normed2 * gain_mlp).astype(BF)
        h2[rows, :] = h2b
        pre = dot(h2b, w_up[...])
        square = pre * pre
        tangent = jnp.tanh(0.7978845608 * pre * (1.0 + 0.044715 * square))
        half = 0.5 * (1.0 + tangent)
        actb = (pre * half).astype(BF)
        act[rows, :] = actb
        slope = half + 0.5 * pre * (1.0 - tangent * tangent) * 0.7978845608 * (
            1.0 + 3.0 * 0.044715 * square
        )
        out_q[rows, :] = (mixed + dot(actb, w_down[...], NT)).astype(BF)
        dpreb = (dot(g, w_down[...]) * slope).astype(BF)
        dpre[rows, :] = dpreb
        dh2 = dot(dpreb, w_up[...], NT)
        dm = g.astype(F32) + norm_back(dh2, normed2, inverse2, gain_mlp)
        dmix[rows, :] = dm
        dmb = dm.astype(BF)
        dmixb[rows, :] = dmb
        downs[rows, :] = dot(dmb, w_out[...], NT).astype(BF).astype(F32)
        return jnp.sum(dh2 * normed2, 0, keepdims=True)

    t_norm[0:144, :] = normed[0:144]
    keys_of(0, 1)
    forward(0)
    for load in loads[5:10]:
        load.wait()
    g_q[...] = dot(gather[0:NQS, :], grad[...]).astype(BF)
    term_m = mlp(pl.ds(0, 144))
    backward(0)

    for copy in there:
        copy.wait_recv()
    norm_h[...] = norm(halo_x[...].astype(F32))[0]
    for w in range(1, 9):
        t_norm[pl.ds(KAT[w], NQ[w]), :] = norm_q[pl.ds(QAT[w], NQ[w]), :]
        to = KAT[w] + NQ[w]
        for start, size in PARTS[w]:
            t_norm[pl.ds(to, size), :] = norm_h[pl.ds(start, size), :]
            to += size
    keys_of(1, 9)
    for w in range(1, 9):
        forward(w)
    term_m = term_m + mlp(pl.ds(144, NQS - 144))

    def core_copy(which, stage, src, dst):
        return pltpu.make_async_remote_copy(
            src_ref=src, dst_ref=dst,
            send_sem=core_send.at[which, stage], recv_sem=core_recv.at[which, stage],
            device_id=sibling, device_id_type=MESH,
        )

    def remote(which, stage, k, src, dst, device):
        return pltpu.make_async_remote_copy(
            src_ref=src, dst_ref=dst,
            send_sem=red_send.at[which, stage, k], recv_sem=red_recv.at[which, stage, k],
            device_id=device, device_id_type=MESH,
        )

    def each(n, one, fn, back=None):
        others(n, lambda k: one(k, fn) if back is None else one(k, fn, wrap(back - k, n)))

    def go(copy):
        copy.start()

    def got(copy):
        copy.wait_recv()

    def sent(copy):
        copy.wait_send()

    def split_row(block):
        total = block[0:1] + block[1:2]
        high = total.astype(BF).astype(F32)
        at_row = lax.broadcasted_iota(jnp.int32, block.shape, 0)
        rest = jnp.where(at_row == 1, jnp.broadcast_to(total - high, block.shape), 0.0)
        return jnp.where(at_row == 0, jnp.broadcast_to(high, block.shape), rest).astype(BF)

    class Chain:
        def __init__(self, which, plan, src, rc, s0, r1, s1, r2, fin, sh, gat):
            self.which, self.plan = which, plan
            self.src, self.rc, self.s0, self.r1 = src, rc, s0, r1
            self.s1, self.r2, self.fin, self.sh, self.gat = s1, r2, fin, sh, gat
            self.mine = m1 < plan.own
            self.first = core_copy(which, 0, src.at[1 - core], rc)
            self.last = core_copy(which, 1, gat.at[core], gat.at[core])

        def a2a1(self, k, fn):
            target = wrap(m1 + k, g1)
            start = pl.multiple_of(target * self.plan.r, 16)
            copy = remote(
                self.which, 0, k, self.s0.at[pl.ds(start, self.plan.r)], self.r1.at[k],
                peer1(target),
            )
            pl.when(target < self.plan.own)(functools.partial(fn, copy))

        def come1(self, k, fn):
            fn(remote(self.which, 0, k, self.r1.at[k], self.r1.at[k], peer1(wrap(m1 + k, g1))))

        def a2a2(self, k, fn):
            target = wrap(z_at + k, g2)
            copy = remote(self.which, 1, k, self.s1.at[target], self.r2.at[k], peer2(target))
            pl.when(self.mine & (target < self.plan.pieces))(functools.partial(fn, copy))

        def come2(self, k, fn):
            fn(remote(self.which, 1, k, self.r2.at[k], self.r2.at[k], peer2(wrap(z_at + k, g2))))

        def all2(self, k, fn, source=None):
            source = z_at if source is None else source
            copy = remote(
                self.which, 2, k, self.fin.at[source], self.fin.at[source],
                peer2(wrap(z_at + k, g2)),
            )
            pl.when(self.mine & (source < self.plan.pieces))(functools.partial(fn, copy))

        def all1(self, k, fn, source=None):
            source = m1 if source is None else source
            copy = remote(
                self.which, 3, k, self.sh, self.gat.at[core, source], peer1(wrap(m1 + k, g1))
            )
            pl.when(source < self.plan.own)(functools.partial(fn, copy))

        def begin(self):
            self.first.start()

        def pair(self):
            self.first.wait_recv()
            total = self.src[core] + self.rc[...]
            self.s0[...] = total.astype(BF)
            if self.which == 1:
                self.s0[C : C + 16, :] = split_row(total[C : C + 16])
            each(g1, self.a2a1, go)

        def plane(self):
            plan = self.plan

            @pl.when(self.mine)
            def _():
                each(g1, self.come1, got)
                start = pl.multiple_of(m1 * plan.r, 16)
                total = self.s0[pl.ds(start, plan.r), :].astype(F32)
                for k in range(1, g1):
                    total = total + self.r1[k].astype(F32)
                for j in range(plan.pieces):
                    i, t = j // plan.across, j % plan.across
                    self.s1[j] = total[
                        i * plan.piece : (i + 1) * plan.piece, t * plan.lanes : (t + 1) * plan.lanes
                    ]

            each(g2, self.a2a2, go)

        def line(self):
            @pl.when(self.mine & (z_at < self.plan.pieces))
            def _():
                each(g2, self.come2, got)
                total = self.s1[z_at]
                for k in range(1, g2):
                    total = total + self.r2[k]
                self.fin[z_at] = total

            each(g2, self.all2, go)

        def spread(self):
            each(g2, self.all2, got, z_at)

            @pl.when(self.mine)
            def _():
                across = self.plan.across
                rows = [
                    jnp.concatenate([self.fin[across * i + t] for t in range(across)], 1)
                    for i in range(2)
                ]
                whole = jnp.concatenate(rows, 0)
                shard = whole.astype(BF)
                if self.which == 1:
                    first = jnp.where(m1 == C // self.plan.r, split_row(whole[:16]), shard[:16])
                    shard = first if self.plan.r == 16 else jnp.concatenate([first, shard[16:]], 0)
                self.sh[...] = shard
                self.gat[core, m1] = shard

            each(g1, self.all1, go)

        def collect(self):
            each(g1, self.all1, got, m1)
            self.last.start()

        def end(self):
            self.last.wait_recv()

        def drain(self):
            self.first.wait_send()
            each(g1, self.a2a1, sent)
            each(g2, self.a2a2, sent)

        def drain_late(self):
            each(g2, self.all2, sent)
            each(g1, self.all1, sent)

    ab = Chain(0, plan_ab, ab_src, ab_rc, ab_s0, ab_r1, ab_s1, ab_r2, ab_fin, ab_sh, gat_ab)
    dd = Chain(1, plan_d, d_src, d_rc, d_s0, d_r1, d_s1, d_r2, d_fin, d_sh, gat_d)

    down_term = dot(g_q[...], act[...], TN)
    up_term = dot(h2[...], dpre[...], TN)
    for i in range(2):
        cols = slice(i * HALF, (i + 1) * HALF)
        ab_src[i, 0:C, :] = down_term[:, cols]
        ab_src[i, C : 2 * C, :] = up_term[:, cols]
        if plan_ab.rows > 2 * C:
            ab_src[i, 2 * C :, :] = jnp.zeros((plan_ab.rows - 2 * C, HALF), F32)
    ab.begin()

    for w in range(1, 9):
        backward(w)
        if w == 4:
            ab.pair()

    dsource = dot(dk_all[...], wpad[:, 256 : 256 + C], NT) + dot(dv_all[...], wpad[:, 512 : 512 + C], NT)
    dq_b = dq_all[...].astype(BF)
    dq_source = dot(dq_b, wpad[:, 0:C], NT)
    back_f[...] = jnp.zeros_like(back_f)
    for w in range(9):
        dsq[pl.ds(QAT[w], NQ[w]), :] = (
            dsource[KAT[w] : KAT[w] + NQ[w]] + dq_source[QAT[w] : QAT[w + 1]]
        )
        to = KAT[w] + NQ[w]
        for start, size in PARTS[w]:
            back_f[pl.ds(start, size), :] = dsource[to : to + size]
            to += size
    back_src[...] = back_f[...].astype(BF)
    for copy in reversed(back):
        copy.start()

    term_a = jnp.sum(dsource * t_norm[...], 0, keepdims=True) + jnp.sum(
        dq_source * norm_q[...], 0, keepdims=True
    )
    d_term = jnp.concatenate(
        [
            dot(h1_q[...], dq_b, TN), dot(t_win[...], dk_all[...], TN),
            dot(t_win[...], dv_all[...], TN), dot(own_b[...], dmixb[...], TN),
        ],
        1,
    )
    gains = jnp.concatenate([term_a, term_m], 1)
    first_row = lax.broadcasted_iota(jnp.int32, (16, HALF), 0) == 0
    for i in range(2):
        d_src[i, 0:C, :] = d_term[:, i * HALF : (i + 1) * HALF]
        if plan_d.rows > C + 16:
            d_src[i, C + 16 :, :] = jnp.zeros((plan_d.rows - C - 16, HALF), F32)
    d_src[0, C : C + 16, :] = jnp.where(first_row, jnp.broadcast_to(gains, (16, HALF)), 0.0)
    d_src[1, C : C + 16, :] = jnp.zeros((16, HALF), F32)
    dd.begin()

    dd.pair()
    loads[10].wait()
    loads[11].wait()
    output[...] = dot(to_nat[...], out_q[...]).astype(BF)
    stores[0].start()
    ab.plane()
    dd.plane()
    for copy in back:
        copy.wait_recv()
    dshift = (dsq[...] + dot(collect[...], back_dst[...])).astype(BF).astype(F32)
    gf = dmix[...] + norm_back(dshift, norm_q[...], inverse1, gain_attn)
    grad_field[...] = dot(to_nat[...], gf.astype(BF)).astype(BF)
    stores[1].start()
    ab.line()
    dd.line()
    ab.spread()
    dd.spread()
    for copy in there + back:
        copy.wait_send()
    ab.drain()
    dd.drain()
    ab.collect()
    stores[2].start()
    dd.collect()
    stores[3].start()
    ab.drain_late()
    dd.drain_late()
    ab.end()
    stores[4].start()
    dd.end()
    stores[5].start()
    ab.last.wait_send()
    dd.last.wait_send()
    for store in stores:
        store.wait()


def final(plans, out_n, gf_n, gat_ab_in, gat_d_in, *refs):
    outs = refs[:8]
    out_v8, gf_v, gat_ab, gat_d, qkv_v, out_v, up_v, down_v, ga_v, gm_v, in_sem, out_sem = refs[8:]
    loads = [
        pltpu.make_async_copy(src, dst, in_sem.at[i])
        for i, (src, dst) in enumerate(
            [(gat_d_in, gat_d), (gat_ab_in, gat_ab), (out_n, out_v8), (gf_n, gf_v)]
        )
    ]
    for load in loads:
        load.start()
    stores = [
        pltpu.make_async_copy(src, dst, out_sem.at[i])
        for i, (src, dst) in enumerate(
            zip((out_v8, gf_v, qkv_v, out_v, up_v, down_v, ga_v, gm_v), outs)
        )
    ]

    def whole(plan, gat):
        halves = [gat[i].astype(F32).reshape(plan.rows, HALF) for i in range(2)]
        return jnp.concatenate(halves, 1)

    loads[0].wait()
    d = whole(plans[1], gat_d)
    qkv_v[...] = d[:C, : 3 * C]
    out_v[...] = d[:C, 3 * C :]
    gains = d[C : C + 1] + d[C + 1 : C + 2]
    ga_v[...] = gains[:, :C]
    gm_v[...] = gains[:, C : 2 * C]
    for at in (2, 3, 6, 7):
        stores[at].start()
    for at in range(2):
        loads[2 + at].wait()
        stores[at].start()
    loads[1].wait()
    ab = whole(plans[0], gat_ab)
    down_v[...] = ab[:C]
    up_v[...] = ab[C : 2 * C]
    stores[4].start()
    stores[5].start()
    for store in stores:
        store.wait()


def body(nlon, nlat, field, region, w_qkv, w_out, w_up, w_down, gain_attn, gain_mlp, grad_next):
    sizes = (nlon // 8, 2, 4, nlat) if nlon >= 16 else (nlon // 2, 1, 2, nlat)
    nz, ny, nx, _ = sizes
    g1, g2 = ny * (nlat // 2) * nx, nz
    plans = (Plan(2 * C, g1, g2), Plan(C + 16, g1, g2))
    hbm = pl.BlockSpec(memory_space=pltpu.HBM)
    V = pltpu.VMEM
    consts = [jnp.asarray(a) for a in tables()]
    operands = [
        field.reshape(TOK, C), grad_next.reshape(TOK, C), region, w_qkv, w_out, w_up, w_down.T,
        gain_attn.reshape(1, C), gain_mlp.reshape(1, C), *consts,
    ]

    def pair(shape_of, kind):
        return [V(shape_of(p), kind) for p in plans]

    shapes = [jax.ShapeDtypeStruct((TOK, C), BF)] * 2 + [
        jax.ShapeDtypeStruct((2, p.own, p.r, HALF), BF) for p in plans
    ]
    scratch = (
        [V(a.shape, a.dtype) for a in shapes]
        + [(pltpu.SMEM if i == 2 else V)(a.shape, a.dtype) for i, a in enumerate(operands)]
        + [V((HALO, C), BF)] * 4 + [V((HALO, C), F32)]
        + [
            V((NQS, C), F32), V((NQS, C), BF), V((NQS, C), BF), V((NQS, C), F32),
            V((HALO, C), F32), V((NKS, C), F32), V((NKS, C), BF), V((C, FF), BF),
            V((NQS, 256), F32), V((NKS, 256), BF), V((NKS, C), BF), V((NKS, 256), F32),
            V((HEADS * NQS, 256), BF),
            V((144, HEADS * 144), F32), V((4, 144, HEADS * 72), F32), V((4, 160, HEADS * 40), F32),
            V((144, HEADS * 144), BF), V((72, HEADS * 72), BF), V((40, HEADS * 40), BF),
            V((NQS, C), F32), V((NQS, C), BF),
            V((NQS, C), BF), V((NQS, FF), BF), V((NQS, FF), BF), V((NQS, C), F32),
            V((NQS, C), BF), V((NQS, C), F32), V((NQS, C), F32),
            V((NKS, C), BF), V((NKS, C), BF), V((NQS, C), F32), V((NQS, C), BF),
        ]
        + pair(lambda p: (2, p.rows, HALF), F32)
        + pair(lambda p: (p.rows, HALF), F32)
        + pair(lambda p: (p.rows, HALF), BF)
        + pair(lambda p: (g1, p.r, HALF), BF)
        + pair(lambda p: (p.pieces, p.piece, p.lanes), F32)
        + pair(lambda p: (g2, p.piece, p.lanes), F32)
        + pair(lambda p: (p.pieces, p.piece, p.lanes), F32)
        + pair(lambda p: (p.r, HALF), BF)
        + [
            pltpu.SemaphoreType.DMA((13,)),
            pltpu.SemaphoreType.DMA((6,)),
            pltpu.SemaphoreType.DMA((2, 8)),
            pltpu.SemaphoreType.DMA((2, 8)),
            pltpu.SemaphoreType.DMA((2, 2)),
            pltpu.SemaphoreType.DMA((2, 2)),
            pltpu.SemaphoreType.DMA((2, 4, 16)),
            pltpu.SemaphoreType.DMA((2, 4, 16)),
        ]
    )
    mids = pl.pallas_call(
        functools.partial(kernel, sizes, plans),
        out_shape=shapes,
        in_specs=[hbm] * len(operands),
        out_specs=[hbm] * 4,
        scratch_shapes=scratch,
        compiler_params=pltpu.CompilerParams(
            collective_id=0, has_side_effects=True, vmem_limit_bytes=VLIM
        ),
        name="block",
    )(*operands)
    results = [
        jax.ShapeDtypeStruct((TOK, C), BF),
        jax.ShapeDtypeStruct((TOK, C), BF),
        jax.ShapeDtypeStruct((C, 3 * C), F32),
        jax.ShapeDtypeStruct((C, C), F32),
        jax.ShapeDtypeStruct((C, FF), F32),
        jax.ShapeDtypeStruct((C, FF), F32),
        jax.ShapeDtypeStruct((1, C), F32),
        jax.ShapeDtypeStruct((1, C), F32),
    ]
    outs = pl.pallas_call(
        functools.partial(final, plans),
        out_shape=results,
        in_specs=[hbm] * 4,
        out_specs=[hbm] * 8,
        scratch_shapes=[V(a.shape, a.dtype) for a in shapes + results[2:]]
        + [pltpu.SemaphoreType.DMA((4,)), pltpu.SemaphoreType.DMA((8,))],
        compiler_params=pltpu.CompilerParams(vmem_limit_bytes=VLIM),
        name="final",
    )(*mids)
    output, grad_field, grad_qkv, grad_out, grad_up, grad_down_t, grad_ga, grad_gm = outs
    return (
        output.reshape(field.shape), grad_field.reshape(field.shape),
        grad_qkv, grad_out, grad_up, grad_down_t.T, grad_ga.reshape(C), grad_gm.reshape(C),
    )


def solution(mesh):
    grid = P(None, "lat", "lon", None)
    return jax.shard_map(
        functools.partial(body, mesh.shape["lon"], mesh.shape["lat"]),
        mesh=mesh,
        in_specs=(grid, P(), P(), P(), P(), P(), P(), P(), grid),
        out_specs=(grid, grid, P(), P(), P(), P(), P(), P()),
        check_vma=False,
    )
```

```python
import functools

import jax
import jax.numpy as jnp
import ml_dtypes
import numpy as np
from jax import lax
from jax.experimental import pallas as pl
from jax.experimental.pallas import tpu as pltpu
from jax.sharding import PartitionSpec as P

C = 192
HEADS = 6
FF = 768
HALF = 384
ROWS = 12
COLS = 24
TOK = 2 * ROWS * COLS
SCALE = 32.0 ** -0.5
LOG2E = 1.4426950408889634
F32 = jnp.float32
BF = jnp.bfloat16
MESH = pl.DeviceIdType.MESH
VLIM = 54 << 20

NQ = (144,) + (72,) * 4 + (40,) * 4
NK = (144,) + (144,) * 4 + (160,) * 4
QAT = tuple(int(v) for v in np.cumsum((0,) + NQ))
KAT = tuple(int(v) for v in np.cumsum((0,) + NK))
NQS, NKS = QAT[-1], KAT[-1]
WAY = ((0, -1), (0, 1), (-1, 0), (1, 0), (-1, -1), (-1, 1), (1, -1), (1, 1))
MAT = (0, 160, 320, 480, 640, 688, 736, 784)
MROWS = (160,) * 4 + (48,) * 4
HALO = 832
PARTS = (
    (),
    ((0, 72),),
    ((160, 72),),
    ((320, 72),),
    ((480, 72),),
    ((112, 40), (320 + 112, 40), (640, 40)),
    ((160 + 112, 40), (320 + 72, 40), (688, 40)),
    ((72, 40), (480 + 112, 40), (736, 40)),
    ((160 + 72, 40), (480 + 72, 40), (784, 40)),
)
BANDS = 18
FOLD = C // 4
GAINS = 3 * FOLD


def tables():
    def piece(rows, cols, size=None):
        got = [(l * ROWS * COLS + r * COLS + c, r) for l in range(2) for r in rows for c in cols]
        return got + [(-1, None)] * ((size or len(got)) - len(got))

    top, mid, bot = range(0, 3), range(3, 9), range(9, 12)
    left, cen, rig = range(0, 6), range(6, 18), range(18, 24)
    own = [
        piece(mid, cen),
        piece(mid, rig), piece(mid, left), piece(bot, cen), piece(top, cen),
        piece(bot, rig, 40), piece(bot, left, 40), piece(top, rig, 40), piece(top, left, 40),
    ]
    sent = [
        piece(mid, side) + piece(top, side, 40) + piece(bot, side, 48) for side in (left, rig)
    ] + [
        piece(rows, cen) + piece(rows, left, 40) + piece(rows, rig, 48) for rows in (top, bot)
    ] + [
        piece(top, left, 48), piece(top, rig, 48), piece(bot, left, 48), piece(bot, rig, 48),
    ]
    shift = (0, 0, ROWS, -ROWS, ROWS, ROWS, -ROWS, -ROWS)
    flat_own = sum(own, [])
    flat_sent = sum(sent, [])
    moved = sum(
        [[(i, None if r is None else r + s) for i, r in part] for part, s in zip(sent, shift)], []
    )
    assert len(flat_own) == NQS and len(flat_sent) == HALO

    def hot(tokens):
        out = np.zeros((len(tokens), TOK), np.float32)
        for at, (index, _) in enumerate(tokens):
            if index >= 0:
                out[at, index] = 1
        return out

    keys = []
    for w in range(9):
        keys += own[w]
        for start, size in PARTS[w]:
            keys += moved[start : start + size]
    row_of = np.zeros((NKS, 32), np.float32)
    for at, (_, row) in enumerate(keys):
        row_of[at, BANDS if row is None else row + 3] = 1
    to_own, to_sent = hot(flat_own), hot(flat_sent)
    kind = ml_dtypes.bfloat16
    return [
        np.ascontiguousarray(a).astype(kind)
        for a in (np.concatenate([to_own, to_sent]), to_own.T, to_own @ to_sent.T, row_of)
    ]


def dot(a, b, dims=((1,), (0,))):
    return lax.dot_general(a, b, (dims, ((), ())), preferred_element_type=F32)


NT = ((1,), (1,))
TN = ((0,), (0,))


def fold(square):
    return jnp.concatenate([square[FOLD * j : FOLD * (j + 1)] for j in range(4)], 1)


def unfold(wide):
    return jnp.concatenate([wide[:, C * j : C * (j + 1)] for j in range(4)], 0)


def norm(x):
    mean = jnp.mean(x, -1, keepdims=True)
    centred = x - mean
    inverse = lax.rsqrt(jnp.mean(centred * centred, -1, keepdims=True) + 1e-05)
    return centred * inverse, inverse


def norm_back(d, normed, inverse, gain):
    dn = d * gain
    return inverse * (
        dn - jnp.mean(dn, -1, keepdims=True) - normed * jnp.mean(dn * normed, -1, keepdims=True)
    )


class Plan:
    def __init__(self, rows, g1, g2):
        self.r = 16 * -(-rows // (16 * g1))
        self.own = -(-rows // self.r)
        self.rows = self.own * self.r
        self.piece = self.r // 2
        self.across = 3 if g2 >= 6 else 1
        self.pieces = 2 * self.across
        self.lanes = HALF // self.across


def kernel(
    sizes, plans,
    field_in, grad_in, region_in, wqkv_in, wout_in, wup_in, wdown_in, gaina_in, gainm_in,
    gather_in, to_nat_in, collect_in, row_of_in,
    output_hbm, grad_field_hbm, gat_ab_hbm, gat_d_hbm,
    output, grad_field, gat_ab, gat_d,
    field, grad, region, w_qkv, w_out, w_up, w_down, gain_a, gain_m, gather, to_nat, collect, row_of,
    msg, halo_x, back_src, back_dst, back_f,
    x_q, g_q, h1_q, norm_q, norm_h, t_norm, t_win, wpad, qf, kx, vx, closed,
    qm, p0, p1, p2, tile0, tile1, tile2, heads, own_b,
    h2, act, dpre, dmix, dmixb, downs, dq_all, dk_all, dv_all, dsq, out_q,
    ab_src, d_src, ab_rc, d_rc, ab_s0, d_s0, ab_r1, d_r1, ab_s1, d_s1, ab_r2, d_r2,
    ab_fin, d_fin, ab_sh, d_sh,
    in_sem, out_sem, halo_send, halo_recv, core_send, core_recv, red_send, red_recv,
):
    nz, ny, nx, nlat = sizes
    nlon = nz * ny * nx
    g1, g2 = ny * (nlat // 2) * nx, nz
    lon = lax.axis_index("lon")
    lat = lax.axis_index("lat")
    core = lax.rem(lat, 2)
    x_at, y_at, z_at = lax.rem(lon, nx), lax.rem(lax.div(lon, nx), ny), lax.div(lon, nx * ny)
    m1 = (y_at * (nlat // 2) + lax.div(lat, 2)) * nx + x_at
    plan_ab, plan_d = plans

    def wrap(i, n):
        return lax.rem(i + n, n)

    def at(dlat, dlon):
        return {"lon": wrap(lon + dlon, nlon), "lat": wrap(lat + dlat, nlat)}

    def peer1(m):
        y = lax.div(m, nx)
        return {
            "lon": (z_at * ny + lax.div(y, nlat // 2)) * nx + lax.rem(m, nx),
            "lat": lax.rem(y, nlat // 2) * 2 + core,
        }

    def peer2(v):
        return {"lon": v * (nx * ny) + lax.rem(lon, nx * ny), "lat": lat}

    sibling = {"lon": lon, "lat": lat + 1 - 2 * core}

    loads = [
        pltpu.make_async_copy(src, dst, in_sem.at[i])
        for i, (src, dst) in enumerate(
            [
                (field_in, field), (gather_in, gather), (row_of_in, row_of), (gaina_in, gain_a),
                (wqkv_in, w_qkv), (grad_in, grad), (wout_in, w_out), (gainm_in, gain_m),
                (wup_in, w_up), (wdown_in, w_down), (to_nat_in, to_nat), (collect_in, collect),
                (region_in, region),
            ]
        )
    ]
    loads[0].start()
    loads[1].start()
    loads[12].start()
    stores = [
        pltpu.make_async_copy(src, dst, out_sem.at[i])
        for i, (src, dst) in enumerate(
            [
                (output, output_hbm), (grad_field, grad_field_hbm),
                (gat_ab.at[core], gat_ab_hbm.at[core]), (gat_d.at[core], gat_d_hbm.at[core]),
                (gat_ab.at[1 - core], gat_ab_hbm.at[1 - core]),
                (gat_d.at[1 - core], gat_d_hbm.at[1 - core]),
            ]
        )
    ]

    barrier = pltpu.get_barrier_semaphore()

    def greet(device):
        pl.semaphore_signal(barrier, inc=1, device_id=device, device_id_type=MESH)

    def others(n, fn):
        def step(j, _):
            half = lax.div(j, 2)
            fn(n // 2 + jnp.where(lax.rem(j, 2) == 1, half, -half))
            return 0

        lax.fori_loop(1, n, step, 0)

    for way in reversed(WAY):
        greet(at(*way))
    others(g2, lambda k: greet(peer2(wrap(z_at + k, g2))))
    others(g1, lambda k: greet(peer1(wrap(m1 + k, g1))))
    greet(sibling)

    def halo(which, src, dst, sign):
        return [
            pltpu.make_async_remote_copy(
                src_ref=src.at[pl.ds(MAT[i], MROWS[i])],
                dst_ref=dst.at[pl.ds(MAT[i], MROWS[i])],
                send_sem=halo_send.at[which, i],
                recv_sem=halo_recv.at[which, i],
                device_id=at(sign * WAY[i][0], sign * WAY[i][1]),
                device_id_type=MESH,
            )
            for i in range(8)
        ]

    there = halo(0, msg, halo_x, 1)
    back = halo(1, back_src, back_dst, -1)

    lane = lax.broadcasted_iota(jnp.int32, (1, 256), 1)
    for n, tile in ((144, tile0), (72, tile1), (40, tile2)):
        rows = lax.broadcasted_iota(jnp.int32, (n, HEADS * n), 0)
        cols = lax.broadcasted_iota(jnp.int32, (n, HEADS * n), 1)
        hit = jnp.zeros((n, HEADS * n), F32)
        for h in range(HEADS):
            hit = jnp.where(cols == rows + n * h, 1.0, hit)
        tile[...] = hit.astype(BF)
    eye = (
        lax.broadcasted_iota(jnp.int32, (C, C), 0) == lax.broadcasted_iota(jnp.int32, (C, C), 1)
    ).astype(F32).astype(BF)

    loads[0].wait()
    loads[1].wait()
    for load in loads[2:12]:
        load.start()
    msg[...] = dot(gather[NQS:, :], field[...]).astype(BF)
    pl.semaphore_wait(barrier, 9 + (g1 - 1) + (g2 - 1))
    for copy in reversed(there):
        copy.start()
    x_q[...] = dot(gather[0:NQS, :], field[...])

    loads[2].wait()
    loads[12].wait()
    slot = lax.broadcasted_iota(jnp.int32, (32, 256), 0)
    value = jnp.where(slot == BANDS, 3, -1)
    for j in range(BANDS):
        band = region[wrap(lat * ROWS + j - 3, nlat * ROWS)]
        value = jnp.where(slot == j, band, value)
    column = lax.broadcasted_iota(jnp.int32, (32, 256), 1) - C
    band_hot = jnp.where((column >= 0) & (value == column), 1.0, 0.0).astype(BF)
    member = dot(row_of[...], band_hot)
    closed[...] = jnp.where((lane >= C) & (lane < C + 4), (member - 1.0) * 1e30, 0.0)

    for load in loads[3:5]:
        load.wait()
    wpad[...] = jnp.zeros_like(wpad)
    for i in range(3):
        wpad[:, 256 * i : 256 * i + C] = w_qkv[:, C * i : C * i + C]
    gain_attn = gain_a[...]

    normed, inverse1 = norm(x_q[...])
    norm_q[...] = normed
    h1_q[...] = (normed * gain_attn).astype(BF)
    qf[...] = dot(h1_q[...], wpad[:, 0:256]).astype(BF).astype(F32)

    def keys_of(first, last):
        rows = pl.ds(KAT[first], KAT[last] - KAT[first])
        t_win[rows, :] = (t_norm[rows, :] * gain_attn).astype(BF)
        both = dot(t_win[rows, :], wpad[:, 256:768])
        kx[rows, :] = (both[:, 0:256] + member[KAT[first] : KAT[last]]).astype(BF)
        vx[rows, :] = both[:, 256 : 256 + C].astype(BF)

    def kept(w):
        if w == 0:
            return p0, tile0
        return (p1.at[w - 1], tile1) if w < 5 else (p2.at[w - 5], tile2)

    def gather_heads(full, tile):
        n = full.shape[1] // HEADS
        at_lane = lax.broadcasted_iota(jnp.int32, (1, HEADS * n), 1)
        parts = [
            jnp.where(
                (at_lane >= n * h) & (at_lane < n * h + n), full[32 * h : 32 * h + 32], 0.0
            )
            for h in range(HEADS)
        ]
        return dot(tile[...], jnp.concatenate(parts, 0).astype(BF), NT)

    def by_head(inside, outside, width):
        at_lane = lane[:, :width]
        return jnp.concatenate(
            [
                jnp.where((at_lane >= 32 * h) & (at_lane < 32 * h + 32), inside, outside)
                for h in range(HEADS)
            ],
            0,
        ).astype(BF)

    def rows_of(w):
        return pl.ds(QAT[w], NQ[w]), pl.ds(KAT[w], NK[w]), pl.ds(HEADS * QAT[w], HEADS * NQ[w])

    def forward(w):
        q_rows, k_rows, m_rows = rows_of(w)
        keep, tile = kept(w)
        qm[m_rows, :] = by_head(qf[q_rows, :], closed[pl.ds(KAT[w], NQ[w]), :], 256)
        scores = dot(kx[k_rows, :], qm[m_rows, :], NT) * (SCALE * LOG2E)
        top = jnp.max(scores, 0, keepdims=True)
        expo = jnp.exp2(scores - top)
        prob = expo * (1.0 / jnp.sum(expo, 0, keepdims=True))
        keep[...] = prob
        value_t = dot(eye, vx[k_rows, :], NT).astype(BF)
        heads[q_rows, :] = gather_heads(dot(value_t, prob.astype(BF)), tile)

    def backward(w):
        q_rows, k_rows, m_rows = rows_of(w)
        keep, tile = kept(w)
        do = by_head(downs[q_rows, :], 0.0, C)
        prob = keep[...]
        dprob = dot(vx[k_rows, :], do, NT)
        dscore = (prob * (dprob - jnp.sum(dprob * prob, 0, keepdims=True))).astype(BF)
        dv_all[k_rows, :] = dot(prob.astype(BF), do).astype(BF)
        dk_all[k_rows, :] = (dot(dscore, qm[m_rows, 0:C]) * SCALE).astype(BF)
        key_t = dot(eye, kx[k_rows, 0:C], NT).astype(BF)
        dq_all[q_rows, :] = gather_heads(dot(key_t, dscore) * SCALE, tile)

    def mlp(rows):
        x = x_q[rows, :]
        g = g_q[rows, :]
        owned = heads[rows, :].astype(BF)
        own_b[rows, :] = owned
        mixed = x + dot(owned, w_out[...])
        normed2, inverse2 = norm(mixed)
        gain_mlp = gain_m[...]
        h2b = (normed2 * gain_mlp).astype(BF)
        h2[rows, :] = h2b
        pre = dot(h2b, w_up[...])
        square = pre * pre
        tangent = jnp.tanh(0.7978845608 * pre * (1.0 + 0.044715 * square))
        half = 0.5 * (1.0 + tangent)
        actb = (pre * half).astype(BF)
        act[rows, :] = actb
        slope = half + 0.5 * pre * (1.0 - tangent * tangent) * 0.7978845608 * (
            1.0 + 3.0 * 0.044715 * square
        )
        out_q[rows, :] = (mixed + dot(actb, w_down[...], NT)).astype(BF)
        dpreb = (dot(g, w_down[...]) * slope).astype(BF)
        dpre[rows, :] = dpreb
        dh2 = dot(dpreb, w_up[...], NT)
        dm = g.astype(F32) + norm_back(dh2, normed2, inverse2, gain_mlp)
        dmix[rows, :] = dm
        dmb = dm.astype(BF)
        dmixb[rows, :] = dmb
        downs[rows, :] = dot(dmb, w_out[...], NT).astype(BF).astype(F32)
        return jnp.sum(dh2 * normed2, 0, keepdims=True)

    t_norm[0:144, :] = normed[0:144]
    keys_of(0, 1)
    forward(0)
    for load in loads[5:10]:
        load.wait()
    g_q[...] = dot(gather[0:NQS, :], grad[...]).astype(BF)
    term_m = mlp(pl.ds(0, 144))
    backward(0)

    for copy in there:
        copy.wait_recv()
    norm_h[...] = norm(halo_x[...].astype(F32))[0]
    for w in range(1, 9):
        t_norm[pl.ds(KAT[w], NQ[w]), :] = norm_q[pl.ds(QAT[w], NQ[w]), :]
        to = KAT[w] + NQ[w]
        for start, size in PARTS[w]:
            t_norm[pl.ds(to, size), :] = norm_h[pl.ds(start, size), :]
            to += size
    keys_of(1, 9)
    for w in range(1, 9):
        forward(w)
    term_m = term_m + mlp(pl.ds(144, NQS - 144))

    def core_copy(which, stage, src, dst):
        return pltpu.make_async_remote_copy(
            src_ref=src, dst_ref=dst,
            send_sem=core_send.at[which, stage], recv_sem=core_recv.at[which, stage],
            device_id=sibling, device_id_type=MESH,
        )

    def remote(which, stage, k, src, dst, device):
        return pltpu.make_async_remote_copy(
            src_ref=src, dst_ref=dst,
            send_sem=red_send.at[which, stage, k], recv_sem=red_recv.at[which, stage, k],
            device_id=device, device_id_type=MESH,
        )

    def each(n, one, fn, back=None):
        others(n, lambda k: one(k, fn) if back is None else one(k, fn, wrap(back - k, n)))

    def go(copy):
        copy.start()

    def got(copy):
        copy.wait_recv()

    def sent(copy):
        copy.wait_send()

    def split_row(block):
        total = block[0:1] + block[1:2]
        high = total.astype(BF).astype(F32)
        at_row = lax.broadcasted_iota(jnp.int32, block.shape, 0)
        rest = jnp.where(at_row == 1, jnp.broadcast_to(total - high, block.shape), 0.0)
        return jnp.where(at_row == 0, jnp.broadcast_to(high, block.shape), rest).astype(BF)

    class Chain:
        def __init__(self, which, plan, src, rc, s0, r1, s1, r2, fin, sh, gat):
            self.which, self.plan = which, plan
            self.src, self.rc, self.s0, self.r1 = src, rc, s0, r1
            self.s1, self.r2, self.fin, self.sh, self.gat = s1, r2, fin, sh, gat
            self.mine = m1 < plan.own
            self.first = core_copy(which, 0, src.at[1 - core], rc)
            self.last = core_copy(which, 1, gat.at[core], gat.at[core])

        def a2a1(self, k, fn):
            target = wrap(m1 + k, g1)
            start = pl.multiple_of(target * self.plan.r, 16)
            copy = remote(
                self.which, 0, k, self.s0.at[pl.ds(start, self.plan.r)], self.r1.at[k],
                peer1(target),
            )
            pl.when(target < self.plan.own)(functools.partial(fn, copy))

        def come1(self, k, fn):
            fn(remote(self.which, 0, k, self.r1.at[k], self.r1.at[k], peer1(wrap(m1 + k, g1))))

        def a2a2(self, k, fn):
            target = wrap(z_at + k, g2)
            copy = remote(self.which, 1, k, self.s1.at[target], self.r2.at[k], peer2(target))
            pl.when(self.mine & (target < self.plan.pieces))(functools.partial(fn, copy))

        def come2(self, k, fn):
            fn(remote(self.which, 1, k, self.r2.at[k], self.r2.at[k], peer2(wrap(z_at + k, g2))))

        def all2(self, k, fn, source=None):
            source = z_at if source is None else source
            copy = remote(
                self.which, 2, k, self.fin.at[source], self.fin.at[source],
                peer2(wrap(z_at + k, g2)),
            )
            pl.when(self.mine & (source < self.plan.pieces))(functools.partial(fn, copy))

        def all1(self, k, fn, source=None):
            source = m1 if source is None else source
            copy = remote(
                self.which, 3, k, self.sh, self.gat.at[core, source], peer1(wrap(m1 + k, g1))
            )
            pl.when(source < self.plan.own)(functools.partial(fn, copy))

        def begin(self):
            self.first.start()

        def pair(self):
            self.first.wait_recv()
            total = self.src[core] + self.rc[...]
            self.s0[...] = total.astype(BF)
            if self.which == 1:
                self.s0[GAINS : GAINS + 16, :] = split_row(total[GAINS : GAINS + 16])
            each(g1, self.a2a1, go)

        def plane(self):
            plan = self.plan

            @pl.when(self.mine)
            def _():
                each(g1, self.come1, got)
                start = pl.multiple_of(m1 * plan.r, 16)
                total = self.s0[pl.ds(start, plan.r), :].astype(F32)
                for k in range(1, g1):
                    total = total + self.r1[k].astype(F32)
                for j in range(plan.pieces):
                    i, t = j // plan.across, j % plan.across
                    self.s1[j] = total[
                        i * plan.piece : (i + 1) * plan.piece, t * plan.lanes : (t + 1) * plan.lanes
                    ]

            each(g2, self.a2a2, go)

        def line(self):
            @pl.when(self.mine & (z_at < self.plan.pieces))
            def _():
                each(g2, self.come2, got)
                total = self.s1[z_at]
                for k in range(1, g2):
                    total = total + self.r2[k]
                self.fin[z_at] = total

            each(g2, self.all2, go)

        def spread(self):
            each(g2, self.all2, got, z_at)

            @pl.when(self.mine)
            def _():
                across = self.plan.across
                rows = [
                    jnp.concatenate([self.fin[across * i + t] for t in range(across)], 1)
                    for i in range(2)
                ]
                whole = jnp.concatenate(rows, 0)
                shard = whole.astype(BF)
                if self.which == 1:
                    first = jnp.where(m1 == GAINS // self.plan.r, split_row(whole[:16]), shard[:16])
                    shard = first if self.plan.r == 16 else jnp.concatenate([first, shard[16:]], 0)
                self.sh[...] = shard
                self.gat[core, m1] = shard

            each(g1, self.all1, go)

        def collect(self):
            each(g1, self.all1, got, m1)
            self.last.start()

        def end(self):
            self.last.wait_recv()

        def drain(self):
            self.first.wait_send()
            each(g1, self.a2a1, sent)
            each(g2, self.a2a2, sent)

        def drain_late(self):
            each(g2, self.all2, sent)
            each(g1, self.all1, sent)

    ab = Chain(0, plan_ab, ab_src, ab_rc, ab_s0, ab_r1, ab_s1, ab_r2, ab_fin, ab_sh, gat_ab)
    dd = Chain(1, plan_d, d_src, d_rc, d_s0, d_r1, d_s1, d_r2, d_fin, d_sh, gat_d)

    down_term = dot(g_q[...], act[...], TN)
    up_term = dot(h2[...], dpre[...], TN)
    out_term = fold(dot(own_b[...], dmixb[...], TN))
    for i in range(2):
        cols = slice(i * HALF, (i + 1) * HALF)
        ab_src[i, 0:C, :] = down_term[:, cols]
        ab_src[i, C : 2 * C, :] = up_term[:, cols]
        ab_src[i, 2 * C : 2 * C + FOLD, :] = out_term[:, cols]
        if plan_ab.rows > 2 * C + FOLD:
            ab_src[i, 2 * C + FOLD :, :] = jnp.zeros((plan_ab.rows - 2 * C - FOLD, HALF), F32)
    ab.begin()

    for w in range(1, 9):
        backward(w)
        if w == 4:
            ab.pair()

    dsource = dot(dk_all[...], wpad[:, 256 : 256 + C], NT) + dot(dv_all[...], wpad[:, 512 : 512 + C], NT)
    dq_b = dq_all[...].astype(BF)
    dq_source = dot(dq_b, wpad[:, 0:C], NT)
    back_f[...] = jnp.zeros_like(back_f)
    for w in range(9):
        dsq[pl.ds(QAT[w], NQ[w]), :] = (
            dsource[KAT[w] : KAT[w] + NQ[w]] + dq_source[QAT[w] : QAT[w + 1]]
        )
        to = KAT[w] + NQ[w]
        for start, size in PARTS[w]:
            back_f[pl.ds(start, size), :] = dsource[to : to + size]
            to += size
    back_src[...] = back_f[...].astype(BF)
    for copy in reversed(back):
        copy.start()

    term_a = jnp.sum(dsource * t_norm[...], 0, keepdims=True) + jnp.sum(
        dq_source * norm_q[...], 0, keepdims=True
    )
    d_term = jnp.concatenate(
        [
            fold(dot(h1_q[...], dq_b, TN)), fold(dot(t_win[...], dk_all[...], TN)),
            fold(dot(t_win[...], dv_all[...], TN)),
        ],
        0,
    )
    gains = jnp.concatenate([term_a, term_m], 1)
    first_row = lax.broadcasted_iota(jnp.int32, (16, HALF), 0) == 0
    for i in range(2):
        d_src[i, 0:GAINS, :] = d_term[:, i * HALF : (i + 1) * HALF]
        if plan_d.rows > GAINS + 16:
            d_src[i, GAINS + 16 :, :] = jnp.zeros((plan_d.rows - GAINS - 16, HALF), F32)
    d_src[0, GAINS : GAINS + 16, :] = jnp.where(first_row, jnp.broadcast_to(gains, (16, HALF)), 0.0)
    d_src[1, GAINS : GAINS + 16, :] = jnp.zeros((16, HALF), F32)
    dd.begin()

    dd.pair()
    loads[10].wait()
    loads[11].wait()
    output[...] = dot(to_nat[...], out_q[...]).astype(BF)
    stores[0].start()
    ab.plane()
    dd.plane()
    for copy in back:
        copy.wait_recv()
    dshift = (dsq[...] + dot(collect[...], back_dst[...])).astype(BF).astype(F32)
    gf = dmix[...] + norm_back(dshift, norm_q[...], inverse1, gain_attn)
    grad_field[...] = dot(to_nat[...], gf.astype(BF)).astype(BF)
    stores[1].start()
    ab.line()
    dd.line()
    ab.spread()
    dd.spread()
    for copy in there + back:
        copy.wait_send()
    ab.drain()
    dd.drain()
    ab.collect()
    stores[2].start()
    dd.collect()
    stores[3].start()
    ab.drain_late()
    dd.drain_late()
    ab.end()
    stores[4].start()
    dd.end()
    stores[5].start()
    ab.last.wait_send()
    dd.last.wait_send()
    for store in stores:
        store.wait()


def final(plans, out_n, gf_n, gat_ab_in, gat_d_in, *refs):
    outs = refs[:8]
    out_v8, gf_v, gat_ab, gat_d, qkv_v, out_v, up_v, down_v, ga_v, gm_v, in_sem, out_sem = refs[8:]
    loads = [
        pltpu.make_async_copy(src, dst, in_sem.at[i])
        for i, (src, dst) in enumerate(
            [(gat_d_in, gat_d), (gat_ab_in, gat_ab), (out_n, out_v8), (gf_n, gf_v)]
        )
    ]
    for load in loads:
        load.start()
    stores = [
        pltpu.make_async_copy(src, dst, out_sem.at[i])
        for i, (src, dst) in enumerate(
            zip((out_v8, gf_v, qkv_v, out_v, up_v, down_v, ga_v, gm_v), outs)
        )
    ]

    def whole(plan, gat):
        halves = [gat[i].astype(F32).reshape(plan.rows, HALF) for i in range(2)]
        return jnp.concatenate(halves, 1)

    loads[0].wait()
    d = whole(plans[1], gat_d)
    qkv_v[...] = jnp.concatenate([unfold(d[FOLD * i : FOLD * (i + 1)]) for i in range(3)], 1)
    gains = d[GAINS : GAINS + 1] + d[GAINS + 1 : GAINS + 2]
    ga_v[...] = gains[:, :C]
    gm_v[...] = gains[:, C : 2 * C]
    for at in (2, 6, 7):
        stores[at].start()
    for at in range(2):
        loads[2 + at].wait()
        stores[at].start()
    loads[1].wait()
    ab = whole(plans[0], gat_ab)
    down_v[...] = ab[:C]
    up_v[...] = ab[C : 2 * C]
    out_v[...] = unfold(ab[2 * C : 2 * C + FOLD])
    stores[3].start()
    stores[4].start()
    stores[5].start()
    for store in stores:
        store.wait()


def body(nlon, nlat, field, region, w_qkv, w_out, w_up, w_down, gain_attn, gain_mlp, grad_next):
    sizes = (nlon // 8, 2, 4, nlat) if nlon >= 16 else (nlon // 2, 1, 2, nlat)
    nz, ny, nx, _ = sizes
    g1, g2 = ny * (nlat // 2) * nx, nz
    plans = (Plan(2 * C + FOLD, g1, g2), Plan(GAINS + 16, g1, g2))
    hbm = pl.BlockSpec(memory_space=pltpu.HBM)
    V = pltpu.VMEM
    consts = [jnp.asarray(a) for a in tables()]
    operands = [
        field.reshape(TOK, C), grad_next.reshape(TOK, C), region, w_qkv, w_out, w_up, w_down.T,
        gain_attn.reshape(1, C), gain_mlp.reshape(1, C), *consts,
    ]

    def pair(shape_of, kind):
        return [V(shape_of(p), kind) for p in plans]

    shapes = [jax.ShapeDtypeStruct((TOK, C), BF)] * 2 + [
        jax.ShapeDtypeStruct((2, p.own, p.r, HALF), BF) for p in plans
    ]
    scratch = (
        [V(a.shape, a.dtype) for a in shapes]
        + [(pltpu.SMEM if i == 2 else V)(a.shape, a.dtype) for i, a in enumerate(operands)]
        + [V((HALO, C), BF)] * 4 + [V((HALO, C), F32)]
        + [
            V((NQS, C), F32), V((NQS, C), BF), V((NQS, C), BF), V((NQS, C), F32),
            V((HALO, C), F32), V((NKS, C), F32), V((NKS, C), BF), V((C, FF), BF),
            V((NQS, 256), F32), V((NKS, 256), BF), V((NKS, C), BF), V((NKS, 256), F32),
            V((HEADS * NQS, 256), BF),
            V((144, HEADS * 144), F32), V((4, 144, HEADS * 72), F32), V((4, 160, HEADS * 40), F32),
            V((144, HEADS * 144), BF), V((72, HEADS * 72), BF), V((40, HEADS * 40), BF),
            V((NQS, C), F32), V((NQS, C), BF),
            V((NQS, C), BF), V((NQS, FF), BF), V((NQS, FF), BF), V((NQS, C), F32),
            V((NQS, C), BF), V((NQS, C), F32), V((NQS, C), F32),
            V((NKS, C), BF), V((NKS, C), BF), V((NQS, C), F32), V((NQS, C), BF),
        ]
        + pair(lambda p: (2, p.rows, HALF), F32)
        + pair(lambda p: (p.rows, HALF), F32)
        + pair(lambda p: (p.rows, HALF), BF)
        + pair(lambda p: (g1, p.r, HALF), BF)
        + pair(lambda p: (p.pieces, p.piece, p.lanes), F32)
        + pair(lambda p: (g2, p.piece, p.lanes), F32)
        + pair(lambda p: (p.pieces, p.piece, p.lanes), F32)
        + pair(lambda p: (p.r, HALF), BF)
        + [
            pltpu.SemaphoreType.DMA((13,)),
            pltpu.SemaphoreType.DMA((6,)),
            pltpu.SemaphoreType.DMA((2, 8)),
            pltpu.SemaphoreType.DMA((2, 8)),
            pltpu.SemaphoreType.DMA((2, 2)),
            pltpu.SemaphoreType.DMA((2, 2)),
            pltpu.SemaphoreType.DMA((2, 4, 16)),
            pltpu.SemaphoreType.DMA((2, 4, 16)),
        ]
    )
    mids = pl.pallas_call(
        functools.partial(kernel, sizes, plans),
        out_shape=shapes,
        in_specs=[hbm] * len(operands),
        out_specs=[hbm] * 4,
        scratch_shapes=scratch,
        compiler_params=pltpu.CompilerParams(
            collective_id=0, has_side_effects=True, vmem_limit_bytes=VLIM
        ),
        name="block",
    )(*operands)
    results = [
        jax.ShapeDtypeStruct((TOK, C), BF),
        jax.ShapeDtypeStruct((TOK, C), BF),
        jax.ShapeDtypeStruct((C, 3 * C), F32),
        jax.ShapeDtypeStruct((C, C), F32),
        jax.ShapeDtypeStruct((C, FF), F32),
        jax.ShapeDtypeStruct((C, FF), F32),
        jax.ShapeDtypeStruct((1, C), F32),
        jax.ShapeDtypeStruct((1, C), F32),
    ]
    outs = pl.pallas_call(
        functools.partial(final, plans),
        out_shape=results,
        in_specs=[hbm] * 4,
        out_specs=[hbm] * 8,
        scratch_shapes=[V(a.shape, a.dtype) for a in shapes + results[2:]]
        + [pltpu.SemaphoreType.DMA((4,)), pltpu.SemaphoreType.DMA((8,))],
        compiler_params=pltpu.CompilerParams(vmem_limit_bytes=VLIM),
        name="final",
    )(*mids)
    output, grad_field, grad_qkv, grad_out, grad_up, grad_down_t, grad_ga, grad_gm = outs
    return (
        output.reshape(field.shape), grad_field.reshape(field.shape),
        grad_qkv, grad_out, grad_up, grad_down_t.T, grad_ga.reshape(C), grad_gm.reshape(C),
    )


def solution(mesh):
    grid = P(None, "lat", "lon", None)
    return jax.shard_map(
        functools.partial(body, mesh.shape["lon"], mesh.shape["lat"]),
        mesh=mesh,
        in_specs=(grid, P(), P(), P(), P(), P(), P(), P(), grid),
        out_specs=(grid, grid, P(), P(), P(), P(), P(), P()),
        check_vma=False,
    )
```

```python
import functools

import jax
import jax.numpy as jnp
import ml_dtypes
import numpy as np
from jax import lax
from jax.experimental import pallas as pl
from jax.experimental.pallas import tpu as pltpu
from jax.sharding import PartitionSpec as P

C = 192
HEADS = 6
FF = 768
HALF = 384
ROWS = 12
COLS = 24
TOK = 2 * ROWS * COLS
SCALE = 32.0 ** -0.5
LOG2E = 1.4426950408889634
F32 = jnp.float32
BF = jnp.bfloat16
MESH = pl.DeviceIdType.MESH
VLIM = 54 << 20

NQ = (144,) + (72,) * 4 + (40,) * 4
NK = (144,) + (144,) * 4 + (160,) * 4
QAT = tuple(int(v) for v in np.cumsum((0,) + NQ))
KAT = tuple(int(v) for v in np.cumsum((0,) + NK))
NQS, NKS = QAT[-1], KAT[-1]
WAY = ((0, -1), (0, 1), (-1, 0), (1, 0), (-1, -1), (-1, 1), (1, -1), (1, 1))
MAT = (0, 160, 320, 480, 640, 688, 736, 784)
MROWS = (160,) * 4 + (48,) * 4
HALO = 832
PARTS = (
    (),
    ((0, 72),),
    ((160, 72),),
    ((320, 72),),
    ((480, 72),),
    ((112, 40), (320 + 112, 40), (640, 40)),
    ((160 + 112, 40), (320 + 72, 40), (688, 40)),
    ((72, 40), (480 + 112, 40), (736, 40)),
    ((160 + 72, 40), (480 + 72, 40), (784, 40)),
)
BANDS = 18
FOLD = C // 4
GAINS = 3 * FOLD


def tables():
    def piece(rows, cols, size=None):
        got = [(l * ROWS * COLS + r * COLS + c, r) for l in range(2) for r in rows for c in cols]
        return got + [(-1, None)] * ((size or len(got)) - len(got))

    top, mid, bot = range(0, 3), range(3, 9), range(9, 12)
    left, cen, rig = range(0, 6), range(6, 18), range(18, 24)
    own = [
        piece(mid, cen),
        piece(mid, rig), piece(mid, left), piece(bot, cen), piece(top, cen),
        piece(bot, rig, 40), piece(bot, left, 40), piece(top, rig, 40), piece(top, left, 40),
    ]
    sent = [
        piece(mid, side) + piece(top, side, 40) + piece(bot, side, 48) for side in (left, rig)
    ] + [
        piece(rows, cen) + piece(rows, left, 40) + piece(rows, rig, 48) for rows in (top, bot)
    ] + [
        piece(top, left, 48), piece(top, rig, 48), piece(bot, left, 48), piece(bot, rig, 48),
    ]
    shift = (0, 0, ROWS, -ROWS, ROWS, ROWS, -ROWS, -ROWS)
    flat_own = sum(own, [])
    flat_sent = sum(sent, [])
    moved = sum(
        [[(i, None if r is None else r + s) for i, r in part] for part, s in zip(sent, shift)], []
    )
    assert len(flat_own) == NQS and len(flat_sent) == HALO

    def hot(tokens):
        out = np.zeros((len(tokens), TOK), np.float32)
        for at, (index, _) in enumerate(tokens):
            if index >= 0:
                out[at, index] = 1
        return out

    keys = []
    for w in range(9):
        keys += own[w]
        for start, size in PARTS[w]:
            keys += moved[start : start + size]
    row_of = np.zeros((NKS, 32), np.float32)
    for at, (_, row) in enumerate(keys):
        row_of[at, BANDS if row is None else row + 3] = 1
    to_own, to_sent = hot(flat_own), hot(flat_sent)
    kind = ml_dtypes.bfloat16
    return [
        np.ascontiguousarray(a).astype(kind)
        for a in (np.concatenate([to_own, to_sent]), to_own.T, to_own @ to_sent.T, row_of)
    ]


def dot(a, b, dims=((1,), (0,))):
    return lax.dot_general(a, b, (dims, ((), ())), preferred_element_type=F32)


NT = ((1,), (1,))
TN = ((0,), (0,))


def fold(square):
    return jnp.concatenate([square[FOLD * j : FOLD * (j + 1)] for j in range(4)], 1)


def unfold(wide):
    return jnp.concatenate([wide[:, C * j : C * (j + 1)] for j in range(4)], 0)


def norm(x):
    mean = jnp.mean(x, -1, keepdims=True)
    centred = x - mean
    inverse = lax.rsqrt(jnp.mean(centred * centred, -1, keepdims=True) + 1e-05)
    return centred * inverse, inverse


def norm_back(d, normed, inverse, gain):
    dn = d * gain
    return inverse * (
        dn - jnp.mean(dn, -1, keepdims=True) - normed * jnp.mean(dn * normed, -1, keepdims=True)
    )


class Plan:
    def __init__(self, rows, g1, g2):
        self.r = 16 * -(-rows // (16 * g1))
        self.own = -(-rows // self.r)
        self.rows = self.own * self.r
        self.piece = self.r // 2
        self.across = 3 if g2 >= 6 else 1
        self.pieces = 2 * self.across
        self.lanes = HALF // self.across


def kernel(
    sizes, plans,
    field_in, grad_in, region_in, wqkv_in, wout_in, wup_in, wdown_in, gaina_in, gainm_in,
    gather_in, to_nat_in, collect_in, row_of_in,
    output_hbm, grad_field_hbm, gat_ab_hbm, gat_d_hbm,
    output, grad_field, gat_ab, gat_d,
    field, grad, region, w_qkv, w_out, w_up, w_down, gain_a, gain_m, gather, to_nat, collect, row_of,
    msg, halo_x, back_src, back_dst, back_f,
    x_q, g_q, h1_q, norm_q, norm_h, t_norm, t_win, wpad, qf, kx, vx, closed,
    qm, p0, p1, p2, tile0, tile1, tile2, heads, own_b,
    h2, act, dpre, dmix, dmixb, downs, dq_all, dk_all, dv_all, dsq, out_q,
    ab_src, d_src, ab_rc, d_rc, ab_s0, d_s0, ab_r1, d_r1, ab_s1, d_s1, ab_r2, d_r2,
    ab_fin, d_fin, ab_sh, d_sh,
    in_sem, out_sem, halo_send, halo_recv, core_send, core_recv, red_send, red_recv,
):
    nz, ny, nx, nlat = sizes
    nlon = nz * ny * nx
    g1, g2 = ny * (nlat // 2) * nx, nz
    lon = lax.axis_index("lon")
    lat = lax.axis_index("lat")
    core = lax.rem(lat, 2)
    x_at, y_at, z_at = lax.rem(lon, nx), lax.rem(lax.div(lon, nx), ny), lax.div(lon, nx * ny)
    m1 = (y_at * (nlat // 2) + lax.div(lat, 2)) * nx + x_at
    plan_ab, plan_d = plans

    def wrap(i, n):
        return lax.rem(i + n, n)

    def at(dlat, dlon):
        return {"lon": wrap(lon + dlon, nlon), "lat": wrap(lat + dlat, nlat)}

    def peer1(m):
        y = lax.div(m, nx)
        return {
            "lon": (z_at * ny + lax.div(y, nlat // 2)) * nx + lax.rem(m, nx),
            "lat": lax.rem(y, nlat // 2) * 2 + core,
        }

    def peer2(v):
        return {"lon": v * (nx * ny) + lax.rem(lon, nx * ny), "lat": lat}

    sibling = {"lon": lon, "lat": lat + 1 - 2 * core}

    loads = [
        pltpu.make_async_copy(src, dst, in_sem.at[i])
        for i, (src, dst) in enumerate(
            [
                (field_in, field), (gather_in, gather), (row_of_in, row_of), (gaina_in, gain_a),
                (wqkv_in, w_qkv), (grad_in, grad), (wout_in, w_out), (gainm_in, gain_m),
                (wup_in, w_up), (wdown_in, w_down), (to_nat_in, to_nat), (collect_in, collect),
                (region_in, region),
            ]
        )
    ]
    loads[0].start()
    loads[1].start()
    loads[12].start()
    stores = [
        pltpu.make_async_copy(src, dst, out_sem.at[i])
        for i, (src, dst) in enumerate(
            [
                (output, output_hbm), (grad_field, grad_field_hbm),
                (gat_ab.at[core], gat_ab_hbm.at[core]), (gat_d.at[core], gat_d_hbm.at[core]),
                (gat_ab.at[1 - core], gat_ab_hbm.at[1 - core]),
                (gat_d.at[1 - core], gat_d_hbm.at[1 - core]),
            ]
        )
    ]

    barrier = pltpu.get_barrier_semaphore()

    def greet(device):
        pl.semaphore_signal(barrier, inc=1, device_id=device, device_id_type=MESH)

    def others(n, fn):
        def step(j, _):
            half = lax.div(j, 2)
            fn(n // 2 + jnp.where(lax.rem(j, 2) == 1, half, -half))
            return 0

        lax.fori_loop(1, n, step, 0)

    for way in reversed(WAY):
        greet(at(*way))
    others(g2, lambda k: greet(peer2(wrap(z_at + k, g2))))
    others(g1, lambda k: greet(peer1(wrap(m1 + k, g1))))
    greet(sibling)

    def halo(which, src, dst, sign):
        return [
            pltpu.make_async_remote_copy(
                src_ref=src.at[pl.ds(MAT[i], MROWS[i])],
                dst_ref=dst.at[pl.ds(MAT[i], MROWS[i])],
                send_sem=halo_send.at[which, i],
                recv_sem=halo_recv.at[which, i],
                device_id=at(sign * WAY[i][0], sign * WAY[i][1]),
                device_id_type=MESH,
            )
            for i in range(8)
        ]

    there = halo(0, msg, halo_x, 1)
    back = halo(1, back_src, back_dst, -1)

    lane = lax.broadcasted_iota(jnp.int32, (1, 256), 1)
    for n, tile in ((144, tile0), (72, tile1), (40, tile2)):
        rows = lax.broadcasted_iota(jnp.int32, (n, HEADS * n), 0)
        cols = lax.broadcasted_iota(jnp.int32, (n, HEADS * n), 1)
        hit = jnp.zeros((n, HEADS * n), F32)
        for h in range(HEADS):
            hit = jnp.where(cols == rows + n * h, 1.0, hit)
        tile[...] = hit.astype(BF)
    eye = (
        lax.broadcasted_iota(jnp.int32, (C, C), 0) == lax.broadcasted_iota(jnp.int32, (C, C), 1)
    ).astype(F32).astype(BF)

    loads[0].wait()
    loads[1].wait()
    for load in loads[2:12]:
        load.start()
    msg[...] = dot(gather[NQS:, :], field[...]).astype(BF)
    pl.semaphore_wait(barrier, 9 + (g1 - 1) + (g2 - 1))
    for copy in reversed(there):
        copy.start()
    x_q[...] = dot(gather[0:NQS, :], field[...])

    loads[2].wait()
    loads[12].wait()
    slot = lax.broadcasted_iota(jnp.int32, (32, 256), 0)
    value = jnp.where(slot == BANDS, 3, -1)
    for j in range(BANDS):
        band = region[wrap(lat * ROWS + j - 3, nlat * ROWS)]
        value = jnp.where(slot == j, band, value)
    column = lax.broadcasted_iota(jnp.int32, (32, 256), 1) - C
    band_hot = jnp.where((column >= 0) & (value == column), 1.0, 0.0).astype(BF)
    member = dot(row_of[...], band_hot)
    closed[...] = jnp.where((lane >= C) & (lane < C + 4), (member - 1.0) * 1e30, 0.0)

    for load in loads[3:5]:
        load.wait()
    wpad[...] = jnp.zeros_like(wpad)
    for i in range(3):
        wpad[:, 256 * i : 256 * i + C] = w_qkv[:, C * i : C * i + C]
    gain_attn = gain_a[...]

    normed, inverse1 = norm(x_q[...])
    norm_q[...] = normed
    h1_q[...] = (normed * gain_attn).astype(BF)
    qf[...] = dot(h1_q[...], wpad[:, 0:256]).astype(BF).astype(F32)

    def keys_of(first, last):
        rows = pl.ds(KAT[first], KAT[last] - KAT[first])
        t_win[rows, :] = (t_norm[rows, :] * gain_attn).astype(BF)
        both = dot(t_win[rows, :], wpad[:, 256:768])
        kx[rows, :] = (both[:, 0:256] + member[KAT[first] : KAT[last]]).astype(BF)
        vx[rows, :] = both[:, 256 : 256 + C].astype(BF)

    def kept(w):
        if w == 0:
            return p0, tile0
        return (p1.at[w - 1], tile1) if w < 5 else (p2.at[w - 5], tile2)

    def gather_heads(full, tile):
        n = full.shape[1] // HEADS
        at_lane = lax.broadcasted_iota(jnp.int32, (1, HEADS * n), 1)
        parts = [
            jnp.where(
                (at_lane >= n * h) & (at_lane < n * h + n), full[32 * h : 32 * h + 32], 0.0
            )
            for h in range(HEADS)
        ]
        return dot(tile[...], jnp.concatenate(parts, 0).astype(BF), NT)

    def by_head(inside, outside, width):
        at_lane = lane[:, :width]
        return jnp.concatenate(
            [
                jnp.where((at_lane >= 32 * h) & (at_lane < 32 * h + 32), inside, outside)
                for h in range(HEADS)
            ],
            0,
        ).astype(BF)

    def rows_of(w):
        return pl.ds(QAT[w], NQ[w]), pl.ds(KAT[w], NK[w]), pl.ds(HEADS * QAT[w], HEADS * NQ[w])

    def forward(w):
        q_rows, k_rows, m_rows = rows_of(w)
        keep, tile = kept(w)
        qm[m_rows, :] = by_head(qf[q_rows, :], closed[pl.ds(KAT[w], NQ[w]), :], 256)
        scores = dot(kx[k_rows, :], qm[m_rows, :], NT) * (SCALE * LOG2E)
        top = jnp.max(scores, 0, keepdims=True)
        expo = jnp.exp2(scores - top)
        prob = expo * (1.0 / jnp.sum(expo, 0, keepdims=True))
        keep[...] = prob
        value_t = dot(eye, vx[k_rows, :], NT).astype(BF)
        heads[q_rows, :] = gather_heads(dot(value_t, prob.astype(BF)), tile)

    def backward(w):
        q_rows, k_rows, m_rows = rows_of(w)
        keep, tile = kept(w)
        do = by_head(downs[q_rows, :], 0.0, C)
        prob = keep[...]
        dprob = dot(vx[k_rows, :], do, NT)
        dscore = (prob * (dprob - jnp.sum(dprob * prob, 0, keepdims=True))).astype(BF)
        dv_all[k_rows, :] = dot(prob.astype(BF), do).astype(BF)
        dk_all[k_rows, :] = (dot(dscore, qm[m_rows, 0:C]) * SCALE).astype(BF)
        key_t = dot(eye, kx[k_rows, 0:C], NT).astype(BF)
        dq_all[q_rows, :] = gather_heads(dot(key_t, dscore) * SCALE, tile)

    def mlp(rows):
        x = x_q[rows, :]
        g = g_q[rows, :]
        owned = heads[rows, :].astype(BF)
        own_b[rows, :] = owned
        mixed = x + dot(owned, w_out[...])
        normed2, inverse2 = norm(mixed)
        gain_mlp = gain_m[...]
        h2b = (normed2 * gain_mlp).astype(BF)
        h2[rows, :] = h2b
        pre = dot(h2b, w_up[...])
        square = pre * pre
        tangent = jnp.tanh(0.7978845608 * pre * (1.0 + 0.044715 * square))
        half = 0.5 * (1.0 + tangent)
        actb = (pre * half).astype(BF)
        act[rows, :] = actb
        slope = half + 0.5 * pre * (1.0 - tangent * tangent) * 0.7978845608 * (
            1.0 + 3.0 * 0.044715 * square
        )
        out_q[rows, :] = (mixed + dot(actb, w_down[...], NT)).astype(BF)
        dpreb = (dot(g, w_down[...]) * slope).astype(BF)
        dpre[rows, :] = dpreb
        dh2 = dot(dpreb, w_up[...], NT)
        dm = g.astype(F32) + norm_back(dh2, normed2, inverse2, gain_mlp)
        dmix[rows, :] = dm
        dmb = dm.astype(BF)
        dmixb[rows, :] = dmb
        downs[rows, :] = dot(dmb, w_out[...], NT).astype(BF).astype(F32)
        return jnp.sum(dh2 * normed2, 0, keepdims=True)

    t_norm[0:144, :] = normed[0:144]
    keys_of(0, 1)
    forward(0)
    for load in loads[5:10]:
        load.wait()
    g_q[...] = dot(gather[0:NQS, :], grad[...]).astype(BF)
    term_m = mlp(pl.ds(0, 144))
    backward(0)

    for copy in there:
        copy.wait_recv()
    norm_h[...] = norm(halo_x[...].astype(F32))[0]
    for w in range(1, 9):
        t_norm[pl.ds(KAT[w], NQ[w]), :] = norm_q[pl.ds(QAT[w], NQ[w]), :]
        to = KAT[w] + NQ[w]
        for start, size in PARTS[w]:
            t_norm[pl.ds(to, size), :] = norm_h[pl.ds(start, size), :]
            to += size
    keys_of(1, 9)
    for w in range(1, 9):
        forward(w)
    term_m = term_m + mlp(pl.ds(144, NQS - 144))

    def core_copy(which, stage, src, dst):
        return pltpu.make_async_remote_copy(
            src_ref=src, dst_ref=dst,
            send_sem=core_send.at[which, stage], recv_sem=core_recv.at[which, stage],
            device_id=sibling, device_id_type=MESH,
        )

    def remote(which, stage, k, src, dst, device):
        return pltpu.make_async_remote_copy(
            src_ref=src, dst_ref=dst,
            send_sem=red_send.at[which, stage, k], recv_sem=red_recv.at[which, stage, k],
            device_id=device, device_id_type=MESH,
        )

    def each(n, one, fn, back=None):
        others(n, lambda k: one(k, fn) if back is None else one(k, fn, wrap(back - k, n)))

    def go(copy):
        copy.start()

    def got(copy):
        copy.wait_recv()

    def sent(copy):
        copy.wait_send()

    def split_row(block):
        total = block[0:1] + block[1:2]
        high = total.astype(BF).astype(F32)
        at_row = lax.broadcasted_iota(jnp.int32, block.shape, 0)
        rest = jnp.where(at_row == 1, jnp.broadcast_to(total - high, block.shape), 0.0)
        return jnp.where(at_row == 0, jnp.broadcast_to(high, block.shape), rest).astype(BF)

    class Chain:
        def __init__(self, which, plan, src, rc, s0, r1, s1, r2, fin, sh, gat):
            self.which, self.plan = which, plan
            self.src, self.rc, self.s0, self.r1 = src, rc, s0, r1
            self.s1, self.r2, self.fin, self.sh, self.gat = s1, r2, fin, sh, gat
            self.mine = m1 < plan.own
            self.first = core_copy(which, 0, src.at[1 - core], rc)
            self.last = core_copy(which, 1, gat.at[core], gat.at[core])

        def a2a1(self, k, fn):
            target = wrap(m1 + k, g1)
            start = pl.multiple_of(target * self.plan.r, 16)
            copy = remote(
                self.which, 0, k, self.s0.at[pl.ds(start, self.plan.r)], self.r1.at[k],
                peer1(target),
            )
            pl.when(target < self.plan.own)(functools.partial(fn, copy))

        def come1(self, k, fn):
            fn(remote(self.which, 0, k, self.r1.at[k], self.r1.at[k], peer1(wrap(m1 + k, g1))))

        def a2a2(self, k, fn):
            target = wrap(z_at + k, g2)
            copy = remote(self.which, 1, k, self.s1.at[target], self.r2.at[k], peer2(target))
            pl.when(self.mine & (target < self.plan.pieces))(functools.partial(fn, copy))

        def come2(self, k, fn):
            fn(remote(self.which, 1, k, self.r2.at[k], self.r2.at[k], peer2(wrap(z_at + k, g2))))

        def all2(self, k, fn, source=None):
            source = z_at if source is None else source
            copy = remote(
                self.which, 2, k, self.fin.at[source], self.fin.at[source],
                peer2(wrap(z_at + k, g2)),
            )
            pl.when(self.mine & (source < self.plan.pieces))(functools.partial(fn, copy))

        def all1(self, k, fn, source=None):
            source = m1 if source is None else source
            copy = remote(
                self.which, 3, k, self.sh, self.gat.at[core, source], peer1(wrap(m1 + k, g1))
            )
            pl.when(source < self.plan.own)(functools.partial(fn, copy))

        def begin(self):
            self.first.start()

        def pair(self):
            self.first.wait_recv()
            total = self.src[core] + self.rc[...]
            self.s0[...] = total.astype(BF)
            if self.which == 1:
                self.s0[GAINS : GAINS + 16, :] = split_row(total[GAINS : GAINS + 16])
            each(g1, self.a2a1, go)

        def plane(self):
            plan = self.plan

            @pl.when(self.mine)
            def _():
                each(g1, self.come1, got)
                start = pl.multiple_of(m1 * plan.r, 16)
                total = self.s0[pl.ds(start, plan.r), :].astype(F32)
                for k in range(1, g1):
                    total = total + self.r1[k].astype(F32)
                for j in range(plan.pieces):
                    i, t = j // plan.across, j % plan.across
                    self.s1[j] = total[
                        i * plan.piece : (i + 1) * plan.piece, t * plan.lanes : (t + 1) * plan.lanes
                    ]

            each(g2, self.a2a2, go)

        def line(self):
            @pl.when(self.mine & (z_at < self.plan.pieces))
            def _():
                each(g2, self.come2, got)
                total = self.s1[z_at]
                for k in range(1, g2):
                    total = total + self.r2[k]
                self.fin[z_at] = total

            each(g2, self.all2, go)

        def spread(self):
            each(g2, self.all2, got, z_at)

            @pl.when(self.mine)
            def _():
                across = self.plan.across
                rows = [
                    jnp.concatenate([self.fin[across * i + t] for t in range(across)], 1)
                    for i in range(2)
                ]
                whole = jnp.concatenate(rows, 0)
                shard = whole.astype(BF)
                if self.which == 1:
                    first = jnp.where(m1 == GAINS // self.plan.r, split_row(whole[:16]), shard[:16])
                    shard = first if self.plan.r == 16 else jnp.concatenate([first, shard[16:]], 0)
                self.sh[...] = shard
                self.gat[core, m1] = shard

            each(g1, self.all1, go)

        def collect(self):
            each(g1, self.all1, got, m1)
            self.last.start()

        def end(self):
            self.last.wait_recv()

        def drain(self):
            self.first.wait_send()
            each(g1, self.a2a1, sent)
            each(g2, self.a2a2, sent)

        def drain_late(self):
            each(g2, self.all2, sent)
            each(g1, self.all1, sent)

    ab = Chain(0, plan_ab, ab_src, ab_rc, ab_s0, ab_r1, ab_s1, ab_r2, ab_fin, ab_sh, gat_ab)
    dd = Chain(1, plan_d, d_src, d_rc, d_s0, d_r1, d_s1, d_r2, d_fin, d_sh, gat_d)

    down_term = dot(g_q[...], act[...], TN)
    up_term = dot(h2[...], dpre[...], TN)
    out_term = fold(dot(own_b[...], dmixb[...], TN))
    for i in range(2):
        cols = slice(i * HALF, (i + 1) * HALF)
        ab_src[i, 0:C, :] = down_term[:, cols]
        ab_src[i, C : 2 * C, :] = up_term[:, cols]
        ab_src[i, 2 * C : 2 * C + FOLD, :] = out_term[:, cols]
        if plan_ab.rows > 2 * C + FOLD:
            ab_src[i, 2 * C + FOLD :, :] = jnp.zeros((plan_ab.rows - 2 * C - FOLD, HALF), F32)
    ab.begin()

    for w in range(1, 9):
        backward(w)
        if w == 4:
            ab.pair()

    dsource = dot(dk_all[...], wpad[:, 256 : 256 + C], NT) + dot(dv_all[...], wpad[:, 512 : 512 + C], NT)
    dq_b = dq_all[...].astype(BF)
    dq_source = dot(dq_b, wpad[:, 0:C], NT)
    term_a = jnp.sum(dsource * t_norm[...], 0, keepdims=True) + jnp.sum(
        dq_source * norm_q[...], 0, keepdims=True
    )
    d_term = jnp.concatenate(
        [
            fold(dot(h1_q[...], dq_b, TN)), fold(dot(t_win[...], dk_all[...], TN)),
            fold(dot(t_win[...], dv_all[...], TN)),
        ],
        0,
    )
    gains = jnp.concatenate([term_a, term_m], 1)
    first_row = lax.broadcasted_iota(jnp.int32, (16, HALF), 0) == 0
    for i in range(2):
        d_src[i, 0:GAINS, :] = d_term[:, i * HALF : (i + 1) * HALF]
        if plan_d.rows > GAINS + 16:
            d_src[i, GAINS + 16 :, :] = jnp.zeros((plan_d.rows - GAINS - 16, HALF), F32)
    d_src[0, GAINS : GAINS + 16, :] = jnp.where(first_row, jnp.broadcast_to(gains, (16, HALF)), 0.0)
    d_src[1, GAINS : GAINS + 16, :] = jnp.zeros((16, HALF), F32)
    dd.begin()

    back_f[...] = jnp.zeros_like(back_f)
    for w in range(9):
        dsq[pl.ds(QAT[w], NQ[w]), :] = (
            dsource[KAT[w] : KAT[w] + NQ[w]] + dq_source[QAT[w] : QAT[w + 1]]
        )
        to = KAT[w] + NQ[w]
        for start, size in PARTS[w]:
            back_f[pl.ds(start, size), :] = dsource[to : to + size]
            to += size
    back_src[...] = back_f[...].astype(BF)
    for copy in reversed(back):
        copy.start()

    dd.pair()
    loads[10].wait()
    loads[11].wait()
    output[...] = dot(to_nat[...], out_q[...]).astype(BF)
    stores[0].start()
    ab.plane()
    dd.plane()
    for copy in back:
        copy.wait_recv()
    dshift = (dsq[...] + dot(collect[...], back_dst[...])).astype(BF).astype(F32)
    gf = dmix[...] + norm_back(dshift, norm_q[...], inverse1, gain_attn)
    grad_field[...] = dot(to_nat[...], gf.astype(BF)).astype(BF)
    stores[1].start()
    ab.line()
    dd.line()
    ab.spread()
    dd.spread()
    for copy in there + back:
        copy.wait_send()
    ab.drain()
    dd.drain()
    ab.collect()
    stores[2].start()
    dd.collect()
    stores[3].start()
    ab.drain_late()
    dd.drain_late()
    ab.end()
    stores[4].start()
    dd.end()
    stores[5].start()
    ab.last.wait_send()
    dd.last.wait_send()
    for store in stores:
        store.wait()


def final(plans, out_n, gf_n, gat_ab_in, gat_d_in, *refs):
    outs = refs[:8]
    out_v8, gf_v, gat_ab, gat_d, qkv_v, out_v, up_v, down_v, ga_v, gm_v, in_sem, out_sem = refs[8:]
    loads = [
        pltpu.make_async_copy(src, dst, in_sem.at[i])
        for i, (src, dst) in enumerate(
            [(gat_d_in, gat_d), (gat_ab_in, gat_ab), (out_n, out_v8), (gf_n, gf_v)]
        )
    ]
    for load in loads:
        load.start()
    stores = [
        pltpu.make_async_copy(src, dst, out_sem.at[i])
        for i, (src, dst) in enumerate(
            zip((out_v8, gf_v, qkv_v, out_v, up_v, down_v, ga_v, gm_v), outs)
        )
    ]

    def whole(plan, gat):
        halves = [gat[i].astype(F32).reshape(plan.rows, HALF) for i in range(2)]
        return jnp.concatenate(halves, 1)

    loads[0].wait()
    d = whole(plans[1], gat_d)
    qkv_v[...] = jnp.concatenate([unfold(d[FOLD * i : FOLD * (i + 1)]) for i in range(3)], 1)
    gains = d[GAINS : GAINS + 1] + d[GAINS + 1 : GAINS + 2]
    ga_v[...] = gains[:, :C]
    gm_v[...] = gains[:, C : 2 * C]
    for at in (2, 6, 7):
        stores[at].start()
    for at in range(2):
        loads[2 + at].wait()
        stores[at].start()
    loads[1].wait()
    ab = whole(plans[0], gat_ab)
    down_v[...] = ab[:C]
    up_v[...] = ab[C : 2 * C]
    out_v[...] = unfold(ab[2 * C : 2 * C + FOLD])
    stores[3].start()
    stores[4].start()
    stores[5].start()
    for store in stores:
        store.wait()


def body(nlon, nlat, field, region, w_qkv, w_out, w_up, w_down, gain_attn, gain_mlp, grad_next):
    sizes = (nlon // 8, 2, 4, nlat) if nlon >= 16 else (nlon // 2, 1, 2, nlat)
    nz, ny, nx, _ = sizes
    g1, g2 = ny * (nlat // 2) * nx, nz
    plans = (Plan(2 * C + FOLD, g1, g2), Plan(GAINS + 16, g1, g2))
    hbm = pl.BlockSpec(memory_space=pltpu.HBM)
    V = pltpu.VMEM
    consts = [jnp.asarray(a) for a in tables()]
    operands = [
        field.reshape(TOK, C), grad_next.reshape(TOK, C), region, w_qkv, w_out, w_up, w_down.T,
        gain_attn.reshape(1, C), gain_mlp.reshape(1, C), *consts,
    ]

    def pair(shape_of, kind):
        return [V(shape_of(p), kind) for p in plans]

    shapes = [jax.ShapeDtypeStruct((TOK, C), BF)] * 2 + [
        jax.ShapeDtypeStruct((2, p.own, p.r, HALF), BF) for p in plans
    ]
    scratch = (
        [V(a.shape, a.dtype) for a in shapes]
        + [(pltpu.SMEM if i == 2 else V)(a.shape, a.dtype) for i, a in enumerate(operands)]
        + [V((HALO, C), BF)] * 4 + [V((HALO, C), F32)]
        + [
            V((NQS, C), F32), V((NQS, C), BF), V((NQS, C), BF), V((NQS, C), F32),
            V((HALO, C), F32), V((NKS, C), F32), V((NKS, C), BF), V((C, FF), BF),
            V((NQS, 256), F32), V((NKS, 256), BF), V((NKS, C), BF), V((NKS, 256), F32),
            V((HEADS * NQS, 256), BF),
            V((144, HEADS * 144), F32), V((4, 144, HEADS * 72), F32), V((4, 160, HEADS * 40), F32),
            V((144, HEADS * 144), BF), V((72, HEADS * 72), BF), V((40, HEADS * 40), BF),
            V((NQS, C), F32), V((NQS, C), BF),
            V((NQS, C), BF), V((NQS, FF), BF), V((NQS, FF), BF), V((NQS, C), F32),
            V((NQS, C), BF), V((NQS, C), F32), V((NQS, C), F32),
            V((NKS, C), BF), V((NKS, C), BF), V((NQS, C), F32), V((NQS, C), BF),
        ]
        + pair(lambda p: (2, p.rows, HALF), F32)
        + pair(lambda p: (p.rows, HALF), F32)
        + pair(lambda p: (p.rows, HALF), BF)
        + pair(lambda p: (g1, p.r, HALF), BF)
        + pair(lambda p: (p.pieces, p.piece, p.lanes), F32)
        + pair(lambda p: (g2, p.piece, p.lanes), F32)
        + pair(lambda p: (p.pieces, p.piece, p.lanes), F32)
        + pair(lambda p: (p.r, HALF), BF)
        + [
            pltpu.SemaphoreType.DMA((13,)),
            pltpu.SemaphoreType.DMA((6,)),
            pltpu.SemaphoreType.DMA((2, 8)),
            pltpu.SemaphoreType.DMA((2, 8)),
            pltpu.SemaphoreType.DMA((2, 2)),
            pltpu.SemaphoreType.DMA((2, 2)),
            pltpu.SemaphoreType.DMA((2, 4, 16)),
            pltpu.SemaphoreType.DMA((2, 4, 16)),
        ]
    )
    mids = pl.pallas_call(
        functools.partial(kernel, sizes, plans),
        out_shape=shapes,
        in_specs=[hbm] * len(operands),
        out_specs=[hbm] * 4,
        scratch_shapes=scratch,
        compiler_params=pltpu.CompilerParams(
            collective_id=0, has_side_effects=True, vmem_limit_bytes=VLIM
        ),
        name="block",
    )(*operands)
    results = [
        jax.ShapeDtypeStruct((TOK, C), BF),
        jax.ShapeDtypeStruct((TOK, C), BF),
        jax.ShapeDtypeStruct((C, 3 * C), F32),
        jax.ShapeDtypeStruct((C, C), F32),
        jax.ShapeDtypeStruct((C, FF), F32),
        jax.ShapeDtypeStruct((C, FF), F32),
        jax.ShapeDtypeStruct((1, C), F32),
        jax.ShapeDtypeStruct((1, C), F32),
    ]
    outs = pl.pallas_call(
        functools.partial(final, plans),
        out_shape=results,
        in_specs=[hbm] * 4,
        out_specs=[hbm] * 8,
        scratch_shapes=[V(a.shape, a.dtype) for a in shapes + results[2:]]
        + [pltpu.SemaphoreType.DMA((4,)), pltpu.SemaphoreType.DMA((8,))],
        compiler_params=pltpu.CompilerParams(vmem_limit_bytes=VLIM),
        name="final",
    )(*mids)
    output, grad_field, grad_qkv, grad_out, grad_up, grad_down_t, grad_ga, grad_gm = outs
    return (
        output.reshape(field.shape), grad_field.reshape(field.shape),
        grad_qkv, grad_out, grad_up, grad_down_t.T, grad_ga.reshape(C), grad_gm.reshape(C),
    )


def solution(mesh):
    grid = P(None, "lat", "lon", None)
    return jax.shard_map(
        functools.partial(body, mesh.shape["lon"], mesh.shape["lat"]),
        mesh=mesh,
        in_specs=(grid, P(), P(), P(), P(), P(), P(), P(), grid),
        out_specs=(grid, grid, P(), P(), P(), P(), P(), P()),
        check_vma=False,
    )
```
